32 devices in a mesh: clips: 2 (over y), seq: 8 (over z, x), mp: 2 (over core).
Axes of the slice: x: 2, y: 2, z: 4, core: 2. Of those that a mesh axis runs over, the one named last changes fastest.
Arguments:
- queries: bfloat16 [12, 4096, 128], P('mp', ('clips', 'seq')), parts along dimension 1, may hold values from -6 to 6
- keys: bfloat16 [12, 4096, 128], P('mp', ('clips', 'seq')), parts along dimension 1, may hold values from -6 to 6
- values: bfloat16 [12, 4096, 128], P('mp', ('clips', 'seq')), parts along dimension 1, may hold values from -12 to 12
- out_grad: bfloat16 [12, 4096, 128], P('mp', ('clips', 'seq')), parts along dimension 1, may hold values from -12 to 12
- tile_lists: int32 [12, 8, 4], P('mp'), may hold values from -1 to 7, as said below
Outputs:
- attn_out: bfloat16 [12, 4096, 128], P('mp', ('clips', 'seq')), parts along dimension 1
- query_grad: bfloat16 [12, 4096, 128], P('mp', ('clips', 'seq')), parts along dimension 1
- key_grad: bfloat16 [12, 4096, 128], P('mp', ('clips', 'seq')), parts along dimension 1
- value_grad: bfloat16 [12, 4096, 128], P('mp', ('clips', 'seq')), parts along dimension 1
The draws below stay inside these ranges and needn't reach their ends.
There are 2 independent parts, one for each index of `clips`. The reference program is written for one: setup_inputs(seed, part) draws one part's arguments, and reference() takes and returns one part's arrays. A program takes and returns all parts, laid end to end along the dimension named above; an argument that names none is the same for every part. Nothing has to cross between parts.
Inputs may be any that keep to these rules, and one draw needn't show every extreme that they name: `tile_lists`: tile ids count (time + row) * 8 + column over a grid of 1 x 1 x 8 tiles. Entry 0 of the list of head h and query tile q is q itself; the further entries name distinct tiles that share a face with q inside the grid, filled entries first and -1 in empty ones. For every tile and each of its six face directions, at most 3 heads of each group of 6 consecutive heads name that neighbour.
All inputs are finite; a program needn't handle non-finite values.
Results may differ from the reference program's by a relative error of at most 0.0067.
Values may be sent and summed in bfloat16 or wider, within the bound.
No kernel may reach another device: no remote copies, remote signals or barrier semaphores. Data moves between devices by JAX's collectives and lax.ppermute only.
A program may use at most 64 MiB of HBM per device.

```python
import jax
import jax.numpy as jnp
from jax import lax

HEADS = 12
HD = 128
TILE = 256
MAXT = 4
GX = 8
GY = 1
GT = 1
TILES = 8
TOKENS = 2048


def draw_queries(key, part):
    shape_full = (HEADS, TILES, TILE, HD)
    sample = 1.4 * jax.random.normal(jax.random.fold_in(key, 1), shape_full, jnp.float32)
    return jnp.clip(sample, -6.0, 6.0).reshape(HEADS, TILES * TILE, HD).astype(jnp.bfloat16)


def draw_keys(key, part):
    shape_full = (HEADS, TILES, TILE, HD)
    sample = 1.4 * jax.random.normal(jax.random.fold_in(key, 2), shape_full, jnp.float32)
    return jnp.clip(sample, -6.0, 6.0).reshape(HEADS, TILES * TILE, HD).astype(jnp.bfloat16)


def shuffle_six(subkey):
    return jax.random.permutation(subkey, 6)


def draw_tile_lists(key, part):
    groups = HEADS // 6
    tile_ids = jnp.arange(TILES, dtype=jnp.int32)
    across = tile_ids % GX
    downward = tile_ids // GX % GY
    frames = tile_ids // (GX * GY)
    layer_size = GX * GY
    neighbour_ids = jnp.stack([tile_ids + 1, tile_ids - 1, tile_ids + GX, tile_ids - GX, tile_ids + layer_size, tile_ids - layer_size], axis=-1)
    inside = jnp.stack([across < GX - 1, across > 0, downward < GY - 1, downward > 0, frames < GT - 1, frames > 0], axis=-1)
    row_shift = jax.vmap(shuffle_six)(jax.random.split(jax.random.fold_in(key, 5), TILES * groups)).reshape(TILES, groups, 6)
    column_shift = jax.vmap(shuffle_six)(jax.random.split(jax.random.fold_in(key, 6), TILES * groups)).reshape(TILES, groups, 6)
    latin_square = (row_shift[:, :, :, None] + column_shift[:, :, None, :]) % 6 < 3
    frame_pick = jnp.minimum(jax.random.randint(jax.random.fold_in(key, 11), (), 1, max(2, GT - 1)), GT - 1)
    row_pick = jnp.minimum(jax.random.randint(jax.random.fold_in(key, 12), (), 1, max(2, GY - 1)), GY - 1)
    column_pick = jax.random.randint(jax.random.fold_in(key, 13), (), 1, GX - 1)
    forced = (frame_pick * GY + row_pick) * GX + column_pick
    level_draw = jax.random.randint(jax.random.fold_in(key, 7), (TILES,), 1, 4)
    levels = jnp.where(tile_ids == forced, 3, level_draw)
    coin_draw = jax.random.randint(jax.random.fold_in(key, 9), (TILES, groups, 6, 6), 0, 3)
    in_use = latin_square & (coin_draw < levels[:, None, None, None]) & inside[:, None, None, :]
    ranking = jnp.cumsum(in_use.astype(jnp.int32), axis=-1)
    entries = [jnp.broadcast_to(tile_ids[:, None, None], (TILES, groups, 6))]
    for position in range(1, MAXT):
        matched = in_use & (ranking == position)
        picked = jnp.sum(jnp.where(matched, neighbour_ids[:, None, None, :], 0), axis=-1)
        entries.append(jnp.where(jnp.any(matched, axis=-1), picked, -1))
    lists_table = jnp.stack(entries, axis=-1)
    return jnp.transpose(lists_table, (1, 2, 0, 3)).reshape(HEADS, TILES, MAXT).astype(jnp.int32)


def level_of(own_key, extent, pieces, low, largest):
    gain, own = 1.0, jax.random.fold_in(own_key, 6)
    for axis_at, parts in pieces:
        draws = jnp.exp(jax.random.uniform(jax.random.fold_in(own, axis_at), (parts,), jnp.float32, low / len(pieces), largest / len(pieces)))
        gain = gain * jnp.repeat(draws, extent[axis_at] // parts).reshape([-1 if axis == axis_at else 1 for axis in range(len(extent))])
    return gain


def bell_draw(stream_key, dims, scale, reach, cuts=(), kind=jnp.bfloat16):
    result = scale * jax.random.normal(stream_key, dims, jnp.float32)
    if cuts:
        result = result * level_of(stream_key, dims, cuts, -0.22, 0.18)
    return jnp.clip(result, -reach, reach).astype(kind)


def setup_inputs(seed: int = 0, part: int = 0) -> dict:
    splits = jax.random.split(jax.random.key(seed), 6)
    own_keys = jax.random.split(jax.random.fold_in(splits[5], part), 6)
    queries = draw_queries(jax.random.fold_in(jax.random.fold_in(splits[5], part), 71), part)
    keys = draw_keys(jax.random.fold_in(jax.random.fold_in(splits[5], part), 71), part)
    values = bell_draw(own_keys[2], (HEADS, TOKENS, HD), 2.0, 12.0, ((0, 2), (1, 8)))
    out_grad = bell_draw(own_keys[3], (HEADS, TOKENS, HD), 2.0, 12.0, ((0, 2), (1, 8)))
    tile_lists = draw_tile_lists(jax.random.fold_in(splits[5], 71), part)
    return dict(queries=queries, keys=keys, values=values, out_grad=out_grad, tile_lists=tile_lists)


def head_pass(operands):
    query_tiles, key_tiles, value_tiles, grad_tiles, head_lists = operands
    score_scale = HD ** -0.5
    live_slots = head_lists >= 0
    safe_lists = jnp.where(live_slots, head_lists, 0).astype(jnp.int32)
    key_chosen = key_tiles[safe_lists].astype(jnp.float32)
    value_chosen = value_tiles[safe_lists].astype(jnp.float32)
    query_wide = query_tiles.astype(jnp.float32)
    grad_wide = grad_tiles.astype(jnp.float32)
    scores = jnp.einsum('aid,ajtd->aijt', query_wide, key_chosen) * score_scale
    scores = jnp.where(live_slots[:, None, :, None], scores, -jnp.inf)
    row_max = jnp.max(scores, axis=(2, 3), keepdims=True)
    weights = jnp.exp(scores - row_max)
    probs = weights / jnp.sum(weights, axis=(2, 3), keepdims=True)
    probs_low = lax.optimization_barrier(probs.astype(jnp.bfloat16)).astype(jnp.float32)
    attention = jnp.einsum('aijt,ajtd->aid', probs_low, value_chosen).astype(jnp.bfloat16)
    prob_grad = jnp.einsum('aid,ajtd->aijt', grad_wide, value_chosen)
    delta = jnp.sum(probs * prob_grad, axis=(2, 3), keepdims=True)
    score_grad = lax.optimization_barrier((probs * (prob_grad - delta)).astype(jnp.bfloat16)).astype(jnp.float32)
    query_result = (jnp.einsum('aijt,ajtd->aid', score_grad, key_chosen) * score_scale).astype(jnp.bfloat16)
    key_part = (jnp.einsum('aijt,aid->ajtd', score_grad, query_wide) * score_scale).astype(jnp.bfloat16)
    value_part = jnp.einsum('aijt,aid->ajtd', probs_low, grad_wide).astype(jnp.bfloat16)
    live_wide = live_slots[:, :, None, None]
    key_total = jnp.zeros((TILES, TILE, HD), jnp.float32).at[safe_lists].add(
        jnp.where(live_wide, key_part.astype(jnp.float32), 0.0))
    value_total = jnp.zeros((TILES, TILE, HD), jnp.float32).at[safe_lists].add(
        jnp.where(live_wide, value_part.astype(jnp.float32), 0.0))
    return attention, query_result, key_total.astype(jnp.bfloat16), value_total.astype(jnp.bfloat16)


def reference(queries, keys, values, out_grad, tile_lists):
    shaped = (HEADS, TILES, TILE, HD)
    operands = (queries.reshape(shaped), keys.reshape(shaped), values.reshape(shaped),
                out_grad.reshape(shaped), tile_lists.astype(jnp.int32))
    attention, query_result, key_result, value_result = lax.map(head_pass, operands)
    flat = (HEADS, TOKENS, HD)
    return (attention.reshape(flat), query_result.reshape(flat),
            key_result.reshape(flat), value_result.reshape(flat))
```

```python
import functools

import jax
import jax.numpy as jnp
from jax import lax
from jax.experimental import pallas as pl
from jax.experimental.pallas import tpu as pltpu
from jax.sharding import PartitionSpec as P

GX = 8
LOG2E = 1.4426950408889634
VMEM_LIMIT = 48 * 1024 * 1024


def channel_list(tile_count):
    row_tiles = min(4, tile_count // GX)
    layer_size = GX * row_tiles
    distances = [1]
    if row_tiles > 1:
        distances.append(GX)
    if tile_count // layer_size > 1:
        distances.append(layer_size)
    return [(distance, colour) for distance in distances for colour in (0, 1)]


def swap_route(channel, tile_count):
    distance, colour = channel
    route = []
    for low in range(tile_count - distance):
        if (low // distance) % 2 == colour:
            route += [(low, low + distance), (low + distance, low)]
    return route


def swapped(block, channel):
    return lax.ppermute(block, "seq", swap_route(channel, lax.axis_size("seq")))


def partner_of(own_tile, channel):
    distance, colour = channel
    is_low = lax.rem(lax.div(own_tile, distance), 2) == colour
    return jnp.where(is_low, own_tile + distance, own_tile - distance)


def dot_nt(a, b):
    return lax.dot_general(a, b, (((1,), (1,)), ((), ())), preferred_element_type=jnp.float32)


def dot_tn(a, b):
    return lax.dot_general(a, b, (((0,), (0,)), ((), ())), preferred_element_type=jnp.float32)


def dot_nn(a, b):
    return lax.dot_general(a, b, (((1,), (0,)), ((), ())), preferred_element_type=jnp.float32)


def pack_keys_kernel(channels, cap, lists, keys, values, table, *rest):
    targets, sems = rest[: len(channels)], rest[len(channels)]
    heads, tile_count, entries = lists.shape
    own_tile = lax.axis_index("seq")
    started = []
    for number, channel in enumerate(channels):
        partner = partner_of(own_tile, channel)
        inside = (partner >= 0) & (partner < tile_count)
        reader = jnp.clip(partner, 0, tile_count - 1)
        for slot in range(cap):
            table[heads * len(channels) + number * cap + slot] = -1
        slot = jnp.int32(0)
        pairs = []
        for head in range(heads):
            wanted = lists[head, reader, 1] == own_tile
            for entry in range(2, entries):
                wanted = wanted | (lists[head, reader, entry] == own_tile)
            wanted = wanted & inside & (slot < cap)
            pairs.append((wanted, head, slot))

            @pl.when(wanted)
            def _():
                table[heads * len(channels) + number * cap + slot] = head
                for part, source in enumerate((keys, values)):
                    pltpu.make_async_copy(
                        source.at[head], targets[number].at[part, slot], sems.at[number, part, head]
                    ).start()

            slot = slot + wanted.astype(jnp.int32)
        started.append(pairs)
    for number, channel in enumerate(channels):
        partner = partner_of(own_tile, channel)
        slot = jnp.int32(0)
        for head in range(heads):
            named = lists[head, own_tile, 1] == partner
            for entry in range(2, entries):
                named = named | (lists[head, own_tile, entry] == partner)
            named = named & (partner >= 0) & (partner < tile_count) & (slot < cap)
            table[head * len(channels) + number] = jnp.where(named, slot, -1)
            slot = slot + named.astype(jnp.int32)
    for number, pairs in enumerate(started):
        for wanted, head, slot in pairs:

            @pl.when(wanted)
            def _():
                for part, source in enumerate((keys, values)):
                    pltpu.make_async_copy(
                        source.at[head], targets[number].at[part, slot], sems.at[number, part, head]
                    ).wait()


def pack_queries_kernel(channels, cap, table, queries, grads, *rest):
    targets, sems = rest[: len(channels)], rest[len(channels)]
    heads = queries.shape[0]
    for stage in ("start", "wait"):
        for number in range(len(channels)):
            for head in range(heads):
                slot = table[head * len(channels) + number]

                @pl.when(slot >= 0)
                def _():
                    for part, source in enumerate((queries, grads)):
                        copy = pltpu.make_async_copy(
                            source.at[head],
                            targets[number].at[part, slot],
                            sems.at[number, part, head],
                        )
                        if stage == "start":
                            copy.start()
                        else:
                            copy.wait()


def attend_kernel(channels, extra, scale, table, q_ref, k_ref, v_ref, g_ref, *rest):
    count = len(channels)
    fetched = rest[:count]
    o_ref, dq_ref, dk_ref, dv_ref = rest[count : count + 4]
    stats = rest[count + 4 : 2 * count + 4]
    more_keys, more_values, row_stats = rest[2 * count + 4 :]
    head = pl.program_id(0)
    slots = [table[head * count + number] for number in range(count)]
    live = jnp.int32(0)
    for number in range(count):

        @pl.when(slots[number] >= 0)
        def _():
            more_keys[live] = fetched[number][0, slots[number]]
            more_values[live] = fetched[number][1, slots[number]]

        live = live + (slots[number] >= 0).astype(jnp.int32)

    def attend(tiles):
        query, grad = q_ref[0], g_ref[0]
        keys = [k_ref[0]] + [more_keys[tile] for tile in range(tiles)]
        values = [v_ref[0]] + [more_values[tile] for tile in range(tiles)]
        scores = [dot_nt(key, query) * (scale * LOG2E) for key in keys]
        top = functools.reduce(jnp.maximum, [jnp.max(s, axis=0, keepdims=True) for s in scores])
        weights = [jnp.exp2(s - top) for s in scores]
        total = sum(jnp.sum(w, axis=0, keepdims=True) for w in weights)
        inverse = 1.0 / total
        probs = [w * inverse for w in weights]
        prob_grads = [dot_nt(value, grad) for value in values]
        delta = sum(
            jnp.sum(p * pg, axis=0, keepdims=True) for p, pg in zip(probs, prob_grads)
        )
        probs_low = [p.astype(jnp.bfloat16) for p in probs]
        score_grads = [
            (p * (pg - delta)).astype(jnp.bfloat16) for p, pg in zip(probs, prob_grads)
        ]
        attention = sum(dot_tn(value, p) for value, p in zip(values, probs_low))
        query_grad = sum(dot_tn(key, sg) for key, sg in zip(keys, score_grads))
        o_ref[0] = attention.T.astype(jnp.bfloat16)
        dq_ref[0] = (query_grad * scale).T.astype(jnp.bfloat16)
        dk_ref[0] = (dot_nn(score_grads[0], query) * scale).astype(jnp.bfloat16)
        dv_ref[0] = dot_nn(probs_low[0], grad).astype(jnp.bfloat16)
        row_stats[0:1] = top + jnp.log2(total)
        row_stats[1:2] = delta

    for tiles in range(extra + 1):
        pl.when(live == tiles)(functools.partial(attend, tiles))
    for number in range(count):

        @pl.when(slots[number] >= 0)
        def _():
            stats[number][slots[number]] = row_stats[...]


def owner_kernel(channels, cap, scale, table, k_ref, v_ref, dk_own, dv_own, *rest):
    count = len(channels)
    arrived, stats = rest[:count], rest[count : 2 * count]
    dk_ref, dv_ref, dk_sum, dv_sum = rest[2 * count :]
    heads = k_ref.shape[0]
    for head in range(heads):
        dk_sum[head] = dk_own[head].astype(jnp.float32)
        dv_sum[head] = dv_own[head].astype(jnp.float32)
    for number in range(count):
        for slot in range(cap):
            head = table[heads * count + number * cap + slot]

            @pl.when(head >= 0)
            def _():
                query, grad = arrived[number][0, slot], arrived[number][1, slot]
                level = stats[number][slot, 0:1]
                delta = stats[number][slot, 1:2]
                score = dot_nt(k_ref[head], query) * (scale * LOG2E)
                prob = jnp.exp2(score - level)
                prob_grad = dot_nt(v_ref[head], grad)
                score_grad = (prob * (prob_grad - delta)).astype(jnp.bfloat16)
                dk_sum[head] += dot_nn(score_grad, query) * scale
                dv_sum[head] += dot_nn(prob.astype(jnp.bfloat16), grad)

    for head in range(heads):
        dk_ref[head] = dk_sum[head].astype(jnp.bfloat16)
        dv_ref[head] = dv_sum[head].astype(jnp.bfloat16)


def per_device(queries, keys, values, out_grad, tile_lists):
    heads, tokens, width = queries.shape
    tile_count = lax.axis_size("seq")
    channels = channel_list(tile_count)
    count = len(channels)
    cap = heads // 2
    extra = min(count, tile_lists.shape[2] - 1)
    scale = width ** (-0.5)
    smem = pl.BlockSpec(memory_space=pltpu.SMEM)
    anywhere = pl.BlockSpec(memory_space=pl.ANY)
    vmem = pl.BlockSpec(memory_space=pltpu.VMEM)
    params = pltpu.CompilerParams(vmem_limit_bytes=VMEM_LIMIT)
    packed = jax.ShapeDtypeStruct((2, cap, tokens, width), jnp.bfloat16)
    whole = jax.ShapeDtypeStruct((heads, tokens, width), jnp.bfloat16)
    copies = pltpu.SemaphoreType.DMA((count, 2, heads))
    table, *key_value = pl.pallas_call(
        functools.partial(pack_keys_kernel, channels, cap),
        out_shape=[jax.ShapeDtypeStruct((count * (heads + cap),), jnp.int32)] + [packed] * count,
        in_specs=[smem, anywhere, anywhere],
        out_specs=[smem] + [anywhere] * count,
        scratch_shapes=[copies],
        compiler_params=params,
        name="pack_keys",
    )(tile_lists, keys, values)
    fetched = [swapped(block, channel) for block, channel in zip(key_value, channels)]
    query_grads = pl.pallas_call(
        functools.partial(pack_queries_kernel, channels, cap),
        out_shape=[packed] * count,
        in_specs=[smem, anywhere, anywhere],
        out_specs=[anywhere] * count,
        scratch_shapes=[copies],
        compiler_params=params,
        name="pack_queries",
    )(table, queries, out_grad)
    arrived = [swapped(block, channel) for block, channel in zip(query_grads, channels)]
    row_stats = jax.ShapeDtypeStruct((cap, 2, tokens), jnp.float32)
    one_head = pl.BlockSpec((1, tokens, width), lambda head: (head, 0, 0))
    attn_out, query_grad, own_dk, own_dv, *stats = pl.pallas_call(
        functools.partial(attend_kernel, channels, extra, scale),
        grid=(heads,),
        out_shape=[whole] * 4 + [row_stats] * count,
        in_specs=[smem]
        + [one_head] * 4
        + [pl.BlockSpec((2, cap, tokens, width), lambda head: (0, 0, 0, 0))] * count,
        out_specs=[one_head] * 4
        + [pl.BlockSpec((cap, 2, tokens), lambda head: (0, 0, 0))] * count,
        scratch_shapes=[
            pltpu.VMEM((extra, tokens, width), jnp.bfloat16),
            pltpu.VMEM((extra, tokens, width), jnp.bfloat16),
            pltpu.VMEM((2, tokens), jnp.float32),
        ],
        compiler_params=params,
        name="attend",
    )(table, queries, keys, values, out_grad, *fetched)
    stats = [swapped(block, channel) for block, channel in zip(stats, channels)]
    key_grad, value_grad = pl.pallas_call(
        functools.partial(owner_kernel, channels, cap, scale),
        out_shape=[whole] * 2,
        in_specs=[smem] + [vmem] * (4 + 2 * count),
        out_specs=[vmem] * 2,
        scratch_shapes=[pltpu.VMEM((heads, tokens, width), jnp.float32)] * 2,
        compiler_params=params,
        name="owner",
    )(table, keys, values, own_dk, own_dv, *arrived, *stats)
    return attn_out, query_grad, key_grad, value_grad


def solution(mesh):
    tokens_placed = P("mp", ("clips", "seq"), None)
    return jax.shard_map(
        per_device,
        mesh=mesh,
        in_specs=(tokens_placed,) * 4 + (P("mp", None, None),),
        out_specs=(tokens_placed,) * 4,
        check_vma=False,
    )
```

```python
import functools

import jax
import jax.numpy as jnp
from jax import lax
from jax.experimental import pallas as pl
from jax.experimental.pallas import tpu as pltpu
from jax.sharding import PartitionSpec as P

GX = 8
LOG2E = 1.4426950408889634
LOWEST = -3.0e38
VMEM_LIMIT = 24 * 1024 * 1024


def channel_list(tile_count):
    row_tiles = min(4, tile_count // GX)
    layer_size = GX * row_tiles
    distances = [1]
    if row_tiles > 1:
        distances.append(GX)
    if tile_count // layer_size > 1:
        distances.append(layer_size)
    return [(distance, colour) for distance in distances for colour in (0, 1)]


def swap_route(channel, tile_count):
    distance, colour = channel
    route = []
    for low in range(tile_count - distance):
        if (low // distance) % 2 == colour:
            route += [(low, low + distance), (low + distance, low)]
    return route


def swapped(block, channel):
    return lax.ppermute(block, "seq", swap_route(channel, lax.axis_size("seq")))


def partner_of(own_tile, channel):
    distance, colour = channel
    is_low = lax.rem(lax.div(own_tile, distance), 2) == colour
    return jnp.where(is_low, own_tile + distance, own_tile - distance)


def dot_nt(a, b):
    return lax.dot_general(a, b, (((1,), (1,)), ((), ())), preferred_element_type=jnp.float32)


def dot_tn(a, b):
    return lax.dot_general(a, b, (((0,), (0,)), ((), ())), preferred_element_type=jnp.float32)


def dot_nn(a, b):
    return lax.dot_general(a, b, (((1,), (0,)), ((), ())), preferred_element_type=jnp.float32)


class Table:
    def __init__(self, ref, heads, count, cap):
        self.ref, self.heads, self.count, self.cap = ref, heads, count, cap

    def slot_at(self, head, number):
        return head * self.count + number

    def reader_at(self, number, slot):
        return self.heads * self.count + number * self.cap + slot

    def owner_at(self, number, slot):
        return self.reader_at(self.count + number, slot)

    def size(self):
        return self.owner_at(self.count - 1, self.cap - 1) + 1


def pack_keys_kernel(channels, cap, lists, keys, values, table_ref, *rest):
    *targets, sems = rest
    heads, entries, tile_count = lists.shape
    count = len(channels)
    table = Table(table_ref, heads, count, cap)
    own_tile = lax.axis_index("seq")
    started = []
    for number, channel in enumerate(channels):
        partner = partner_of(own_tile, channel)
        inside = (partner >= 0) & (partner < tile_count)
        reader = jnp.clip(partner, 0, tile_count - 1)
        for slot in range(cap):
            table_ref[table.owner_at(number, slot)] = -1
            table_ref[table.reader_at(number, slot)] = -1
        slot = jnp.int32(0)
        for head in range(heads):
            wanted = lists[head, 1, reader] == own_tile
            for entry in range(2, entries):
                wanted = wanted | (lists[head, entry, reader] == own_tile)
            wanted = wanted & inside & (slot < cap)

            @pl.when(wanted)
            def _():
                table_ref[table.owner_at(number, slot)] = head
                for part, source in enumerate((keys, values)):
                    pltpu.make_async_copy(
                        source.at[head], targets[number].at[part, slot], sems.at[number, part, slot]
                    ).start()

            slot = slot + wanted.astype(jnp.int32)
        started.append(slot)
    for number, channel in enumerate(channels):
        partner = partner_of(own_tile, channel)
        slot = jnp.int32(0)
        for head in range(heads):
            named = lists[head, 1, own_tile] == partner
            for entry in range(2, entries):
                named = named | (lists[head, entry, own_tile] == partner)
            named = named & (partner >= 0) & (partner < tile_count) & (slot < cap)
            table_ref[table.slot_at(head, number)] = jnp.where(named, slot, -1)

            @pl.when(named)
            def _():
                table_ref[table.reader_at(number, slot)] = head

            slot = slot + named.astype(jnp.int32)
    for number in range(count):
        for slot in range(cap):

            @pl.when(slot < started[number])
            def _():
                for part, source in enumerate((keys, values)):
                    pltpu.make_async_copy(
                        source.at[0], targets[number].at[part, slot], sems.at[number, part, slot]
                    ).wait()


def own_kernel(count, cap, scale, table_ref, q_ref, k_ref, v_ref, g_ref, queries, grads, *rest):
    weight_ref, prob_grad_ref, rows_ref, *targets, sems = rest
    heads = queries.shape[0]
    table = Table(table_ref, heads, count, cap)

    def copies(stage):
        for number in range(count):
            for slot in range(cap):
                head = table_ref[table.reader_at(number, slot)]

                @pl.when(head >= 0)
                def _():
                    for part, source in enumerate((queries, grads)):
                        copy = pltpu.make_async_copy(
                            source.at[head],
                            targets[number].at[part, slot],
                            sems.at[number, part, slot],
                        )
                        if stage == "start":
                            copy.start()
                        else:
                            copy.wait()

    pl.when(pl.program_id(0) == 0)(lambda: copies("start"))
    score = dot_nt(k_ref[0], q_ref[0]) * (scale * LOG2E)
    top = jnp.max(score, axis=0, keepdims=True)
    weight = jnp.exp2(score - top)
    prob_grad = dot_nt(v_ref[0], g_ref[0])
    weight_ref[0] = weight
    prob_grad_ref[0] = prob_grad
    rows_ref[0, 0:1] = top
    rows_ref[0, 1:2] = jnp.sum(weight, axis=0, keepdims=True)
    rows_ref[0, 2:3] = jnp.sum(weight * prob_grad, axis=0, keepdims=True)
    pl.when(pl.program_id(0) == heads - 1)(lambda: copies("wait"))


def statistics_kernel(count, cap, scale, table_ref, q_ref, g_ref, own_rows, *rest):
    fetched, rest = rest[:count], rest[count:]
    weight_ref, prob_grad_ref, own_factors, far_factors = rest[:4]
    stats, far_rows = rest[4 : 4 + count], rest[4 + count]
    heads = q_ref.shape[0]
    table = Table(table_ref, heads, count, cap)
    for number in range(count):
        for slot in range(cap):
            head = jnp.maximum(table_ref[table.reader_at(number, slot)], 0)
            place = number * cap + slot
            score = dot_nt(fetched[number][0, slot], q_ref[head]) * (scale * LOG2E)
            top = jnp.max(score, axis=0, keepdims=True)
            weight = jnp.exp2(score - top)
            prob_grad = dot_nt(fetched[number][1, slot], g_ref[head])
            weight_ref[place] = weight
            prob_grad_ref[place] = prob_grad
            far_rows[place, 0:1] = top
            far_rows[place, 1:2] = jnp.sum(weight, axis=0, keepdims=True)
            far_rows[place, 2:3] = jnp.sum(weight * prob_grad, axis=0, keepdims=True)
    for head in range(heads):
        rows = [own_rows[head]]
        slots = [table_ref[table.slot_at(head, number)] for number in range(count)]
        for number in range(count):
            found = far_rows[number * cap + jnp.maximum(slots[number], 0)]
            missing = jnp.where(
                lax.broadcasted_iota(jnp.int32, found.shape, 0) == 0, LOWEST, 0.0
            )
            rows.append(jnp.where(slots[number] >= 0, found, missing))
        top = functools.reduce(jnp.maximum, [row[0:1] for row in rows])
        factors = [jnp.exp2(row[0:1] - top) for row in rows]
        total = sum(factor * row[1:2] for factor, row in zip(factors, rows))
        inverse = 1.0 / total
        delta = sum(factor * row[2:3] for factor, row in zip(factors, rows)) * inverse
        level = top + jnp.log2(total)
        own_factors[head, 0:1] = factors[0] * inverse
        own_factors[head, 1:2] = delta
        for number in range(count):

            @pl.when(slots[number] >= 0)
            def _():
                place = number * cap + slots[number]
                far_factors[place, 0:1] = factors[1 + number] * inverse
                far_factors[place, 1:2] = delta
                stats[number][slots[number], 0:1] = level
                stats[number][slots[number], 1:2] = delta


def reader_kernel(count, cap, scale, table_ref, q_ref, k_ref, v_ref, g_ref, *rest):
    own_weight, own_prob_grad, own_factors, far_weight, far_prob_grad, far_factors = rest[:6]
    fetched, rest = rest[6 : 6 + count], rest[6 + count :]
    o_ref, dq_ref, dk_ref, dv_ref, o_sum, dq_sum = rest
    heads = q_ref.shape[0]
    table = Table(table_ref, heads, count, cap)

    def softmax_grad(weight, prob_grad, factors):
        prob = weight * factors[0:1]
        score_grad = prob * (prob_grad - factors[1:2])
        return prob.astype(jnp.bfloat16), score_grad.astype(jnp.bfloat16)

    for head in range(heads):
        prob, score_grad = softmax_grad(own_weight[head], own_prob_grad[head], own_factors[head])
        o_sum[head] = dot_tn(v_ref[head], prob)
        dq_sum[head] = dot_tn(k_ref[head], score_grad)
        dk_ref[head] = dot_nn(score_grad, q_ref[head]) * scale
        dv_ref[head] = dot_nn(prob, g_ref[head])
    for number in range(count):
        for slot in range(cap):
            head = table_ref[table.reader_at(number, slot)]
            place = number * cap + slot

            @pl.when(head >= 0)
            def _():
                prob, score_grad = softmax_grad(
                    far_weight[place], far_prob_grad[place], far_factors[place]
                )
                o_sum[head] += dot_tn(fetched[number][1, slot], prob)
                dq_sum[head] += dot_tn(fetched[number][0, slot], score_grad)

    for head in range(heads):
        o_ref[head] = o_sum[head].T.astype(jnp.bfloat16)
        dq_ref[head] = (dq_sum[head] * scale).T.astype(jnp.bfloat16)


def owner_kernel(count, cap, scale, number, table_ref, k_ref, v_ref, dk_in, dv_in, *rest):
    arrived, stats, dk_ref, dv_ref, dk_sum, dv_sum = rest
    heads = k_ref.shape[0]
    table = Table(table_ref, heads, count, cap)
    for head in range(heads):
        dk_sum[head] = dk_in[head]
        dv_sum[head] = dv_in[head]
    for slot in range(cap):
        found = table_ref[table.owner_at(number, slot)]
        head = jnp.maximum(found, 0)
        query, grad = arrived[0, slot], arrived[1, slot]
        score = dot_nt(k_ref[head], query) * (scale * LOG2E)
        prob = jnp.exp2(score - stats[slot, 0:1])
        prob_grad = dot_nt(v_ref[head], grad)
        score_grad = (prob * (prob_grad - stats[slot, 1:2])).astype(jnp.bfloat16)
        dk_term = dot_nn(score_grad, query) * scale
        dv_term = dot_nn(prob.astype(jnp.bfloat16), grad)
        dk_sum[head] += jnp.where(found >= 0, dk_term, 0.0)
        dv_sum[head] += jnp.where(found >= 0, dv_term, 0.0)
    for head in range(heads):
        dk_ref[head] = dk_sum[head].astype(dk_ref.dtype)
        dv_ref[head] = dv_sum[head].astype(dv_ref.dtype)


def per_device(queries, keys, values, out_grad, tile_lists):
    heads, tokens, width = queries.shape
    channels = channel_list(lax.axis_size("seq"))
    count = len(channels)
    cap = heads // 2
    scale = width ** (-0.5)
    table_size = Table(None, heads, count, cap).size()
    smem = pl.BlockSpec(memory_space=pltpu.SMEM)
    anywhere = pl.BlockSpec(memory_space=pl.ANY)
    vmem = pl.BlockSpec(memory_space=pltpu.VMEM)
    params = pltpu.CompilerParams(vmem_limit_bytes=VMEM_LIMIT)
    packed = pltpu.VMEM((2, cap, tokens, width), jnp.bfloat16)
    whole = jax.ShapeDtypeStruct((heads, tokens, width), jnp.bfloat16)
    whole_sum = pltpu.VMEM((heads, tokens, width), jnp.float32)
    squares = pltpu.VMEM((heads, tokens, tokens), jnp.float32)
    far_squares = pltpu.VMEM((count * cap, tokens, tokens), jnp.float32)
    row_stats = pltpu.VMEM((cap, 2, tokens), jnp.float32)
    copies = pltpu.SemaphoreType.DMA((count, 2, cap))
    lists, q_far, k_far, v_far, g_far = (
        pltpu.with_memory_space_constraint(array, pltpu.HBM)
        for array in (jnp.swapaxes(tile_lists, 1, 2), queries, keys, values, out_grad)
    )
    table, *key_value = pl.pallas_call(
        functools.partial(pack_keys_kernel, channels, cap),
        out_shape=[jax.ShapeDtypeStruct((table_size,), jnp.int32)] + [packed] * count,
        in_specs=[smem, anywhere, anywhere],
        out_specs=[smem] + [vmem] * count,
        scratch_shapes=[copies],
        compiler_params=params,
        name="pack_keys",
    )(lists, k_far, v_far)
    fetched = [swapped(block, channel) for block, channel in zip(key_value, channels)]
    one_head = pl.BlockSpec((1, tokens, width), lambda head: (head, 0, 0))
    one_square = pl.BlockSpec((1, tokens, tokens), lambda head: (head, 0, 0))
    own_weight, own_prob_grad, own_rows, *query_grads = pl.pallas_call(
        functools.partial(own_kernel, count, cap, scale),
        grid=(heads,),
        out_shape=[squares] * 2 + [pltpu.VMEM((heads, 3, tokens), jnp.float32)] + [packed] * count,
        in_specs=[smem] + [one_head] * 4 + [anywhere] * 2,
        out_specs=[one_square] * 2
        + [pl.BlockSpec((1, 3, tokens), lambda head: (head, 0, 0))]
        + [pl.BlockSpec(memory_space=pltpu.VMEM)] * count,
        scratch_shapes=[copies],
        compiler_params=params,
        name="own_scores",
    )(table, q_far, k_far, v_far, g_far, q_far, g_far)
    arrived = [swapped(block, channel) for block, channel in zip(query_grads, channels)]
    far_weight, far_prob_grad, own_factors, far_factors, *stats = pl.pallas_call(
        functools.partial(statistics_kernel, count, cap, scale),
        out_shape=[far_squares] * 2
        + [pltpu.VMEM((heads, 2, tokens), jnp.float32)]
        + [pltpu.VMEM((count * cap, 2, tokens), jnp.float32)]
        + [row_stats] * count,
        in_specs=[smem] + [vmem] * (3 + count),
        out_specs=[vmem] * (4 + count),
        scratch_shapes=[pltpu.VMEM((count * cap, 3, tokens), jnp.float32)],
        compiler_params=params,
        name="statistics",
    )(table, queries, out_grad, own_rows, *fetched)
    stats = [swapped(block, channel) for block, channel in zip(stats, channels)]
    transposed_sums = pltpu.VMEM((heads, width, tokens), jnp.float32)
    attn_out, query_grad, key_sum, value_sum = pl.pallas_call(
        functools.partial(reader_kernel, count, cap, scale),
        out_shape=[whole] * 2 + [whole_sum] * 2,
        in_specs=[smem] + [vmem] * (10 + count),
        out_specs=[vmem] * 4,
        scratch_shapes=[transposed_sums] * 2,
        compiler_params=params,
        name="reader",
    )(
        table,
        queries,
        keys,
        values,
        out_grad,
        own_weight,
        own_prob_grad,
        own_factors,
        far_weight,
        far_prob_grad,
        far_factors,
        *fetched,
    )
    for number in range(count):
        last = number == count - 1
        key_sum, value_sum = pl.pallas_call(
            functools.partial(owner_kernel, count, cap, scale, number),
            out_shape=[whole if last else whole_sum] * 2,
            in_specs=[smem] + [vmem] * 6,
            out_specs=[vmem] * 2,
            scratch_shapes=[whole_sum] * 2,
            compiler_params=params,
            name="owner",
        )(table, keys, values, key_sum, value_sum, arrived[number], stats[number])
    return attn_out, query_grad, key_sum, value_sum


def solution(mesh):
    tokens_placed = P("mp", ("clips", "seq"), None)
    return jax.shard_map(
        per_device,
        mesh=mesh,
        in_specs=(tokens_placed,) * 4 + (P("mp", None, None),),
        out_specs=(tokens_placed,) * 4,
        check_vma=False,
    )
```

```python
import functools

import jax
import jax.numpy as jnp
from jax import lax
from jax.experimental import pallas as pl
from jax.experimental.pallas import tpu as pltpu
from jax.sharding import PartitionSpec as P

GX = 8
LOG2E = 1.4426950408889634
LOWEST = -3.0e38
VMEM_LIMIT = 24 * 1024 * 1024


def channel_list(tile_count):
    row_tiles = min(4, tile_count // GX)
    layer_size = GX * row_tiles
    distances = [1]
    if row_tiles > 1:
        distances.append(GX)
    if tile_count // layer_size > 1:
        distances.append(layer_size)
    return [(distance, colour) for distance in distances for colour in (0, 1)]


def swap_route(channel, tile_count):
    distance, colour = channel
    route = []
    for low in range(tile_count - distance):
        if (low // distance) % 2 == colour:
            route += [(low, low + distance), (low + distance, low)]
    return route


def swapped(block, channel):
    return lax.ppermute(block, "seq", swap_route(channel, lax.axis_size("seq")))


def partner_of(own_tile, channel):
    distance, colour = channel
    is_low = lax.rem(lax.div(own_tile, distance), 2) == colour
    return jnp.where(is_low, own_tile + distance, own_tile - distance)


def dot_nt(a, b):
    return lax.dot_general(a, b, (((1,), (1,)), ((), ())), preferred_element_type=jnp.float32)


def dot_tn(a, b):
    return lax.dot_general(a, b, (((0,), (0,)), ((), ())), preferred_element_type=jnp.float32)


def dot_nn(a, b):
    return lax.dot_general(a, b, (((1,), (0,)), ((), ())), preferred_element_type=jnp.float32)


class Table:
    def __init__(self, ref, heads, count, cap):
        self.ref, self.heads, self.count, self.cap = ref, heads, count, cap

    def slot_at(self, head, number):
        return head * self.count + number

    def reader_at(self, number, slot):
        return self.heads * self.count + number * self.cap + slot

    def owner_at(self, number, slot):
        return self.reader_at(self.count + number, slot)

    def size(self):
        return self.owner_at(self.count - 1, self.cap - 1) + 1


def names(lists, head, reader, tile):
    entries = range(1, lists.shape[1])
    return functools.reduce(jnp.logical_or, [lists[head, entry, reader] == tile for entry in entries])


def pack_keys_kernel(cap, channel, lists_hbm, keys, values, target, lists, held, sems):
    heads, _, tile_count = lists.shape
    loads = [pltpu.make_async_copy(lists_hbm, lists, sems.at[2, 0])]
    for part, source in enumerate((keys, values)):
        for head in range(heads):
            loads.append(
                pltpu.make_async_copy(source.at[head], held.at[part, head], sems.at[part, head])
            )
    for load in loads:
        load.start()
    loads[0].wait()
    own_tile = lax.axis_index("seq")
    partner = partner_of(own_tile, channel)
    inside = (partner >= 0) & (partner < tile_count)
    reader = jnp.clip(partner, 0, tile_count - 1)
    filled = jnp.int32(0)
    chosen = [jnp.int32(0)] * cap
    for head in range(heads):
        wanted = names(lists, head, reader, own_tile) & inside
        for slot in range(cap):
            chosen[slot] = jnp.where(wanted & (filled == slot), head, chosen[slot])
        filled = filled + wanted.astype(jnp.int32)
    for load in loads[1:]:
        load.wait()
    for slot in range(cap):
        for part in range(2):
            target[part, slot] = held[part, chosen[slot]]


def pack_more_keys_kernel(count, cap, number, table_ref, keys, values, target, sems):
    table = Table(table_ref, keys.shape[0], count, cap)
    for stage in ("start", "wait"):
        for slot in range(cap):
            head = table_ref[table.owner_at(number, slot)]

            @pl.when(head >= 0)
            def _():
                for part, source in enumerate((keys, values)):
                    copy = pltpu.make_async_copy(
                        source.at[head], target.at[part, slot], sems.at[part, slot]
                    )
                    if stage == "start":
                        copy.start()
                    else:
                        copy.wait()


def table_kernel(channels, cap, lists, table_ref):
    heads, _, tile_count = lists.shape
    table = Table(table_ref, heads, len(channels), cap)
    own_tile = lax.axis_index("seq")
    for number, channel in enumerate(channels):
        partner = partner_of(own_tile, channel)
        inside = (partner >= 0) & (partner < tile_count)
        reader = jnp.clip(partner, 0, tile_count - 1)
        for slot in range(cap):
            table_ref[table.owner_at(number, slot)] = -1
            table_ref[table.reader_at(number, slot)] = -1
        filled = [jnp.int32(0), jnp.int32(0)]
        for head in range(heads):
            given = names(lists, head, reader, own_tile) & inside & (filled[0] < cap)
            named = names(lists, head, own_tile, partner) & inside & (filled[1] < cap)
            table_ref[table.slot_at(head, number)] = jnp.where(named, filled[1], -1)

            @pl.when(given)
            def _():
                table_ref[table.owner_at(number, filled[0])] = head

            @pl.when(named)
            def _():
                table_ref[table.reader_at(number, filled[1])] = head

            filled = [filled[0] + given.astype(jnp.int32), filled[1] + named.astype(jnp.int32)]


def own_kernel(count, cap, scale, table_ref, q_ref, k_ref, v_ref, g_ref, queries, grads, *rest):
    weight_ref, prob_grad_ref, rows_ref, *targets, sems = rest
    heads = queries.shape[0]
    table = Table(table_ref, heads, count, cap)

    def copies(stage):
        for number in range(count):
            for slot in range(cap):
                head = table_ref[table.reader_at(number, slot)]

                @pl.when(head >= 0)
                def _():
                    for part, source in enumerate((queries, grads)):
                        copy = pltpu.make_async_copy(
                            source.at[head],
                            targets[number].at[part, slot],
                            sems.at[number, part, slot],
                        )
                        if stage == "start":
                            copy.start()
                        else:
                            copy.wait()

    pl.when(pl.program_id(0) == 0)(lambda: copies("start"))
    score = dot_nt(k_ref[0], q_ref[0]) * (scale * LOG2E)
    top = jnp.max(score, axis=0, keepdims=True)
    weight = jnp.exp2(score - top)
    prob_grad = dot_nt(v_ref[0], g_ref[0])
    weight_ref[0] = weight
    prob_grad_ref[0] = prob_grad
    rows_ref[0, 0:1] = top
    rows_ref[0, 1:2] = jnp.sum(weight, axis=0, keepdims=True)
    rows_ref[0, 2:3] = jnp.sum(weight * prob_grad, axis=0, keepdims=True)
    pl.when(pl.program_id(0) == heads - 1)(lambda: copies("wait"))


def statistics_kernel(count, cap, scale, table_ref, q_ref, g_ref, own_rows, *rest):
    fetched, rest = rest[:count], rest[count:]
    weight_ref, prob_grad_ref, own_factors, far_factors = rest[:4]
    stats, far_rows = rest[4 : 4 + count], rest[4 + count]
    heads = q_ref.shape[0]
    table = Table(table_ref, heads, count, cap)
    for number in range(count):
        for slot in range(cap):
            head = jnp.maximum(table_ref[table.reader_at(number, slot)], 0)
            place = number * cap + slot
            score = dot_nt(fetched[number][0, slot], q_ref[head]) * (scale * LOG2E)
            top = jnp.max(score, axis=0, keepdims=True)
            weight = jnp.exp2(score - top)
            prob_grad = dot_nt(fetched[number][1, slot], g_ref[head])
            weight_ref[place] = weight
            prob_grad_ref[place] = prob_grad
            far_rows[place, 0:1] = top
            far_rows[place, 1:2] = jnp.sum(weight, axis=0, keepdims=True)
            far_rows[place, 2:3] = jnp.sum(weight * prob_grad, axis=0, keepdims=True)
    for head in range(heads):
        rows = [own_rows[head]]
        slots = [table_ref[table.slot_at(head, number)] for number in range(count)]
        for number in range(count):
            found = far_rows[number * cap + jnp.maximum(slots[number], 0)]
            missing = jnp.where(
                lax.broadcasted_iota(jnp.int32, found.shape, 0) == 0, LOWEST, 0.0
            )
            rows.append(jnp.where(slots[number] >= 0, found, missing))
        top = functools.reduce(jnp.maximum, [row[0:1] for row in rows])
        factors = [jnp.exp2(row[0:1] - top) for row in rows]
        total = sum(factor * row[1:2] for factor, row in zip(factors, rows))
        inverse = 1.0 / total
        delta = sum(factor * row[2:3] for factor, row in zip(factors, rows)) * inverse
        level = top + jnp.log2(total)
        own_factors[head, 0:1] = factors[0] * inverse
        own_factors[head, 1:2] = delta
        for number in range(count):

            @pl.when(slots[number] >= 0)
            def _():
                place = number * cap + slots[number]
                far_factors[place, 0:1] = factors[1 + number] * inverse
                far_factors[place, 1:2] = delta
                stats[number][slots[number], 0:1] = level
                stats[number][slots[number], 1:2] = delta


def reader_kernel(count, cap, scale, table_ref, q_ref, k_ref, v_ref, g_ref, *rest):
    own_weight, own_prob_grad, own_factors, far_weight, far_prob_grad, far_factors = rest[:6]
    fetched, rest = rest[6 : 6 + count], rest[6 + count :]
    o_ref, dq_ref, dk_ref, dv_ref, o_sum, dq_sum = rest
    heads = q_ref.shape[0]
    table = Table(table_ref, heads, count, cap)

    def softmax_grad(weight, prob_grad, factors):
        prob = weight * factors[0:1]
        score_grad = prob * (prob_grad - factors[1:2])
        return prob.astype(jnp.bfloat16), score_grad.astype(jnp.bfloat16)

    for head in range(heads):
        prob, score_grad = softmax_grad(own_weight[head], own_prob_grad[head], own_factors[head])
        o_sum[head] = dot_tn(v_ref[head], prob)
        dq_sum[head] = dot_tn(k_ref[head], score_grad)
        dk_ref[head] = dot_nn(score_grad, q_ref[head]) * scale
        dv_ref[head] = dot_nn(prob, g_ref[head])
    for number in range(count):
        for slot in range(cap):
            head = table_ref[table.reader_at(number, slot)]
            place = number * cap + slot

            @pl.when(head >= 0)
            def _():
                prob, score_grad = softmax_grad(
                    far_weight[place], far_prob_grad[place], far_factors[place]
                )
                o_sum[head] += dot_tn(fetched[number][1, slot], prob)
                dq_sum[head] += dot_tn(fetched[number][0, slot], score_grad)

    for head in range(heads):
        o_ref[head] = o_sum[head].T.astype(jnp.bfloat16)
        dq_ref[head] = (dq_sum[head] * scale).T.astype(jnp.bfloat16)


def owner_terms(table, number, scale, k_ref, v_ref, arrived, stats, slot):
    found = table.ref[table.owner_at(number, slot)]
    head = jnp.maximum(found, 0)
    query, grad = arrived[0, slot], arrived[1, slot]
    score = dot_nt(k_ref[head], query) * (scale * LOG2E)
    prob = jnp.exp2(score - stats[slot, 0:1])
    prob_grad = dot_nt(v_ref[head], grad)
    score_grad = (prob * (prob_grad - stats[slot, 1:2])).astype(jnp.bfloat16)
    dk_term = dot_nn(score_grad, query) * scale
    dv_term = dot_nn(prob.astype(jnp.bfloat16), grad)
    return found, head, jnp.where(found >= 0, dk_term, 0.0), jnp.where(found >= 0, dv_term, 0.0)


def owner_kernel(count, cap, scale, number, table_ref, k_ref, v_ref, dk_in, dv_in, *rest):
    arrived, stats, dk_sum, dv_sum, *rounded = rest
    heads = k_ref.shape[0]
    table = Table(table_ref, heads, count, cap)
    for head in range(heads):
        dk_sum[head] = dk_in[head]
        dv_sum[head] = dv_in[head]
    for slot in range(cap):
        _, head, dk_term, dv_term = owner_terms(
            table, number, scale, k_ref, v_ref, arrived, stats, slot
        )
        dk_sum[head] += dk_term
        dv_sum[head] += dv_term
    for head in range(heads if rounded else 0):
        rounded[0][head] = dk_sum[head].astype(jnp.bfloat16)
        rounded[1][head] = dv_sum[head].astype(jnp.bfloat16)


def last_owner_kernel(count, cap, scale, table_ref, k_ref, v_ref, dk_in, dv_in, *rest):
    arrived, stats, _, _, dk_out, dv_out, staged, sems = rest
    table = Table(table_ref, k_ref.shape[0], count, cap)
    copies = []
    for slot in range(cap):
        found, head, dk_term, dv_term = owner_terms(
            table, 0, scale, k_ref, v_ref, arrived, stats, slot
        )
        staged[0, slot] = (dk_in[head] + dk_term).astype(jnp.bfloat16)
        staged[1, slot] = (dv_in[head] + dv_term).astype(jnp.bfloat16)
        for part, result in enumerate((dk_out, dv_out)):
            copy = pltpu.make_async_copy(
                staged.at[part, slot], result.at[head], sems.at[part, slot]
            )
            copies.append((found, copy))
    for found, copy in copies:
        pl.when(found >= 0)(copy.start)
    for found, copy in copies:
        pl.when(found >= 0)(copy.wait)


def per_device(queries, keys, values, out_grad, tile_lists):
    heads, tokens, width = queries.shape
    channels = channel_list(lax.axis_size("seq"))
    count = len(channels)
    cap = heads // 2
    scale = width ** (-0.5)
    table_size = Table(None, heads, count, cap).size()
    smem = pl.BlockSpec(memory_space=pltpu.SMEM)
    anywhere = pl.BlockSpec(memory_space=pl.ANY)
    vmem = pl.BlockSpec(memory_space=pltpu.VMEM)
    params = pltpu.CompilerParams(vmem_limit_bytes=VMEM_LIMIT)
    brief = pl.CostEstimate(flops=1, bytes_accessed=1, transcendentals=0)
    packed = pltpu.VMEM((2, cap, tokens, width), jnp.bfloat16)
    whole = jax.ShapeDtypeStruct((heads, tokens, width), jnp.bfloat16)
    whole_sum = pltpu.VMEM((heads, tokens, width), jnp.float32)
    squares = pltpu.VMEM((heads, tokens, tokens), jnp.float32)
    far_squares = pltpu.VMEM((count * cap, tokens, tokens), jnp.float32)
    row_stats = pltpu.VMEM((cap, 2, tokens), jnp.float32)
    copies = pltpu.SemaphoreType.DMA((count, 2, cap))
    lists, q_far, k_far, v_far, g_far = (
        pltpu.with_memory_space_constraint(array, pltpu.HBM)
        for array in (jnp.swapaxes(tile_lists, 1, 2), queries, keys, values, out_grad)
    )
    table = pl.pallas_call(
        functools.partial(table_kernel, channels, cap),
        out_shape=jax.ShapeDtypeStruct((table_size,), jnp.int32),
        in_specs=[smem],
        out_specs=smem,
        compiler_params=params,
        cost_estimate=brief,
        name="table",
    )(lists)
    fetched = []
    for number, channel in enumerate(channels):
        first = number == 0
        pack = (
            functools.partial(pack_keys_kernel, cap, channel)
            if first
            else functools.partial(pack_more_keys_kernel, count, cap, number)
        )
        key_value = pl.pallas_call(
            pack,
            out_shape=packed,
            in_specs=[anywhere if first else smem, anywhere, anywhere],
            out_specs=vmem,
            scratch_shapes=[
                pltpu.SMEM(lists.shape, jnp.int32),
                pltpu.VMEM((2, heads, tokens, width), jnp.bfloat16),
                pltpu.SemaphoreType.DMA((3, heads)),
            ]
            if first
            else [pltpu.SemaphoreType.DMA((2, cap))],
            compiler_params=params,
            cost_estimate=brief,
            name="pack_keys",
        )(lists if first else table, k_far, v_far)
        fetched.append(swapped(key_value, channel))
    one_head = pl.BlockSpec((1, tokens, width), lambda head: (head, 0, 0))
    one_square = pl.BlockSpec((1, tokens, tokens), lambda head: (head, 0, 0))
    own_weight, own_prob_grad, own_rows, *query_grads = pl.pallas_call(
        functools.partial(own_kernel, count, cap, scale),
        grid=(heads,),
        out_shape=[squares] * 2 + [pltpu.VMEM((heads, 3, tokens), jnp.float32)] + [packed] * count,
        in_specs=[smem] + [one_head] * 4 + [anywhere] * 2,
        out_specs=[one_square] * 2
        + [pl.BlockSpec((1, 3, tokens), lambda head: (head, 0, 0))]
        + [pl.BlockSpec(memory_space=pltpu.VMEM)] * count,
        scratch_shapes=[copies],
        compiler_params=params,
        cost_estimate=brief,
        name="own_scores",
    )(table, q_far, k_far, v_far, g_far, q_far, g_far)
    query_grads[1:], fetched[0] = lax.optimization_barrier((query_grads[1:], fetched[0]))
    arrived = [swapped(block, channel) for block, channel in zip(query_grads, channels)]
    far_weight, far_prob_grad, own_factors, far_factors, *stats = pl.pallas_call(
        functools.partial(statistics_kernel, count, cap, scale),
        out_shape=[far_squares] * 2
        + [pltpu.VMEM((heads, 2, tokens), jnp.float32)]
        + [pltpu.VMEM((count * cap, 2, tokens), jnp.float32)]
        + [row_stats] * count,
        in_specs=[smem] + [vmem] * (3 + count),
        out_specs=[vmem] * (4 + count),
        scratch_shapes=[pltpu.VMEM((count * cap, 3, tokens), jnp.float32)],
        compiler_params=params,
        cost_estimate=brief,
        name="statistics",
    )(table, queries, out_grad, own_rows, *fetched)
    stats = [swapped(block, channel) for block, channel in zip(stats, channels)]
    transposed_sums = pltpu.VMEM((heads, width, tokens), jnp.float32)
    attn_out, query_grad, key_sum, value_sum = pl.pallas_call(
        functools.partial(reader_kernel, count, cap, scale),
        out_shape=[whole] * 2 + [whole_sum] * 2,
        in_specs=[smem] + [vmem] * (10 + count),
        out_specs=[vmem] * 4,
        scratch_shapes=[transposed_sums] * 2,
        compiler_params=params,
        cost_estimate=pl.CostEstimate(flops=100000000000, bytes_accessed=1, transcendentals=0),
        name="reader",
    )(
        table,
        queries,
        keys,
        values,
        out_grad,
        own_weight,
        own_prob_grad,
        own_factors,
        far_weight,
        far_prob_grad,
        far_factors,
        *fetched,
    )
    sums = [key_sum, value_sum]
    for number in range(count - 1, 0, -1):
        closing = number == 1
        sums = pl.pallas_call(
            functools.partial(owner_kernel, count, cap, scale, number),
            out_shape=[whole_sum] * 2 + [whole] * (2 if closing else 0),
            in_specs=[smem] + [vmem] * 6,
            out_specs=[vmem] * (4 if closing else 2),
            compiler_params=params,
            cost_estimate=brief,
            name="owner",
        )(table, keys, values, *sums[:2], arrived[number], stats[number])
    key_sum, value_sum, *rounded = sums
    last, key_sum = lax.optimization_barrier((arrived[0], key_sum))
    key_grad, value_grad = pl.pallas_call(
        functools.partial(last_owner_kernel, count, cap, scale),
        out_shape=[whole] * 2,
        in_specs=[smem] + [vmem] * 6 + [anywhere] * 2,
        out_specs=[anywhere] * 2,
        scratch_shapes=[
            pltpu.VMEM((2, cap, tokens, width), jnp.bfloat16),
            pltpu.SemaphoreType.DMA((2, cap)),
        ],
        input_output_aliases={7: 0, 8: 1},
        compiler_params=params,
        cost_estimate=brief,
        name="last_owner",
    )(table, keys, values, key_sum, value_sum, last, stats[0], *rounded)
    return attn_out, query_grad, key_grad, value_grad


def solution(mesh):
    tokens_placed = P("mp", ("clips", "seq"), None)
    return jax.shard_map(
        per_device,
        mesh=mesh,
        in_specs=(tokens_placed,) * 4 + (P("mp", None, None),),
        out_specs=(tokens_placed,) * 4,
        check_vma=False,
    )
```

```python
import functools

import jax
import jax.numpy as jnp
from jax import lax
from jax.experimental import pallas as pl
from jax.experimental.pallas import tpu as pltpu
from jax.sharding import PartitionSpec as P

GX = 8
LOG2E = 1.4426950408889634
LOWEST = -3.0e38
VMEM_LIMIT = 24 * 1024 * 1024


def channel_list(tile_count):
    row_tiles = min(4, tile_count // GX)
    layer_size = GX * row_tiles
    distances = [1]
    if row_tiles > 1:
        distances.append(GX)
    if tile_count // layer_size > 1:
        distances.append(layer_size)
    return [(distance, colour) for distance in distances for colour in (0, 1)]


def swap_route(channel, tile_count):
    distance, colour = channel
    route = []
    for low in range(tile_count - distance):
        if (low // distance) % 2 == colour:
            route += [(low, low + distance), (low + distance, low)]
    return route


def swapped(block, channel):
    return lax.ppermute(block, "seq", swap_route(channel, lax.axis_size("seq")))


def partner_of(own_tile, channel):
    distance, colour = channel
    is_low = lax.rem(lax.div(own_tile, distance), 2) == colour
    return jnp.where(is_low, own_tile + distance, own_tile - distance)


def dot_nt(a, b):
    return lax.dot_general(a, b, (((1,), (1,)), ((), ())), preferred_element_type=jnp.float32)


def dot_tn(a, b):
    return lax.dot_general(a, b, (((0,), (0,)), ((), ())), preferred_element_type=jnp.float32)


def dot_nn(a, b):
    return lax.dot_general(a, b, (((1,), (0,)), ((), ())), preferred_element_type=jnp.float32)


class Table:
    def __init__(self, ref, heads, count, cap):
        self.ref, self.heads, self.count, self.cap = ref, heads, count, cap

    def slot_at(self, head, number):
        return head * self.count + number

    def reader_at(self, number, slot):
        return self.heads * self.count + number * self.cap + slot

    def owner_at(self, number, slot):
        return self.reader_at(self.count + number, slot)

    def size(self):
        return self.owner_at(self.count - 1, self.cap - 1) + 1


def names(lists, head, reader, tile):
    entries = range(1, lists.shape[1])
    return functools.reduce(jnp.logical_or, [lists[head, entry, reader] == tile for entry in entries])


def pack_keys_kernel(cap, channel, lists_hbm, keys, values, target, lists, held, sems):
    heads, _, tile_count = lists.shape
    loads = [pltpu.make_async_copy(lists_hbm, lists, sems.at[2, 0])]
    for part, source in enumerate((keys, values)):
        for head in range(heads):
            loads.append(
                pltpu.make_async_copy(source.at[head], held.at[part, head], sems.at[part, head])
            )
    for load in loads:
        load.start()
    loads[0].wait()
    own_tile = lax.axis_index("seq")
    partner = partner_of(own_tile, channel)
    inside = (partner >= 0) & (partner < tile_count)
    reader = jnp.clip(partner, 0, tile_count - 1)
    filled = jnp.int32(0)
    chosen = [jnp.int32(0)] * cap
    for head in range(heads):
        wanted = names(lists, head, reader, own_tile) & inside
        for slot in range(cap):
            chosen[slot] = jnp.where(wanted & (filled == slot), head, chosen[slot])
        filled = filled + wanted.astype(jnp.int32)
    for load in loads[1:]:
        load.wait()
    for slot in range(cap):
        for part in range(2):
            target[part, slot] = held[part, chosen[slot]]


def pack_more_keys_kernel(count, cap, number, table_ref, keys, values, target, sems):
    table = Table(table_ref, keys.shape[0], count, cap)
    for stage in ("start", "wait"):
        for slot in range(cap):
            head = table_ref[table.owner_at(number, slot)]

            @pl.when(head >= 0)
            def _():
                for part, source in enumerate((keys, values)):
                    copy = pltpu.make_async_copy(
                        source.at[head], target.at[part, slot], sems.at[part, slot]
                    )
                    if stage == "start":
                        copy.start()
                    else:
                        copy.wait()


def table_kernel(channels, cap, lists, table_ref):
    heads, _, tile_count = lists.shape
    table = Table(table_ref, heads, len(channels), cap)
    own_tile = lax.axis_index("seq")
    for number, channel in enumerate(channels):
        partner = partner_of(own_tile, channel)
        inside = (partner >= 0) & (partner < tile_count)
        reader = jnp.clip(partner, 0, tile_count - 1)
        for slot in range(cap):
            table_ref[table.owner_at(number, slot)] = -1
            table_ref[table.reader_at(number, slot)] = -1
        filled = [jnp.int32(0), jnp.int32(0)]
        for head in range(heads):
            given = names(lists, head, reader, own_tile) & inside & (filled[0] < cap)
            named = names(lists, head, own_tile, partner) & inside & (filled[1] < cap)
            table_ref[table.slot_at(head, number)] = jnp.where(named, filled[1], -1)

            @pl.when(given)
            def _():
                table_ref[table.owner_at(number, filled[0])] = head

            @pl.when(named)
            def _():
                table_ref[table.reader_at(number, filled[1])] = head

            filled = [filled[0] + given.astype(jnp.int32), filled[1] + named.astype(jnp.int32)]


def own_kernel(count, cap, scale, table_ref, q_ref, k_ref, v_ref, g_ref, queries, grads, *rest):
    weight_ref, prob_grad_ref, rows_ref, *targets, sems = rest
    heads = queries.shape[0]
    table = Table(table_ref, heads, count, cap)

    def copies(stage):
        for number in range(count):
            for slot in range(cap):
                head = table_ref[table.reader_at(number, slot)]

                @pl.when(head >= 0)
                def _():
                    for part, source in enumerate((queries, grads)):
                        copy = pltpu.make_async_copy(
                            source.at[head],
                            targets[number].at[part, slot],
                            sems.at[number, part, slot],
                        )
                        if stage == "start":
                            copy.start()
                        else:
                            copy.wait()

    pl.when(pl.program_id(0) == 0)(lambda: copies("start"))
    score = dot_nt(k_ref[0], q_ref[0]) * (scale * LOG2E)
    top = jnp.max(score, axis=0, keepdims=True)
    weight = jnp.exp2(score - top)
    prob_grad = dot_nt(v_ref[0], g_ref[0])
    weight_ref[0] = weight
    prob_grad_ref[0] = prob_grad
    rows_ref[0, 0:1] = top
    rows_ref[0, 1:2] = jnp.sum(weight, axis=0, keepdims=True)
    rows_ref[0, 2:3] = jnp.sum(weight * prob_grad, axis=0, keepdims=True)
    pl.when(pl.program_id(0) == heads - 1)(lambda: copies("wait"))


def statistics_kernel(count, cap, scale, table_ref, q_ref, g_ref, own_rows, *rest):
    fetched, rest = rest[:count], rest[count:]
    weight_ref, prob_grad_ref, own_factors, far_factors = rest[:4]
    stats, far_rows = rest[4 : 4 + count], rest[4 + count]
    heads = q_ref.shape[0]
    table = Table(table_ref, heads, count, cap)
    for number in range(count):
        for slot in range(cap):
            head = jnp.maximum(table_ref[table.reader_at(number, slot)], 0)
            place = number * cap + slot
            score = dot_nt(fetched[number][0, slot], q_ref[head]) * (scale * LOG2E)
            top = jnp.max(score, axis=0, keepdims=True)
            weight = jnp.exp2(score - top)
            prob_grad = dot_nt(fetched[number][1, slot], g_ref[head])
            weight_ref[place] = weight
            prob_grad_ref[place] = prob_grad
            far_rows[place, 0:1] = top
            far_rows[place, 1:2] = jnp.sum(weight, axis=0, keepdims=True)
            far_rows[place, 2:3] = jnp.sum(weight * prob_grad, axis=0, keepdims=True)
    for head in range(heads):
        rows = [own_rows[head]]
        slots = [table_ref[table.slot_at(head, number)] for number in range(count)]
        for number in range(count):
            found = far_rows[number * cap + jnp.maximum(slots[number], 0)]
            missing = jnp.where(
                lax.broadcasted_iota(jnp.int32, found.shape, 0) == 0, LOWEST, 0.0
            )
            rows.append(jnp.where(slots[number] >= 0, found, missing))
        top = functools.reduce(jnp.maximum, [row[0:1] for row in rows])
        factors = [jnp.exp2(row[0:1] - top) for row in rows]
        total = sum(factor * row[1:2] for factor, row in zip(factors, rows))
        inverse = 1.0 / total
        delta = sum(factor * row[2:3] for factor, row in zip(factors, rows)) * inverse
        level = top + jnp.log2(total)
        own_factors[head, 0:1] = factors[0] * inverse
        own_factors[head, 1:2] = delta
        for number in range(count):

            @pl.when(slots[number] >= 0)
            def _():
                place = number * cap + slots[number]
                far_factors[place, 0:1] = factors[1 + number] * inverse
                far_factors[place, 1:2] = delta
                stats[number][slots[number], 0:1] = level
                stats[number][slots[number], 1:2] = delta


def reader_kernel(count, cap, scale, table_ref, q_ref, k_ref, v_ref, g_ref, *rest):
    own_weight, own_prob_grad, own_factors, far_weight, far_prob_grad, far_factors = rest[:6]
    fetched, rest = rest[6 : 6 + count], rest[6 + count :]
    o_ref, dq_ref, dk_ref, dv_ref, o_sum, dq_sum = rest
    heads = q_ref.shape[0]
    table = Table(table_ref, heads, count, cap)

    def softmax_grad(weight, prob_grad, factors):
        prob = weight * factors[0:1]
        score_grad = prob * (prob_grad - factors[1:2])
        return prob.astype(jnp.bfloat16), score_grad.astype(jnp.bfloat16)

    for head in range(heads):
        prob, score_grad = softmax_grad(own_weight[head], own_prob_grad[head], own_factors[head])
        o_sum[head] = dot_tn(v_ref[head], prob)
        dq_sum[head] = dot_tn(k_ref[head], score_grad)
        dk_ref[head] = dot_nn(score_grad, q_ref[head]) * scale
        dv_ref[head] = dot_nn(prob, g_ref[head])
    for number in range(count):
        for slot in range(cap):
            head = table_ref[table.reader_at(number, slot)]
            place = number * cap + slot

            @pl.when(head >= 0)
            def _():
                prob, score_grad = softmax_grad(
                    far_weight[place], far_prob_grad[place], far_factors[place]
                )
                o_sum[head] += dot_tn(fetched[number][1, slot], prob)
                dq_sum[head] += dot_tn(fetched[number][0, slot], score_grad)

    for head in range(heads):
        o_ref[head] = o_sum[head].T.astype(jnp.bfloat16)
        dq_ref[head] = (dq_sum[head] * scale).T.astype(jnp.bfloat16)


def owner_terms(table, number, scale, k_ref, v_ref, arrived, stats, slot):
    found = table.ref[table.owner_at(number, slot)]
    head = jnp.maximum(found, 0)
    query, grad = arrived[0, slot], arrived[1, slot]
    score = dot_nt(k_ref[head], query) * (scale * LOG2E)
    prob = jnp.exp2(score - stats[slot, 0:1])
    prob_grad = dot_nt(v_ref[head], grad)
    score_grad = (prob * (prob_grad - stats[slot, 1:2])).astype(jnp.bfloat16)
    dk_term = dot_nn(score_grad, query) * scale
    dv_term = dot_nn(prob.astype(jnp.bfloat16), grad)
    return found, head, jnp.where(found >= 0, dk_term, 0.0), jnp.where(found >= 0, dv_term, 0.0)


def owner_kernel(count, cap, scale, number, table_ref, k_ref, v_ref, *rest):
    arrived, stats, _, _, dk_sum, dv_sum = rest
    table = Table(table_ref, k_ref.shape[0], count, cap)
    for slot in range(cap):
        _, head, dk_term, dv_term = owner_terms(
            table, number, scale, k_ref, v_ref, arrived, stats, slot
        )
        dk_sum[head] += dk_term
        dv_sum[head] += dv_term


def last_owner_kernel(count, cap, scale, table_ref, k_ref, v_ref, *rest):
    arrived, stats, dk_in, dv_in, dk_out, dv_out, rounded, staged, sems, staged_sems = rest
    heads = k_ref.shape[0]
    table = Table(table_ref, heads, count, cap)
    owners = [table_ref[table.owner_at(0, slot)] for slot in range(cap)]
    copies = []
    for head in range(heads):
        untouched = functools.reduce(jnp.logical_and, [owner != head for owner in owners])
        for part, (total, result) in enumerate(((dk_in, dk_out), (dv_in, dv_out))):
            rounded[part, head] = total[head].astype(jnp.bfloat16)
            copy = pltpu.make_async_copy(
                rounded.at[part, head], result.at[head], sems.at[part, head]
            )
            copies.append((untouched, copy))
    for wanted, copy in copies:
        pl.when(wanted)(copy.start)
    for slot in range(cap):
        found, head, dk_term, dv_term = owner_terms(
            table, 0, scale, k_ref, v_ref, arrived, stats, slot
        )
        staged[0, slot] = (dk_in[head] + dk_term).astype(jnp.bfloat16)
        staged[1, slot] = (dv_in[head] + dv_term).astype(jnp.bfloat16)
        for part, result in enumerate((dk_out, dv_out)):
            copy = pltpu.make_async_copy(
                staged.at[part, slot], result.at[head], staged_sems.at[part, slot]
            )
            copies.append((found >= 0, copy))
            pl.when(found >= 0)(copy.start)
    for wanted, copy in copies:
        pl.when(wanted)(copy.wait)


def per_device(queries, keys, values, out_grad, tile_lists):
    heads, tokens, width = queries.shape
    channels = channel_list(lax.axis_size("seq"))
    count = len(channels)
    cap = heads // 2
    scale = width ** (-0.5)
    table_size = Table(None, heads, count, cap).size()
    smem = pl.BlockSpec(memory_space=pltpu.SMEM)
    anywhere = pl.BlockSpec(memory_space=pl.ANY)
    vmem = pl.BlockSpec(memory_space=pltpu.VMEM)
    params = pltpu.CompilerParams(vmem_limit_bytes=VMEM_LIMIT)
    brief = pl.CostEstimate(flops=1, bytes_accessed=1, transcendentals=0)
    packed = pltpu.VMEM((2, cap, tokens, width), jnp.bfloat16)
    whole = jax.ShapeDtypeStruct((heads, tokens, width), jnp.bfloat16)
    whole_sum = pltpu.VMEM((heads, tokens, width), jnp.float32)
    squares = pltpu.VMEM((heads, tokens, tokens), jnp.float32)
    far_squares = pltpu.VMEM((count * cap, tokens, tokens), jnp.float32)
    row_stats = pltpu.VMEM((cap, 2, tokens), jnp.float32)
    copies = pltpu.SemaphoreType.DMA((count, 2, cap))
    lists, q_far, k_far, v_far, g_far = (
        pltpu.with_memory_space_constraint(array, pltpu.HBM)
        for array in (jnp.swapaxes(tile_lists, 1, 2), queries, keys, values, out_grad)
    )
    key_value, lists = pl.pallas_call(
        functools.partial(pack_keys_kernel, cap, channels[0]),
        out_shape=[packed, pltpu.SMEM(lists.shape, jnp.int32)],
        in_specs=[anywhere] * 3,
        out_specs=[vmem, smem],
        scratch_shapes=[
            pltpu.VMEM((2, heads, tokens, width), jnp.bfloat16),
            pltpu.SemaphoreType.DMA((3, heads)),
        ],
        compiler_params=params,
        cost_estimate=brief,
        name="pack_keys",
    )(lists, k_far, v_far)
    fetched = [swapped(key_value, channels[0])]
    table = pl.pallas_call(
        functools.partial(table_kernel, channels, cap),
        out_shape=pltpu.SMEM((table_size,), jnp.int32),
        in_specs=[smem],
        out_specs=smem,
        compiler_params=params,
        cost_estimate=brief,
        name="table",
    )(lists)
    for number in range(1, count):
        key_value = pl.pallas_call(
            functools.partial(pack_more_keys_kernel, count, cap, number),
            out_shape=packed,
            in_specs=[smem, anywhere, anywhere],
            out_specs=vmem,
            scratch_shapes=[pltpu.SemaphoreType.DMA((2, cap))],
            compiler_params=params,
            cost_estimate=brief,
            name="pack_more_keys",
        )(table, k_far, v_far)
        fetched.append(swapped(key_value, channels[number]))
    one_head = pl.BlockSpec((1, tokens, width), lambda head: (head, 0, 0))
    one_square = pl.BlockSpec((1, tokens, tokens), lambda head: (head, 0, 0))
    own_weight, own_prob_grad, own_rows, *query_grads = pl.pallas_call(
        functools.partial(own_kernel, count, cap, scale),
        grid=(heads,),
        out_shape=[squares] * 2 + [pltpu.VMEM((heads, 3, tokens), jnp.float32)] + [packed] * count,
        in_specs=[smem] + [one_head] * 4 + [anywhere] * 2,
        out_specs=[one_square] * 2
        + [pl.BlockSpec((1, 3, tokens), lambda head: (head, 0, 0))]
        + [pl.BlockSpec(memory_space=pltpu.VMEM)] * count,
        scratch_shapes=[copies],
        compiler_params=params,
        cost_estimate=brief,
        name="own_scores",
    )(table, q_far, k_far, v_far, g_far, q_far, g_far)
    query_grads[1:], fetched[0] = lax.optimization_barrier((query_grads[1:], fetched[0]))
    arrived = [swapped(block, channel) for block, channel in zip(query_grads, channels)]
    far_weight, far_prob_grad, own_factors, far_factors, *stats = pl.pallas_call(
        functools.partial(statistics_kernel, count, cap, scale),
        out_shape=[far_squares] * 2
        + [pltpu.VMEM((heads, 2, tokens), jnp.float32)]
        + [pltpu.VMEM((count * cap, 2, tokens), jnp.float32)]
        + [row_stats] * count,
        in_specs=[smem] + [vmem] * (3 + count),
        out_specs=[vmem] * (4 + count),
        scratch_shapes=[pltpu.VMEM((count * cap, 3, tokens), jnp.float32)],
        compiler_params=params,
        cost_estimate=brief,
        name="statistics",
    )(table, queries, out_grad, own_rows, *fetched)
    stats = [swapped(block, channel) for block, channel in zip(stats, channels)]
    transposed_sums = pltpu.VMEM((heads, width, tokens), jnp.float32)
    attn_out, query_grad, key_sum, value_sum = pl.pallas_call(
        functools.partial(reader_kernel, count, cap, scale),
        out_shape=[whole] * 2 + [whole_sum] * 2,
        in_specs=[smem] + [vmem] * (10 + count),
        out_specs=[vmem] * 4,
        scratch_shapes=[transposed_sums] * 2,
        compiler_params=params,
        cost_estimate=pl.CostEstimate(flops=100000000000, bytes_accessed=1, transcendentals=0),
        name="reader",
    )(
        table,
        queries,
        keys,
        values,
        out_grad,
        own_weight,
        own_prob_grad,
        own_factors,
        far_weight,
        far_prob_grad,
        far_factors,
        *fetched,
    )
    for number in range(count - 1, 0, -1):
        key_sum, value_sum = pl.pallas_call(
            functools.partial(owner_kernel, count, cap, scale, number),
            out_shape=[whole_sum] * 2,
            in_specs=[smem] + [vmem] * 6,
            out_specs=[vmem] * 2,
            input_output_aliases={5: 0, 6: 1},
            compiler_params=params,
            cost_estimate=brief,
            name="owner",
        )(table, keys, values, arrived[number], stats[number], key_sum, value_sum)
    last, key_sum = lax.optimization_barrier((arrived[0], key_sum))
    key_grad, value_grad = pl.pallas_call(
        functools.partial(last_owner_kernel, count, cap, scale),
        out_shape=[whole] * 2,
        in_specs=[smem] + [vmem] * 6,
        out_specs=[anywhere] * 2,
        scratch_shapes=[
            pltpu.VMEM((2, heads, tokens, width), jnp.bfloat16),
            pltpu.VMEM((2, cap, tokens, width), jnp.bfloat16),
            pltpu.SemaphoreType.DMA((2, heads)),
            pltpu.SemaphoreType.DMA((2, cap)),
        ],
        compiler_params=params,
        cost_estimate=brief,
        name="last_owner",
    )(table, keys, values, last, stats[0], key_sum, value_sum)
    return attn_out, query_grad, key_grad, value_grad


def solution(mesh):
    tokens_placed = P("mp", ("clips", "seq"), None)
    return jax.shard_map(
        per_device,
        mesh=mesh,
        in_specs=(tokens_placed,) * 4 + (P("mp", None, None),),
        out_specs=(tokens_placed,) * 4,
        check_vma=False,
    )
```

```python
import functools

import jax
import jax.numpy as jnp
from jax import lax
from jax.experimental import pallas as pl
from jax.experimental.pallas import tpu as pltpu
from jax.sharding import PartitionSpec as P

GX = 8
LOG2E = 1.4426950408889634
LOWEST = -3.0e38
VMEM_LIMIT = 24 * 1024 * 1024


def channel_list(tile_count):
    row_tiles = min(4, tile_count // GX)
    layer_size = GX * row_tiles
    distances = [1]
    if row_tiles > 1:
        distances.append(GX)
    if tile_count // layer_size > 1:
        distances.append(layer_size)
    return [(distance, colour) for distance in distances for colour in (0, 1)]


def swap_route(channel, tile_count):
    distance, colour = channel
    route = []
    for low in range(tile_count - distance):
        if (low // distance) % 2 == colour:
            route += [(low, low + distance), (low + distance, low)]
    return route


def swapped(block, channel):
    return lax.ppermute(block, "seq", swap_route(channel, lax.axis_size("seq")))


def partner_of(own_tile, channel):
    distance, colour = channel
    is_low = lax.rem(lax.div(own_tile, distance), 2) == colour
    return jnp.where(is_low, own_tile + distance, own_tile - distance)


def dot_nt(a, b):
    return lax.dot_general(a, b, (((1,), (1,)), ((), ())), preferred_element_type=jnp.float32)


def dot_tn(a, b):
    return lax.dot_general(a, b, (((0,), (0,)), ((), ())), preferred_element_type=jnp.float32)


def dot_nn(a, b):
    return lax.dot_general(a, b, (((1,), (0,)), ((), ())), preferred_element_type=jnp.float32)


class Table:
    def __init__(self, ref, heads, count, cap):
        self.ref, self.heads, self.count, self.cap = ref, heads, count, cap

    def slot_at(self, head, number):
        return head * self.count + number

    def reader_at(self, number, slot):
        return self.heads * self.count + number * self.cap + slot

    def owner_at(self, number, slot):
        return self.reader_at(self.count + number, slot)

    def size(self):
        return self.owner_at(self.count - 1, self.cap - 1) + 1


def names(lists, head, reader, tile):
    entries = range(1, lists.shape[1])
    return functools.reduce(jnp.logical_or, [lists[head, entry, reader] == tile for entry in entries])


def pack_keys_kernel(cap, channel, lists_hbm, keys, values, target, lists, *rest):
    *held, sems = rest
    heads, _, tile_count = lists.shape
    loads = [pltpu.make_async_copy(lists_hbm, lists, sems.at[2, 0])]
    for part, source in enumerate((keys, values)):
        for head in range(heads):
            loads.append(
                pltpu.make_async_copy(source.at[head], held[part].at[head], sems.at[part, head])
            )
    for load in loads:
        load.start()
    loads[0].wait()
    own_tile = lax.axis_index("seq")
    partner = partner_of(own_tile, channel)
    inside = (partner >= 0) & (partner < tile_count)
    reader = jnp.clip(partner, 0, tile_count - 1)
    filled = jnp.int32(0)
    chosen = [jnp.int32(0)] * cap
    for head in range(heads):
        wanted = names(lists, head, reader, own_tile) & inside
        for slot in range(cap):
            chosen[slot] = jnp.where(wanted & (filled == slot), head, chosen[slot])
        filled = filled + wanted.astype(jnp.int32)
    for load in loads[1:]:
        load.wait()
    for slot in range(cap):
        for part in range(2):
            target[part, slot] = held[part][chosen[slot]]


def pack_more_keys_kernel(count, cap, number, table_ref, keys, values, target, sems):
    table = Table(table_ref, keys.shape[0], count, cap)
    for stage in ("start", "wait"):
        for slot in range(cap):
            head = table_ref[table.owner_at(number, slot)]

            @pl.when(head >= 0)
            def _():
                for part, source in enumerate((keys, values)):
                    copy = pltpu.make_async_copy(
                        source.at[head], target.at[part, slot], sems.at[part, slot]
                    )
                    if stage == "start":
                        copy.start()
                    else:
                        copy.wait()


def table_kernel(channels, cap, lists, table_ref):
    heads, _, tile_count = lists.shape
    table = Table(table_ref, heads, len(channels), cap)
    own_tile = lax.axis_index("seq")
    for number, channel in enumerate(channels):
        partner = partner_of(own_tile, channel)
        inside = (partner >= 0) & (partner < tile_count)
        reader = jnp.clip(partner, 0, tile_count - 1)
        for slot in range(cap):
            table_ref[table.owner_at(number, slot)] = -1
            table_ref[table.reader_at(number, slot)] = -1
        filled = [jnp.int32(0), jnp.int32(0)]
        for head in range(heads):
            given = names(lists, head, reader, own_tile) & inside & (filled[0] < cap)
            named = names(lists, head, own_tile, partner) & inside & (filled[1] < cap)
            table_ref[table.slot_at(head, number)] = jnp.where(named, filled[1], -1)

            @pl.when(given)
            def _():
                table_ref[table.owner_at(number, filled[0])] = head

            @pl.when(named)
            def _():
                table_ref[table.reader_at(number, filled[1])] = head

            filled = [filled[0] + given.astype(jnp.int32), filled[1] + named.astype(jnp.int32)]


def own_kernel(count, cap, scale, table_ref, q_ref, k_ref, v_ref, g_ref, queries, grads, *rest):
    weight_ref, prob_grad_ref, rows_ref, *targets, sems = rest
    heads = queries.shape[0]
    table = Table(table_ref, heads, count, cap)

    def copies(stage):
        for number in range(count):
            for slot in range(targets[number].shape[1]):
                head = table_ref[table.reader_at(number, slot)]

                @pl.when(head >= 0)
                def _():
                    for part, source in enumerate((queries, grads)):
                        copy = pltpu.make_async_copy(
                            source.at[head],
                            targets[number].at[part, slot],
                            sems.at[number, part, slot],
                        )
                        if stage == "start":
                            copy.start()
                        else:
                            copy.wait()

    pl.when(pl.program_id(0) == 0)(lambda: copies("start"))
    score = dot_nt(k_ref[0], q_ref[0]) * (scale * LOG2E)
    top = jnp.max(score, axis=0, keepdims=True)
    weight = jnp.exp2(score - top)
    prob_grad = dot_nt(v_ref[0], g_ref[0])
    weight_ref[0] = weight
    prob_grad_ref[0] = prob_grad
    rows_ref[0, 0:1] = top
    rows_ref[0, 1:2] = jnp.sum(weight, axis=0, keepdims=True)
    rows_ref[0, 2:3] = jnp.sum(weight * prob_grad, axis=0, keepdims=True)
    pl.when(pl.program_id(0) == heads - 1)(lambda: copies("wait"))


def statistics_kernel(count, cap, scale, table_ref, q_ref, g_ref, own_rows, *rest):
    fetched, rest = rest[:count], rest[count:]
    weight_ref, prob_grad_ref, own_factors, far_factors = rest[:4]
    stats, far_rows = rest[4 : 4 + count], rest[4 + count]
    heads = q_ref.shape[0]
    table = Table(table_ref, heads, count, cap)
    for number in range(count):
        for slot in range(cap):
            head = jnp.maximum(table_ref[table.reader_at(number, slot)], 0)
            place = number * cap + slot
            score = dot_nt(fetched[number][0, slot], q_ref[head]) * (scale * LOG2E)
            top = jnp.max(score, axis=0, keepdims=True)
            weight = jnp.exp2(score - top)
            prob_grad = dot_nt(fetched[number][1, slot], g_ref[head])
            weight_ref[place] = weight
            prob_grad_ref[place] = prob_grad
            far_rows[place, 0:1] = top
            far_rows[place, 1:2] = jnp.sum(weight, axis=0, keepdims=True)
            far_rows[place, 2:3] = jnp.sum(weight * prob_grad, axis=0, keepdims=True)
    for head in range(heads):
        rows = [own_rows[head]]
        slots = [table_ref[table.slot_at(head, number)] for number in range(count)]
        for number in range(count):
            found = far_rows[number * cap + jnp.maximum(slots[number], 0)]
            missing = jnp.where(
                lax.broadcasted_iota(jnp.int32, found.shape, 0) == 0, LOWEST, 0.0
            )
            rows.append(jnp.where(slots[number] >= 0, found, missing))
        top = functools.reduce(jnp.maximum, [row[0:1] for row in rows])
        factors = [jnp.exp2(row[0:1] - top) for row in rows]
        total = sum(factor * row[1:2] for factor, row in zip(factors, rows))
        inverse = 1.0 / total
        delta = sum(factor * row[2:3] for factor, row in zip(factors, rows)) * inverse
        level = top + jnp.log2(total)
        own_factors[head, 0:1] = factors[0] * inverse
        own_factors[head, 1:2] = delta
        for number in range(count):

            @pl.when(slots[number] >= 0)
            def _():
                place = number * cap + slots[number]
                far_factors[place, 0:1] = factors[1 + number] * inverse
                far_factors[place, 1:2] = delta
                stats[number][slots[number], 0:1] = level
                stats[number][slots[number], 1:2] = delta


def softmax_grad(weight, prob_grad, factors):
    prob = weight * factors[0:1]
    score_grad = prob * (prob_grad - factors[1:2])
    return prob.astype(jnp.bfloat16), score_grad.astype(jnp.bfloat16)


def returned_kernel(count, cap, scale, table_ref, q_ref, g_ref, *rest):
    far_weight, far_prob_grad, far_factors, terms = rest
    table = Table(table_ref, q_ref.shape[0], count, cap)
    returned = terms.shape[1]
    for number in range(returned):
        place = cap - returned + number
        head = jnp.maximum(table_ref[table.reader_at(0, place)], 0)
        prob, score_grad = softmax_grad(
            far_weight[place], far_prob_grad[place], far_factors[place]
        )
        terms[0, number] = (dot_nn(score_grad, q_ref[head]) * scale).astype(jnp.bfloat16)
        terms[1, number] = dot_nn(prob, g_ref[head]).astype(jnp.bfloat16)


def reader_kernel(count, cap, scale, table_ref, q_ref, k_ref, v_ref, g_ref, *rest):
    own_weight, own_prob_grad, own_factors, far_weight, far_prob_grad, far_factors = rest[:6]
    fetched, rest = rest[6 : 6 + count], rest[6 + count :]
    o_ref, dq_ref, dk_ref, dv_ref, o_sum, dq_sum = rest
    heads = q_ref.shape[0]
    table = Table(table_ref, heads, count, cap)
    for head in range(heads):
        prob, score_grad = softmax_grad(own_weight[head], own_prob_grad[head], own_factors[head])
        o_sum[head] = dot_tn(v_ref[head], prob)
        dq_sum[head] = dot_tn(k_ref[head], score_grad)
        dk_ref[head] = dot_nn(score_grad, q_ref[head]) * scale
        dv_ref[head] = dot_nn(prob, g_ref[head])
    for number in range(count):
        for slot in range(cap):
            found = table_ref[table.reader_at(number, slot)]
            head = jnp.maximum(found, 0)
            place = number * cap + slot
            prob, score_grad = softmax_grad(
                far_weight[place], far_prob_grad[place], far_factors[place]
            )
            o_term = dot_tn(fetched[number][1, slot], prob)
            dq_term = dot_tn(fetched[number][0, slot], score_grad)
            o_sum[head] += jnp.where(found >= 0, o_term, 0.0)
            dq_sum[head] += jnp.where(found >= 0, dq_term, 0.0)
    for head in range(heads):
        o_ref[head] = o_sum[head].T.astype(jnp.bfloat16)
        dq_ref[head] = (dq_sum[head] * scale).T.astype(jnp.bfloat16)


def owner_terms(table, number, scale, k_ref, v_ref, arrived, stats, slot):
    found = table.ref[table.owner_at(number, slot)]
    head = jnp.maximum(found, 0)
    query, grad = arrived[0, slot], arrived[1, slot]
    score = dot_nt(k_ref[head], query) * (scale * LOG2E)
    prob = jnp.exp2(score - stats[slot, 0:1])
    prob_grad = dot_nt(v_ref[head], grad)
    score_grad = (prob * (prob_grad - stats[slot, 1:2])).astype(jnp.bfloat16)
    dk_term = dot_nn(score_grad, query) * scale
    dv_term = dot_nn(prob.astype(jnp.bfloat16), grad)
    return found, head, jnp.where(found >= 0, dk_term, 0.0), jnp.where(found >= 0, dv_term, 0.0)


def owner_kernel(count, cap, scale, number, table_ref, k_ref, v_ref, arrived, stats, *rest):
    *rest, dk_sum, dv_sum, rounded, sems, rounded_sems = rest
    heads = k_ref.shape[0]
    table = Table(table_ref, heads, count, cap)
    closing = number == 1
    results = rest[2:]
    if closing:
        *results, dk_out, dv_out = results
    copies = []
    for part in range(len(results) // 2):
        for head in range(heads):
            source, result = results[part], results[part + len(results) // 2]
            copies.append(
                pltpu.make_async_copy(source.at[head], result.at[head], sems.at[part, head])
            )
    for copy in copies:
        copy.start()
    for slot in range(cap):
        _, head, dk_term, dv_term = owner_terms(
            table, number, scale, k_ref, v_ref, arrived, stats, slot
        )
        dk_sum[head] += dk_term
        dv_sum[head] += dv_term
    complete = []
    if closing:
        awaited = [table_ref[table.owner_at(0, slot)] for slot in range(cap)]
        for head in range(heads):
            wanted = functools.reduce(jnp.logical_and, [owner != head for owner in awaited])
            for part, (total, result) in enumerate(((dk_sum, dk_out), (dv_sum, dv_out))):
                rounded[part, head] = total[head].astype(jnp.bfloat16)
                copy = pltpu.make_async_copy(
                    rounded.at[part, head], result.at[head], rounded_sems.at[part, head]
                )
                complete.append((wanted, copy))
    for wanted, copy in complete:
        pl.when(wanted)(copy.start)
    for copy in copies:
        copy.wait()
    for wanted, copy in complete:
        pl.when(wanted)(copy.wait)


def first_owner_kernel(count, cap, scale, table_ref, k_ref, v_ref, arrived, stats, *rest):
    _, _, dk_sum, dv_sum = rest
    table = Table(table_ref, k_ref.shape[0], count, cap)
    for slot in range(arrived.shape[1]):
        _, head, dk_term, dv_term = owner_terms(
            table, 0, scale, k_ref, v_ref, arrived, stats, slot
        )
        dk_sum[head] += dk_term
        dv_sum[head] += dv_term


def closing_kernel(count, cap, table_ref, terms, dk_in, dv_in, *rest):
    _, _, dk_out, dv_out, staged, sems = rest
    table = Table(table_ref, dk_in.shape[0], count, cap)
    early = cap - terms.shape[1]
    copies = []
    for slot in range(cap):
        found = table_ref[table.owner_at(0, slot)]
        head = jnp.maximum(found, 0)
        for part, (total, result) in enumerate(((dk_in, dk_out), (dv_in, dv_out))):
            value = total[head]
            if slot >= early:
                value = value + terms[part, slot - early].astype(jnp.float32)
            staged[part, slot] = value.astype(jnp.bfloat16)
            copy = pltpu.make_async_copy(
                staged.at[part, slot], result.at[head], sems.at[part, slot]
            )
            copies.append((found >= 0, copy))
    for wanted, copy in copies:
        pl.when(wanted)(copy.start)
    for wanted, copy in copies:
        pl.when(wanted)(copy.wait)


def per_device(queries, keys, values, out_grad, tile_lists):
    heads, tokens, width = queries.shape
    channels = channel_list(lax.axis_size("seq"))
    count = len(channels)
    cap = heads // 2
    early = cap - 1
    scale = width ** (-0.5)
    table_size = Table(None, heads, count, cap).size()
    smem = pl.BlockSpec(memory_space=pltpu.SMEM)
    anywhere = pl.BlockSpec(memory_space=pl.ANY)
    vmem = pl.BlockSpec(memory_space=pltpu.VMEM)
    params = pltpu.CompilerParams(vmem_limit_bytes=VMEM_LIMIT)
    brief = pl.CostEstimate(flops=1, bytes_accessed=1, transcendentals=0)
    lengthy = pl.CostEstimate(flops=10**11, bytes_accessed=1, transcendentals=0)
    packed = pltpu.VMEM((2, cap, tokens, width), jnp.bfloat16)
    whole = jax.ShapeDtypeStruct((heads, tokens, width), jnp.bfloat16)
    whole_near = pltpu.VMEM((heads, tokens, width), jnp.bfloat16)
    whole_pair = pltpu.VMEM((2, heads, tokens, width), jnp.bfloat16)
    copies_whole = pltpu.SemaphoreType.DMA((2, heads))
    whole_sum = pltpu.VMEM((heads, tokens, width), jnp.float32)
    squares = pltpu.VMEM((heads, tokens, tokens), jnp.float32)
    far_squares = pltpu.VMEM((count * cap, tokens, tokens), jnp.float32)
    row_stats = pltpu.VMEM((cap, 2, tokens), jnp.float32)
    copies = pltpu.SemaphoreType.DMA((count, 2, cap))
    lists, q_far, k_far, v_far, g_far = (
        pltpu.with_memory_space_constraint(array, pltpu.HBM)
        for array in (jnp.swapaxes(tile_lists, 1, 2), queries, keys, values, out_grad)
    )
    key_value, lists, keys, values = pl.pallas_call(
        functools.partial(pack_keys_kernel, cap, channels[0]),
        out_shape=[packed, pltpu.SMEM(lists.shape, jnp.int32)] + [whole_near] * 2,
        in_specs=[anywhere] * 3,
        out_specs=[vmem, smem, vmem, vmem],
        scratch_shapes=[pltpu.SemaphoreType.DMA((3, heads))],
        compiler_params=params,
        cost_estimate=brief,
        name="pack_keys",
    )(lists, k_far, v_far)
    fetched = [swapped(key_value, channels[0])]
    table = pl.pallas_call(
        functools.partial(table_kernel, channels, cap),
        out_shape=pltpu.SMEM((table_size,), jnp.int32),
        in_specs=[smem],
        out_specs=smem,
        compiler_params=params,
        cost_estimate=brief,
        name="table",
    )(lists)
    for number in range(1, count):
        key_value = pl.pallas_call(
            functools.partial(pack_more_keys_kernel, count, cap, number),
            out_shape=packed,
            in_specs=[smem, vmem, vmem],
            out_specs=vmem,
            scratch_shapes=[pltpu.SemaphoreType.DMA((2, cap))],
            compiler_params=params,
            cost_estimate=brief,
            name="pack_more_keys",
        )(table, keys, values)
        fetched.append(swapped(key_value, channels[number]))
    one_head = pl.BlockSpec((1, tokens, width), lambda head: (head, 0, 0))
    one_square = pl.BlockSpec((1, tokens, tokens), lambda head: (head, 0, 0))
    sent = [pltpu.VMEM((2, early, tokens, width), jnp.bfloat16)] + [packed] * (count - 1)
    own_weight, own_prob_grad, own_rows, *query_grads = pl.pallas_call(
        functools.partial(own_kernel, count, cap, scale),
        grid=(heads,),
        out_shape=[squares] * 2 + [pltpu.VMEM((heads, 3, tokens), jnp.float32)] + sent,
        in_specs=[smem] + [one_head] * 4 + [anywhere] * 2,
        out_specs=[one_square] * 2
        + [pl.BlockSpec((1, 3, tokens), lambda head: (head, 0, 0))]
        + [pl.BlockSpec(memory_space=pltpu.VMEM)] * count,
        scratch_shapes=[copies],
        compiler_params=params,
        cost_estimate=brief,
        name="own_scores",
    )(table, q_far, keys, values, g_far, q_far, g_far)
    query_grads[1:], fetched[0] = lax.optimization_barrier((query_grads[1:], fetched[0]))
    arrived = [swapped(block, channel) for block, channel in zip(query_grads, channels)]
    far_weight, far_prob_grad, own_factors, far_factors, *stats = pl.pallas_call(
        functools.partial(statistics_kernel, count, cap, scale),
        out_shape=[far_squares] * 2
        + [pltpu.VMEM((heads, 2, tokens), jnp.float32)]
        + [pltpu.VMEM((count * cap, 2, tokens), jnp.float32)]
        + [row_stats] * count,
        in_specs=[smem] + [vmem] * (3 + count),
        out_specs=[vmem] * (4 + count),
        scratch_shapes=[pltpu.VMEM((count * cap, 3, tokens), jnp.float32)],
        compiler_params=params,
        cost_estimate=brief,
        name="statistics",
    )(table, queries, out_grad, own_rows, *fetched)
    stats = [swapped(block, channel) for block, channel in zip(stats, channels)]
    terms = pl.pallas_call(
        functools.partial(returned_kernel, count, cap, scale),
        out_shape=pltpu.VMEM((2, cap - early, tokens, width), jnp.bfloat16),
        in_specs=[smem] + [vmem] * 5,
        out_specs=vmem,
        compiler_params=params,
        cost_estimate=brief,
        name="returned",
    )(table, queries, out_grad, far_weight, far_prob_grad, far_factors)
    terms = swapped(terms, channels[0])
    transposed_sums = pltpu.VMEM((heads, width, tokens), jnp.float32)
    *finished, key_sum, value_sum = pl.pallas_call(
        functools.partial(reader_kernel, count, cap, scale),
        out_shape=[whole_near] * 2 + [whole_sum] * 2,
        in_specs=[smem] + [vmem] * (10 + count),
        out_specs=[vmem] * 4,
        scratch_shapes=[transposed_sums] * 2,
        compiler_params=params,
        cost_estimate=lengthy,
        name="reader",
    )(
        table,
        queries,
        keys,
        values,
        out_grad,
        own_weight,
        own_prob_grad,
        own_factors,
        far_weight,
        far_prob_grad,
        far_factors,
        *fetched,
    )
    results = []
    for number in range(count - 1, 0, -1):
        stored = 2 if number == count - 1 else 0
        outputs = stored + (2 if number == 1 else 0)
        *stored_now, key_sum, value_sum = pl.pallas_call(
            functools.partial(owner_kernel, count, cap, scale, number),
            out_shape=[whole] * outputs + [whole_sum] * 2,
            in_specs=[smem] + [vmem] * (6 + stored),
            out_specs=[anywhere] * outputs + [vmem] * 2,
            scratch_shapes=[whole_pair, copies_whole, copies_whole],
            input_output_aliases={5: outputs, 6: outputs + 1},
            compiler_params=params,
            cost_estimate=brief,
            name="owner",
        )(
            table,
            keys,
            values,
            arrived[number],
            stats[number],
            key_sum,
            value_sum,
            *(finished if stored else []),
        )
        results += stored_now
    *results, key_grad, value_grad = results
    first, key_sum = lax.optimization_barrier((arrived[0], key_sum))
    key_sum, value_sum = pl.pallas_call(
        functools.partial(first_owner_kernel, count, cap, scale),
        out_shape=[whole_sum] * 2,
        in_specs=[smem] + [vmem] * 6,
        out_specs=[vmem] * 2,
        input_output_aliases={5: 0, 6: 1},
        compiler_params=params,
        cost_estimate=brief,
        name="first_owner",
    )(table, keys, values, first, stats[0], key_sum, value_sum)
    terms, key_sum = lax.optimization_barrier((terms, key_sum))
    key_grad, value_grad = pl.pallas_call(
        functools.partial(closing_kernel, count, cap),
        out_shape=[whole] * 2,
        in_specs=[smem] + [vmem] * 3 + [anywhere] * 2,
        out_specs=[anywhere] * 2,
        scratch_shapes=[
            pltpu.VMEM((2, cap, tokens, width), jnp.bfloat16),
            pltpu.SemaphoreType.DMA((2, cap)),
        ],
        input_output_aliases={4: 0, 5: 1},
        compiler_params=params,
        cost_estimate=brief,
        name="closing",
    )(table, terms, key_sum, value_sum, key_grad, value_grad)
    return *results, key_grad, value_grad


def solution(mesh):
    tokens_placed = P("mp", ("clips", "seq"), None)
    return jax.shard_map(
        per_device,
        mesh=mesh,
        in_specs=(tokens_placed,) * 4 + (P("mp", None, None),),
        out_specs=(tokens_placed,) * 4,
        check_vma=False,
    )
```

```python
import functools

import jax
import jax.numpy as jnp
from jax import lax
from jax.experimental import pallas as pl
from jax.experimental.pallas import tpu as pltpu
from jax.sharding import PartitionSpec as P

GX = 8
LOG2E = 1.4426950408889634
LOWEST = -3.0e38
VMEM_LIMIT = 24 * 1024 * 1024


def channel_list(tile_count):
    row_tiles = min(4, tile_count // GX)
    layer_size = GX * row_tiles
    distances = [1]
    if row_tiles > 1:
        distances.append(GX)
    if tile_count // layer_size > 1:
        distances.append(layer_size)
    return [(distance, colour) for distance in distances for colour in (0, 1)]


def swap_route(channel, tile_count):
    distance, colour = channel
    route = []
    for low in range(tile_count - distance):
        if (low // distance) % 2 == colour:
            route += [(low, low + distance), (low + distance, low)]
    return route


def swapped(block, channel):
    return lax.ppermute(block, "seq", swap_route(channel, lax.axis_size("seq")))


def partner_of(own_tile, channel):
    distance, colour = channel
    is_low = lax.rem(lax.div(own_tile, distance), 2) == colour
    return jnp.where(is_low, own_tile + distance, own_tile - distance)


def dot_nt(a, b):
    return lax.dot_general(a, b, (((1,), (1,)), ((), ())), preferred_element_type=jnp.float32)


def dot_tn(a, b):
    return lax.dot_general(a, b, (((0,), (0,)), ((), ())), preferred_element_type=jnp.float32)


def dot_nn(a, b):
    return lax.dot_general(a, b, (((1,), (0,)), ((), ())), preferred_element_type=jnp.float32)


class Table:
    def __init__(self, ref, heads, count, cap):
        self.ref, self.heads, self.count, self.cap = ref, heads, count, cap

    def slot_at(self, head, number):
        return head * self.count + number

    def reader_at(self, number, slot):
        return self.heads * self.count + number * self.cap + slot

    def owner_at(self, number, slot):
        return self.reader_at(self.count + number, slot)

    def size(self):
        return self.owner_at(self.count - 1, self.cap - 1) + 1


def names(lists, head, reader, tile):
    entries = range(1, lists.shape[1])
    return functools.reduce(jnp.logical_or, [lists[head, entry, reader] == tile for entry in entries])


def pack_keys_kernel(cap, channel, lists_hbm, keys, values, target, lists, *rest):
    *held, sems = rest
    heads, _, tile_count = lists.shape
    loads = [pltpu.make_async_copy(lists_hbm, lists, sems.at[2, 0])]
    for part, source in enumerate((keys, values)):
        for head in range(heads):
            loads.append(
                pltpu.make_async_copy(source.at[head], held[part].at[head], sems.at[part, head])
            )
    for load in loads:
        load.start()
    loads[0].wait()
    own_tile = lax.axis_index("seq")
    partner = partner_of(own_tile, channel)
    inside = (partner >= 0) & (partner < tile_count)
    reader = jnp.clip(partner, 0, tile_count - 1)
    filled = jnp.int32(0)
    chosen = [jnp.int32(0)] * cap
    for head in range(heads):
        wanted = names(lists, head, reader, own_tile) & inside
        for slot in range(cap):
            chosen[slot] = jnp.where(wanted & (filled == slot), head, chosen[slot])
        filled = filled + wanted.astype(jnp.int32)
    for load in loads[1:]:
        load.wait()
    for slot in range(cap):
        for part in range(2):
            target[part, slot] = held[part][chosen[slot]]


def pack_more_keys_kernel(count, cap, number, table_ref, keys, values, target, sems):
    table = Table(table_ref, keys.shape[0], count, cap)
    for stage in ("start", "wait"):
        for slot in range(cap):
            head = table_ref[table.owner_at(number, slot)]

            @pl.when(head >= 0)
            def _():
                for part, source in enumerate((keys, values)):
                    copy = pltpu.make_async_copy(
                        source.at[head], target.at[part, slot], sems.at[part, slot]
                    )
                    if stage == "start":
                        copy.start()
                    else:
                        copy.wait()


def table_kernel(channels, cap, lists, table_ref):
    heads, _, tile_count = lists.shape
    table = Table(table_ref, heads, len(channels), cap)
    own_tile = lax.axis_index("seq")
    for number, channel in enumerate(channels):
        partner = partner_of(own_tile, channel)
        inside = (partner >= 0) & (partner < tile_count)
        reader = jnp.clip(partner, 0, tile_count - 1)
        for slot in range(cap):
            table_ref[table.owner_at(number, slot)] = -1
            table_ref[table.reader_at(number, slot)] = -1
        filled = [jnp.int32(0), jnp.int32(0)]
        for head in range(heads):
            given = names(lists, head, reader, own_tile) & inside & (filled[0] < cap)
            named = names(lists, head, own_tile, partner) & inside & (filled[1] < cap)
            table_ref[table.slot_at(head, number)] = jnp.where(named, filled[1], -1)

            @pl.when(given)
            def _():
                table_ref[table.owner_at(number, filled[0])] = head

            @pl.when(named)
            def _():
                table_ref[table.reader_at(number, filled[1])] = head

            filled = [filled[0] + given.astype(jnp.int32), filled[1] + named.astype(jnp.int32)]


def own_kernel(count, cap, scale, table_ref, q_ref, k_ref, v_ref, g_ref, queries, grads, *rest):
    weight_ref, prob_grad_ref, rows_ref, *targets, sems = rest
    heads = queries.shape[0]
    table = Table(table_ref, heads, count, cap)

    def copies(stage):
        for number in range(count):
            for slot in range(targets[number].shape[1]):
                head = table_ref[table.reader_at(number, slot)]

                @pl.when(head >= 0)
                def _():
                    for part, source in enumerate((queries, grads)):
                        copy = pltpu.make_async_copy(
                            source.at[head],
                            targets[number].at[part, slot],
                            sems.at[number, part, slot],
                        )
                        if stage == "start":
                            copy.start()
                        else:
                            copy.wait()

    pl.when(pl.program_id(0) == 0)(lambda: copies("start"))
    score = dot_nt(k_ref[0], q_ref[0]) * (scale * LOG2E)
    top = jnp.max(score, axis=0, keepdims=True)
    weight = jnp.exp2(score - top)
    prob_grad = dot_nt(v_ref[0], g_ref[0])
    weight_ref[0] = weight
    prob_grad_ref[0] = prob_grad
    rows_ref[0, 0:1] = top
    rows_ref[0, 1:2] = jnp.sum(weight, axis=0, keepdims=True)
    rows_ref[0, 2:3] = jnp.sum(weight * prob_grad, axis=0, keepdims=True)
    pl.when(pl.program_id(0) == heads - 1)(lambda: copies("wait"))


def statistics_kernel(count, cap, scale, table_ref, q_ref, g_ref, own_rows, *rest):
    fetched, rest = rest[:count], rest[count:]
    weight_ref, prob_grad_ref, own_factors, far_factors = rest[:4]
    stats, far_rows = rest[4 : 4 + count], rest[4 + count]
    heads = q_ref.shape[0]
    table = Table(table_ref, heads, count, cap)
    for number in range(count):
        for slot in range(cap):
            head = jnp.maximum(table_ref[table.reader_at(number, slot)], 0)
            place = number * cap + slot
            score = dot_nt(fetched[number][0, slot], q_ref[head]) * (scale * LOG2E)
            top = jnp.max(score, axis=0, keepdims=True)
            weight = jnp.exp2(score - top)
            prob_grad = dot_nt(fetched[number][1, slot], g_ref[head])
            weight_ref[place] = weight
            prob_grad_ref[place] = prob_grad
            far_rows[place, 0:1] = top
            far_rows[place, 1:2] = jnp.sum(weight, axis=0, keepdims=True)
            far_rows[place, 2:3] = jnp.sum(weight * prob_grad, axis=0, keepdims=True)
    for head in range(heads):
        rows = [own_rows[head]]
        slots = [table_ref[table.slot_at(head, number)] for number in range(count)]
        for number in range(count):
            found = far_rows[number * cap + jnp.maximum(slots[number], 0)]
            missing = jnp.where(
                lax.broadcasted_iota(jnp.int32, found.shape, 0) == 0, LOWEST, 0.0
            )
            rows.append(jnp.where(slots[number] >= 0, found, missing))
        top = functools.reduce(jnp.maximum, [row[0:1] for row in rows])
        factors = [jnp.exp2(row[0:1] - top) for row in rows]
        total = sum(factor * row[1:2] for factor, row in zip(factors, rows))
        inverse = 1.0 / total
        delta = sum(factor * row[2:3] for factor, row in zip(factors, rows)) * inverse
        level = top + jnp.log2(total)
        own_factors[head, 0:1] = factors[0] * inverse
        own_factors[head, 1:2] = delta
        for number in range(count):

            @pl.when(slots[number] >= 0)
            def _():
                place = number * cap + slots[number]
                far_factors[place, 0:1] = factors[1 + number] * inverse
                far_factors[place, 1:2] = delta
                stats[number][slots[number], 0:1] = level
                stats[number][slots[number], 1:2] = delta


def softmax_grad(weight, prob_grad, factors):
    prob = weight * factors[0:1]
    score_grad = prob * (prob_grad - factors[1:2])
    return prob.astype(jnp.bfloat16), score_grad.astype(jnp.bfloat16)


def returned_kernel(count, cap, scale, table_ref, q_ref, g_ref, *rest):
    far_weight, far_prob_grad, far_factors, terms = rest
    table = Table(table_ref, q_ref.shape[0], count, cap)
    returned = terms.shape[1]
    for number in range(returned):
        place = cap - returned + number
        head = jnp.maximum(table_ref[table.reader_at(0, place)], 0)
        prob, score_grad = softmax_grad(
            far_weight[place], far_prob_grad[place], far_factors[place]
        )
        terms[0, number] = (dot_nn(score_grad, q_ref[head]) * scale).astype(jnp.bfloat16)
        terms[1, number] = dot_nn(prob, g_ref[head]).astype(jnp.bfloat16)


def reader_kernel(count, cap, scale, table_ref, q_ref, k_ref, v_ref, g_ref, *rest):
    own_weight, own_prob_grad, own_factors, far_weight, far_prob_grad, far_factors = rest[:6]
    fetched, rest = rest[6 : 6 + count], rest[6 + count :]
    o_ref, dq_ref, dk_ref, dv_ref, o_sum, dq_sum = rest
    heads = q_ref.shape[0]
    table = Table(table_ref, heads, count, cap)
    for head in range(heads):
        prob, score_grad = softmax_grad(own_weight[head], own_prob_grad[head], own_factors[head])
        o_sum[head] = dot_tn(v_ref[head], prob)
        dq_sum[head] = dot_tn(k_ref[head], score_grad)
        dk_ref[head] = dot_nn(score_grad, q_ref[head]) * scale
        dv_ref[head] = dot_nn(prob, g_ref[head])
    for number in range(count):
        for slot in range(cap):
            found = table_ref[table.reader_at(number, slot)]
            head = jnp.maximum(found, 0)
            place = number * cap + slot
            prob, score_grad = softmax_grad(
                far_weight[place], far_prob_grad[place], far_factors[place]
            )
            o_term = dot_tn(fetched[number][1, slot], prob)
            dq_term = dot_tn(fetched[number][0, slot], score_grad)
            o_sum[head] += jnp.where(found >= 0, o_term, 0.0)
            dq_sum[head] += jnp.where(found >= 0, dq_term, 0.0)
    for head in range(heads):
        o_ref[head] = o_sum[head].T.astype(jnp.bfloat16)
        dq_ref[head] = (dq_sum[head] * scale).T.astype(jnp.bfloat16)


def owner_terms(table, number, scale, k_ref, v_ref, arrived, stats, slot):
    found = table.ref[table.owner_at(number, slot)]
    head = jnp.maximum(found, 0)
    query, grad = arrived[0, slot], arrived[1, slot]
    score = dot_nt(k_ref[head], query) * (scale * LOG2E)
    prob = jnp.exp2(score - stats[slot, 0:1])
    prob_grad = dot_nt(v_ref[head], grad)
    score_grad = (prob * (prob_grad - stats[slot, 1:2])).astype(jnp.bfloat16)
    dk_term = dot_nn(score_grad, query) * scale
    dv_term = dot_nn(prob.astype(jnp.bfloat16), grad)
    return found, head, jnp.where(found >= 0, dk_term, 0.0), jnp.where(found >= 0, dv_term, 0.0)


def owner_kernel(count, cap, scale, number, table_ref, k_ref, v_ref, arrived, stats, *rest):
    *rest, dk_sum, dv_sum, rounded, sems, rounded_sems = rest
    heads = k_ref.shape[0]
    table = Table(table_ref, heads, count, cap)
    closing = number == 1
    results = rest[2:]
    if closing:
        *results, dk_out, dv_out = results
    copies = []
    for part in range(len(results) // 2):
        for head in range(heads):
            source, result = results[part], results[part + len(results) // 2]
            copies.append(
                pltpu.make_async_copy(source.at[head], result.at[head], sems.at[part, head])
            )
    for copy in copies:
        copy.start()
    for slot in range(cap):
        _, head, dk_term, dv_term = owner_terms(
            table, number, scale, k_ref, v_ref, arrived, stats, slot
        )
        dk_sum[head] += dk_term
        dv_sum[head] += dv_term
    complete = []
    if closing:
        awaited = [table_ref[table.owner_at(0, slot)] for slot in range(cap)]
        for head in range(heads):
            wanted = functools.reduce(jnp.logical_and, [owner != head for owner in awaited])
            for part, (total, result) in enumerate(((dk_sum, dk_out), (dv_sum, dv_out))):
                rounded[part, head] = total[head].astype(jnp.bfloat16)
                copy = pltpu.make_async_copy(
                    rounded.at[part, head], result.at[head], rounded_sems.at[part, head]
                )
                complete.append((wanted, copy))
    for wanted, copy in complete:
        pl.when(wanted)(copy.start)
    for copy in copies:
        copy.wait()
    for wanted, copy in complete:
        pl.when(wanted)(copy.wait)


def first_owner_kernel(count, cap, scale, table_ref, k_ref, v_ref, arrived, stats, *rest):
    dk_in, dv_in, _, _, dk_out, dv_out, staged, sems = rest
    table = Table(table_ref, k_ref.shape[0], count, cap)
    stores = []
    for slot in range(arrived.shape[1]):
        found, head, *terms = owner_terms(
            table, 0, scale, k_ref, v_ref, arrived, stats, slot
        )
        for part, (total, result) in enumerate(((dk_in, dk_out), (dv_in, dv_out))):
            staged[part, slot] = (total[head] + terms[part]).astype(jnp.bfloat16)
            store = pltpu.make_async_copy(
                staged.at[part, slot], result.at[head], sems.at[part, slot]
            )
            stores.append((found >= 0, store))
    for wanted, store in stores:
        pl.when(wanted)(store.start)
    for wanted, store in stores:
        pl.when(wanted)(store.wait)


def closing_kernel(count, cap, table_ref, terms, dk_in, dv_in, *rest):
    _, _, dk_out, dv_out, staged, sems = rest
    table = Table(table_ref, dk_in.shape[0], count, cap)
    returned = terms.shape[1]
    stores = []
    for number in range(returned):
        found = table_ref[table.owner_at(0, cap - returned + number)]
        head = jnp.maximum(found, 0)
        for part, (total, result) in enumerate(((dk_in, dk_out), (dv_in, dv_out))):
            term = terms[part, number].astype(jnp.float32)
            staged[part, number] = (total[head] + term).astype(jnp.bfloat16)
            store = pltpu.make_async_copy(
                staged.at[part, number], result.at[head], sems.at[part, number]
            )
            stores.append((found >= 0, store))
    for wanted, store in stores:
        pl.when(wanted)(store.start)
    for wanted, store in stores:
        pl.when(wanted)(store.wait)


def per_device(queries, keys, values, out_grad, tile_lists):
    heads, tokens, width = queries.shape
    channels = channel_list(lax.axis_size("seq"))
    count = len(channels)
    cap = heads // 2
    early = cap - 1
    scale = width ** (-0.5)
    table_size = Table(None, heads, count, cap).size()
    smem = pl.BlockSpec(memory_space=pltpu.SMEM)
    anywhere = pl.BlockSpec(memory_space=pl.ANY)
    vmem = pl.BlockSpec(memory_space=pltpu.VMEM)
    params = pltpu.CompilerParams(vmem_limit_bytes=VMEM_LIMIT)
    brief = pl.CostEstimate(flops=1, bytes_accessed=1, transcendentals=0)
    lengthy = pl.CostEstimate(flops=10**11, bytes_accessed=1, transcendentals=0)
    packed = pltpu.VMEM((2, cap, tokens, width), jnp.bfloat16)
    whole = jax.ShapeDtypeStruct((heads, tokens, width), jnp.bfloat16)
    whole_near = pltpu.VMEM((heads, tokens, width), jnp.bfloat16)
    whole_pair = pltpu.VMEM((2, heads, tokens, width), jnp.bfloat16)
    copies_whole = pltpu.SemaphoreType.DMA((2, heads))
    whole_sum = pltpu.VMEM((heads, tokens, width), jnp.float32)
    squares = pltpu.VMEM((heads, tokens, tokens), jnp.float32)
    far_squares = pltpu.VMEM((count * cap, tokens, tokens), jnp.float32)
    row_stats = pltpu.VMEM((cap, 2, tokens), jnp.float32)
    copies = pltpu.SemaphoreType.DMA((count, 2, cap))
    lists, q_far, k_far, v_far, g_far = (
        pltpu.with_memory_space_constraint(array, pltpu.HBM)
        for array in (jnp.swapaxes(tile_lists, 1, 2), queries, keys, values, out_grad)
    )
    key_value, lists, keys, values = pl.pallas_call(
        functools.partial(pack_keys_kernel, cap, channels[0]),
        out_shape=[packed, pltpu.SMEM(lists.shape, jnp.int32)] + [whole_near] * 2,
        in_specs=[anywhere] * 3,
        out_specs=[vmem, smem, vmem, vmem],
        scratch_shapes=[pltpu.SemaphoreType.DMA((3, heads))],
        compiler_params=params,
        cost_estimate=brief,
        name="pack_keys",
    )(lists, k_far, v_far)
    fetched = [swapped(key_value, channels[0])]
    table = pl.pallas_call(
        functools.partial(table_kernel, channels, cap),
        out_shape=pltpu.SMEM((table_size,), jnp.int32),
        in_specs=[smem],
        out_specs=smem,
        compiler_params=params,
        cost_estimate=brief,
        name="table",
    )(lists)
    for number in range(1, count):
        key_value = pl.pallas_call(
            functools.partial(pack_more_keys_kernel, count, cap, number),
            out_shape=packed,
            in_specs=[smem, vmem, vmem],
            out_specs=vmem,
            scratch_shapes=[pltpu.SemaphoreType.DMA((2, cap))],
            compiler_params=params,
            cost_estimate=brief,
            name="pack_more_keys",
        )(table, keys, values)
        fetched.append(swapped(key_value, channels[number]))
    one_head = pl.BlockSpec((1, tokens, width), lambda head: (head, 0, 0))
    one_square = pl.BlockSpec((1, tokens, tokens), lambda head: (head, 0, 0))
    sent = [pltpu.VMEM((2, early, tokens, width), jnp.bfloat16)] + [packed] * (count - 1)
    own_weight, own_prob_grad, own_rows, *query_grads = pl.pallas_call(
        functools.partial(own_kernel, count, cap, scale),
        grid=(heads,),
        out_shape=[squares] * 2 + [pltpu.VMEM((heads, 3, tokens), jnp.float32)] + sent,
        in_specs=[smem] + [one_head] * 4 + [anywhere] * 2,
        out_specs=[one_square] * 2
        + [pl.BlockSpec((1, 3, tokens), lambda head: (head, 0, 0))]
        + [pl.BlockSpec(memory_space=pltpu.VMEM)] * count,
        scratch_shapes=[copies],
        compiler_params=params,
        cost_estimate=brief,
        name="own_scores",
    )(table, q_far, keys, values, g_far, q_far, g_far)
    query_grads[1:], fetched[0] = lax.optimization_barrier((query_grads[1:], fetched[0]))
    arrived = [swapped(block, channel) for block, channel in zip(query_grads, channels)]
    far_weight, far_prob_grad, own_factors, far_factors, *stats = pl.pallas_call(
        functools.partial(statistics_kernel, count, cap, scale),
        out_shape=[far_squares] * 2
        + [pltpu.VMEM((heads, 2, tokens), jnp.float32)]
        + [pltpu.VMEM((count * cap, 2, tokens), jnp.float32)]
        + [row_stats] * count,
        in_specs=[smem] + [vmem] * (3 + count),
        out_specs=[vmem] * (4 + count),
        scratch_shapes=[pltpu.VMEM((count * cap, 3, tokens), jnp.float32)],
        compiler_params=params,
        cost_estimate=brief,
        name="statistics",
    )(table, queries, out_grad, own_rows, *fetched)
    stats = [swapped(block, channel) for block, channel in zip(stats, channels)]
    terms = pl.pallas_call(
        functools.partial(returned_kernel, count, cap, scale),
        out_shape=pltpu.VMEM((2, cap - early, tokens, width), jnp.bfloat16),
        in_specs=[smem] + [vmem] * 5,
        out_specs=vmem,
        compiler_params=params,
        cost_estimate=brief,
        name="returned",
    )(table, queries, out_grad, far_weight, far_prob_grad, far_factors)
    terms = swapped(terms, channels[0])
    transposed_sums = pltpu.VMEM((heads, width, tokens), jnp.float32)
    *finished, key_sum, value_sum = pl.pallas_call(
        functools.partial(reader_kernel, count, cap, scale),
        out_shape=[whole_near] * 2 + [whole_sum] * 2,
        in_specs=[smem] + [vmem] * (10 + count),
        out_specs=[vmem] * 4,
        scratch_shapes=[transposed_sums] * 2,
        compiler_params=params,
        cost_estimate=lengthy,
        name="reader",
    )(
        table,
        queries,
        keys,
        values,
        out_grad,
        own_weight,
        own_prob_grad,
        own_factors,
        far_weight,
        far_prob_grad,
        far_factors,
        *fetched,
    )
    results = []
    for number in range(count - 1, 0, -1):
        stored = 2 if number == count - 1 else 0
        outputs = stored + (2 if number == 1 else 0)
        *stored_now, key_sum, value_sum = pl.pallas_call(
            functools.partial(owner_kernel, count, cap, scale, number),
            out_shape=[whole] * outputs + [whole_sum] * 2,
            in_specs=[smem] + [vmem] * (6 + stored),
            out_specs=[anywhere] * outputs + [vmem] * 2,
            scratch_shapes=[whole_pair, copies_whole, copies_whole],
            input_output_aliases={5: outputs, 6: outputs + 1},
            compiler_params=params,
            cost_estimate=brief,
            name="owner",
        )(
            table,
            keys,
            values,
            arrived[number],
            stats[number],
            key_sum,
            value_sum,
            *(finished if stored else []),
        )
        results += stored_now
    *results, key_grad, value_grad = results
    first, key_sum = lax.optimization_barrier((arrived[0], key_sum))
    key_grad, value_grad = pl.pallas_call(
        functools.partial(first_owner_kernel, count, cap, scale),
        out_shape=[whole] * 2,
        in_specs=[smem] + [vmem] * 6 + [anywhere] * 2,
        out_specs=[anywhere] * 2,
        scratch_shapes=[packed, pltpu.SemaphoreType.DMA((2, cap))],
        input_output_aliases={7: 0, 8: 1},
        compiler_params=params,
        cost_estimate=brief,
        name="first_owner",
    )(table, keys, values, first, stats[0], key_sum, value_sum, key_grad, value_grad)
    terms, key_grad = lax.optimization_barrier((terms, key_grad))
    key_grad, value_grad = pl.pallas_call(
        functools.partial(closing_kernel, count, cap),
        out_shape=[whole] * 2,
        in_specs=[smem] + [vmem] * 3 + [anywhere] * 2,
        out_specs=[anywhere] * 2,
        scratch_shapes=[packed, pltpu.SemaphoreType.DMA((2, cap))],
        input_output_aliases={4: 0, 5: 1},
        compiler_params=params,
        cost_estimate=brief,
        name="closing",
    )(table, terms, key_sum, value_sum, key_grad, value_grad)
    return *results, key_grad, value_grad


def solution(mesh):
    tokens_placed = P("mp", ("clips", "seq"), None)
    return jax.shard_map(
        per_device,
        mesh=mesh,
        in_specs=(tokens_placed,) * 4 + (P("mp", None, None),),
        out_specs=(tokens_placed,) * 4,
        check_vma=False,
    )
```

```python
import functools

import jax
import jax.numpy as jnp
from jax import lax
from jax.experimental import pallas as pl
from jax.experimental.pallas import tpu as pltpu
from jax.sharding import PartitionSpec as P

GX = 8
LOG2E = 1.4426950408889634
LOWEST = -3.0e38
VMEM_LIMIT = 24 * 1024 * 1024


def channel_list(tile_count):
    row_tiles = min(4, tile_count // GX)
    layer_size = GX * row_tiles
    distances = [1]
    if row_tiles > 1:
        distances.append(GX)
    if tile_count // layer_size > 1:
        distances.append(layer_size)
    return [(distance, colour) for distance in distances for colour in (0, 1)]


def swap_route(channel, tile_count):
    distance, colour = channel
    route = []
    for low in range(tile_count - distance):
        if (low // distance) % 2 == colour:
            route += [(low, low + distance), (low + distance, low)]
    return route


def swapped(block, channel):
    return lax.ppermute(block, "seq", swap_route(channel, lax.axis_size("seq")))


def partner_of(own_tile, channel):
    distance, colour = channel
    is_low = lax.rem(lax.div(own_tile, distance), 2) == colour
    return jnp.where(is_low, own_tile + distance, own_tile - distance)


def dot_nt(a, b):
    return lax.dot_general(a, b, (((1,), (1,)), ((), ())), preferred_element_type=jnp.float32)


def dot_tn(a, b):
    return lax.dot_general(a, b, (((0,), (0,)), ((), ())), preferred_element_type=jnp.float32)


def dot_nn(a, b):
    return lax.dot_general(a, b, (((1,), (0,)), ((), ())), preferred_element_type=jnp.float32)


class Table:
    def __init__(self, ref, heads, count, cap):
        self.ref, self.heads, self.count, self.cap = ref, heads, count, cap

    def slot_at(self, head, number):
        return head * self.count + number

    def reader_at(self, number, slot):
        return self.heads * self.count + number * self.cap + slot

    def owner_at(self, number, slot):
        return self.reader_at(self.count + number, slot)

    def size(self):
        return self.owner_at(self.count - 1, self.cap - 1) + 1


def names(lists, head, reader, tile):
    entries = range(1, lists.shape[1])
    return functools.reduce(jnp.logical_or, [lists[head, entry, reader] == tile for entry in entries])


def pack_keys_kernel(cap, channel, lists_hbm, keys, values, target, lists, *rest):
    *held, sems = rest
    heads, _, tile_count = lists.shape
    loads = [pltpu.make_async_copy(lists_hbm, lists, sems.at[2, 0])]
    for part, source in enumerate((keys, values)):
        for head in range(heads):
            loads.append(
                pltpu.make_async_copy(source.at[head], held[part].at[head], sems.at[part, head])
            )
    for load in loads:
        load.start()
    loads[0].wait()
    own_tile = lax.axis_index("seq")
    partner = partner_of(own_tile, channel)
    inside = (partner >= 0) & (partner < tile_count)
    reader = jnp.clip(partner, 0, tile_count - 1)
    filled = jnp.int32(0)
    chosen = [jnp.int32(0)] * cap
    for head in range(heads):
        wanted = names(lists, head, reader, own_tile) & inside
        for slot in range(cap):
            chosen[slot] = jnp.where(wanted & (filled == slot), head, chosen[slot])
        filled = filled + wanted.astype(jnp.int32)
    for load in loads[1:]:
        load.wait()
    for slot in range(cap):
        for part in range(2):
            target[part, slot] = held[part][chosen[slot]]


def pack_more_keys_kernel(count, cap, number, table_ref, keys, values, target, sems):
    table = Table(table_ref, keys.shape[0], count, cap)
    for stage in ("start", "wait"):
        for slot in range(cap):
            head = table_ref[table.owner_at(number, slot)]

            @pl.when(head >= 0)
            def _():
                for part, source in enumerate((keys, values)):
                    copy = pltpu.make_async_copy(
                        source.at[head], target.at[part, slot], sems.at[part, slot]
                    )
                    if stage == "start":
                        copy.start()
                    else:
                        copy.wait()


def table_kernel(channels, cap, lists, table_ref):
    heads, _, tile_count = lists.shape
    table = Table(table_ref, heads, len(channels), cap)
    own_tile = lax.axis_index("seq")
    for number, channel in enumerate(channels):
        partner = partner_of(own_tile, channel)
        inside = (partner >= 0) & (partner < tile_count)
        reader = jnp.clip(partner, 0, tile_count - 1)
        for slot in range(cap):
            table_ref[table.owner_at(number, slot)] = -1
            table_ref[table.reader_at(number, slot)] = -1
        filled = [jnp.int32(0), jnp.int32(0)]
        for head in range(heads):
            given = names(lists, head, reader, own_tile) & inside & (filled[0] < cap)
            named = names(lists, head, own_tile, partner) & inside & (filled[1] < cap)
            table_ref[table.slot_at(head, number)] = jnp.where(named, filled[1], -1)

            @pl.when(given)
            def _():
                table_ref[table.owner_at(number, filled[0])] = head

            @pl.when(named)
            def _():
                table_ref[table.reader_at(number, filled[1])] = head

            filled = [filled[0] + given.astype(jnp.int32), filled[1] + named.astype(jnp.int32)]


def own_kernel(count, cap, scale, table_ref, q_ref, k_ref, v_ref, g_ref, queries, grads, *rest):
    weight_ref, prob_grad_ref, rows_ref, *targets, sems = rest
    heads = queries.shape[0]
    table = Table(table_ref, heads, count, cap)

    def copies(stage):
        for number in range(count):
            for slot in range(targets[number].shape[1]):
                head = table_ref[table.reader_at(number, slot)]

                @pl.when(head >= 0)
                def _():
                    for part, source in enumerate((queries, grads)):
                        copy = pltpu.make_async_copy(
                            source.at[head],
                            targets[number].at[part, slot],
                            sems.at[number, part, slot],
                        )
                        if stage == "start":
                            copy.start()
                        else:
                            copy.wait()

    pl.when(pl.program_id(0) == 0)(lambda: copies("start"))
    score = dot_nt(k_ref[0], q_ref[0]) * (scale * LOG2E)
    top = jnp.max(score, axis=0, keepdims=True)
    weight = jnp.exp2(score - top)
    prob_grad = dot_nt(v_ref[0], g_ref[0])
    weight_ref[0] = weight
    prob_grad_ref[0] = prob_grad
    rows_ref[0, 0:1] = top
    rows_ref[0, 1:2] = jnp.sum(weight, axis=0, keepdims=True)
    rows_ref[0, 2:3] = jnp.sum(weight * prob_grad, axis=0, keepdims=True)
    pl.when(pl.program_id(0) == heads - 1)(lambda: copies("wait"))


def statistics_kernel(count, cap, scale, table_ref, q_ref, g_ref, own_rows, *rest):
    fetched, rest = rest[:count], rest[count:]
    weight_ref, prob_grad_ref, own_factors, far_factors = rest[:4]
    stats, far_rows = rest[4 : 4 + count], rest[4 + count]
    heads = q_ref.shape[0]
    table = Table(table_ref, heads, count, cap)
    for number in range(count):
        for slot in range(cap):
            head = jnp.maximum(table_ref[table.reader_at(number, slot)], 0)
            place = number * cap + slot
            score = dot_nt(fetched[number][0, slot], q_ref[head]) * (scale * LOG2E)
            top = jnp.max(score, axis=0, keepdims=True)
            weight = jnp.exp2(score - top)
            prob_grad = dot_nt(fetched[number][1, slot], g_ref[head])
            weight_ref[place] = weight
            prob_grad_ref[place] = prob_grad
            far_rows[place, 0:1] = top
            far_rows[place, 1:2] = jnp.sum(weight, axis=0, keepdims=True)
            far_rows[place, 2:3] = jnp.sum(weight * prob_grad, axis=0, keepdims=True)
    for head in range(heads):
        rows = [own_rows[head]]
        slots = [table_ref[table.slot_at(head, number)] for number in range(count)]
        for number in range(count):
            found = far_rows[number * cap + jnp.maximum(slots[number], 0)]
            missing = jnp.where(
                lax.broadcasted_iota(jnp.int32, found.shape, 0) == 0, LOWEST, 0.0
            )
            rows.append(jnp.where(slots[number] >= 0, found, missing))
        top = functools.reduce(jnp.maximum, [row[0:1] for row in rows])
        factors = [jnp.exp2(row[0:1] - top) for row in rows]
        total = sum(factor * row[1:2] for factor, row in zip(factors, rows))
        inverse = 1.0 / total
        delta = sum(factor * row[2:3] for factor, row in zip(factors, rows)) * inverse
        level = top + jnp.log2(total)
        own_factors[head, 0:1] = factors[0] * inverse
        own_factors[head, 1:2] = delta
        for number in range(count):

            @pl.when(slots[number] >= 0)
            def _():
                place = number * cap + slots[number]
                far_factors[place, 0:1] = factors[1 + number] * inverse
                far_factors[place, 1:2] = delta
                stats[number][slots[number], 0:1] = level
                stats[number][slots[number], 1:2] = delta


def softmax_grad(weight, prob_grad, factors):
    prob = weight * factors[0:1]
    score_grad = prob * (prob_grad - factors[1:2])
    return prob.astype(jnp.bfloat16), score_grad.astype(jnp.bfloat16)


def returned_kernel(count, cap, scale, table_ref, q_ref, g_ref, *rest):
    far_weight, far_prob_grad, far_factors, terms = rest
    table = Table(table_ref, q_ref.shape[0], count, cap)
    returned = terms.shape[1]
    for number in range(returned):
        place = cap - returned + number
        head = jnp.maximum(table_ref[table.reader_at(0, place)], 0)
        prob, score_grad = softmax_grad(
            far_weight[place], far_prob_grad[place], far_factors[place]
        )
        terms[0, number] = (dot_nn(score_grad, q_ref[head]) * scale).astype(jnp.bfloat16)
        terms[1, number] = dot_nn(prob, g_ref[head]).astype(jnp.bfloat16)


def reader_kernel(count, cap, scale, table_ref, q_ref, k_ref, v_ref, g_ref, *rest):
    own_weight, own_prob_grad, own_factors, far_weight, far_prob_grad, far_factors = rest[:6]
    fetched, rest = rest[6 : 6 + count], rest[6 + count :]
    o_ref, dq_ref, dk_ref, dv_ref, o_sum, dq_sum = rest
    heads = q_ref.shape[0]
    table = Table(table_ref, heads, count, cap)
    for head in range(heads):
        prob, score_grad = softmax_grad(own_weight[head], own_prob_grad[head], own_factors[head])
        o_sum[head] = dot_tn(v_ref[head], prob)
        dq_sum[head] = dot_tn(k_ref[head], score_grad)
        dk_ref[head] = dot_nn(score_grad, q_ref[head]) * scale
        dv_ref[head] = dot_nn(prob, g_ref[head])
    for number in range(count):
        for slot in range(cap):
            found = table_ref[table.reader_at(number, slot)]
            head = jnp.maximum(found, 0)
            place = number * cap + slot
            prob, score_grad = softmax_grad(
                far_weight[place], far_prob_grad[place], far_factors[place]
            )
            o_term = dot_tn(fetched[number][1, slot], prob)
            dq_term = dot_tn(fetched[number][0, slot], score_grad)
            o_sum[head] += jnp.where(found >= 0, o_term, 0.0)
            dq_sum[head] += jnp.where(found >= 0, dq_term, 0.0)
    for head in range(heads):
        o_ref[head] = o_sum[head].T.astype(jnp.bfloat16)
        dq_ref[head] = (dq_sum[head] * scale).T.astype(jnp.bfloat16)


def owner_terms(table, number, scale, k_ref, v_ref, arrived, stats, slot):
    found = table.ref[table.owner_at(number, slot)]
    head = jnp.maximum(found, 0)
    query, grad = arrived[0, slot], arrived[1, slot]
    score = dot_nt(k_ref[head], query) * (scale * LOG2E)
    prob = jnp.exp2(score - stats[slot, 0:1])
    prob_grad = dot_nt(v_ref[head], grad)
    score_grad = (prob * (prob_grad - stats[slot, 1:2])).astype(jnp.bfloat16)
    dk_term = dot_nn(score_grad, query) * scale
    dv_term = dot_nn(prob.astype(jnp.bfloat16), grad)
    return found, head, jnp.where(found >= 0, dk_term, 0.0), jnp.where(found >= 0, dv_term, 0.0)


def owner_kernel(count, cap, scale, number, table_ref, k_ref, v_ref, arrived, stats, *rest):
    *rest, dk_sum, dv_sum, rounded, sems, rounded_sems = rest
    heads = k_ref.shape[0]
    table = Table(table_ref, heads, count, cap)
    closing = number == 1
    for total, given in zip((dk_sum, dv_sum), rest):
        for head in range(heads):
            total[head] = given[head]
    results = rest[2:]
    if closing:
        *results, dk_out, dv_out = results
    copies = []
    for part in range(len(results) // 2):
        for head in range(heads):
            source, result = results[part], results[part + len(results) // 2]
            copies.append(
                pltpu.make_async_copy(source.at[head], result.at[head], sems.at[part, head])
            )
    for copy in copies:
        copy.start()
    for slot in range(cap):
        _, head, dk_term, dv_term = owner_terms(
            table, number, scale, k_ref, v_ref, arrived, stats, slot
        )
        dk_sum[head] += dk_term
        dv_sum[head] += dv_term
    complete = []
    if closing:
        awaited = [table_ref[table.owner_at(0, slot)] for slot in range(cap)]
        for head in range(heads):
            wanted = functools.reduce(jnp.logical_and, [owner != head for owner in awaited])
            for part, (total, result) in enumerate(((dk_sum, dk_out), (dv_sum, dv_out))):
                rounded[part, head] = total[head].astype(jnp.bfloat16)
                copy = pltpu.make_async_copy(
                    rounded.at[part, head], result.at[head], rounded_sems.at[part, head]
                )
                complete.append((wanted, copy))
    for wanted, copy in complete:
        pl.when(wanted)(copy.start)
    for copy in copies:
        copy.wait()
    for wanted, copy in complete:
        pl.when(wanted)(copy.wait)


def first_owner_kernel(count, cap, scale, table_ref, k_ref, v_ref, arrived, stats, *rest):
    dk_in, dv_in, _, _, dk_out, dv_out, staged, sems = rest
    table = Table(table_ref, k_ref.shape[0], count, cap)
    stores = []
    for slot in range(arrived.shape[1]):
        found, head, *terms = owner_terms(
            table, 0, scale, k_ref, v_ref, arrived, stats, slot
        )
        for part, (total, result) in enumerate(((dk_in, dk_out), (dv_in, dv_out))):
            staged[part, slot] = (total[head] + terms[part]).astype(jnp.bfloat16)
            store = pltpu.make_async_copy(
                staged.at[part, slot], result.at[head], sems.at[part, slot]
            )
            stores.append((found >= 0, store))
    for wanted, store in stores:
        pl.when(wanted)(store.start)
    for wanted, store in stores:
        pl.when(wanted)(store.wait)


def closing_kernel(count, cap, table_ref, terms, dk_in, dv_in, *rest):
    _, _, dk_out, dv_out, staged, sems = rest
    table = Table(table_ref, dk_in.shape[0], count, cap)
    returned = terms.shape[1]
    stores = []
    for number in range(returned):
        found = table_ref[table.owner_at(0, cap - returned + number)]
        head = jnp.maximum(found, 0)
        for part, (total, result) in enumerate(((dk_in, dk_out), (dv_in, dv_out))):
            term = terms[part, number].astype(jnp.float32)
            staged[part, number] = (total[head] + term).astype(jnp.bfloat16)
            store = pltpu.make_async_copy(
                staged.at[part, number], result.at[head], sems.at[part, number]
            )
            stores.append((found >= 0, store))
    for wanted, store in stores:
        pl.when(wanted)(store.start)
    for wanted, store in stores:
        pl.when(wanted)(store.wait)


def per_device(queries, keys, values, out_grad, tile_lists):
    heads, tokens, width = queries.shape
    channels = channel_list(lax.axis_size("seq"))
    count = len(channels)
    cap = heads // 2
    early = cap - 1
    scale = width ** (-0.5)
    table_size = Table(None, heads, count, cap).size()
    smem = pl.BlockSpec(memory_space=pltpu.SMEM)
    anywhere = pl.BlockSpec(memory_space=pl.ANY)
    vmem = pl.BlockSpec(memory_space=pltpu.VMEM)
    params = pltpu.CompilerParams(vmem_limit_bytes=VMEM_LIMIT)
    brief = pl.CostEstimate(flops=1, bytes_accessed=1, transcendentals=0)
    lengthy = pl.CostEstimate(flops=10**11, bytes_accessed=1, transcendentals=0)
    packed = pltpu.VMEM((2, cap, tokens, width), jnp.bfloat16)
    whole = jax.ShapeDtypeStruct((heads, tokens, width), jnp.bfloat16)
    whole_near = pltpu.VMEM((heads, tokens, width), jnp.bfloat16)
    whole_pair = pltpu.VMEM((2, heads, tokens, width), jnp.bfloat16)
    copies_whole = pltpu.SemaphoreType.DMA((2, heads))
    whole_sum = pltpu.VMEM((heads, tokens, width), jnp.float32)
    squares = pltpu.VMEM((heads, tokens, tokens), jnp.float32)
    far_squares = pltpu.VMEM((count * cap, tokens, tokens), jnp.float32)
    row_stats = pltpu.VMEM((cap, 2, tokens), jnp.float32)
    copies = pltpu.SemaphoreType.DMA((count, 2, cap))
    lists, q_far, k_far, v_far, g_far = (
        pltpu.with_memory_space_constraint(array, pltpu.HBM)
        for array in (jnp.swapaxes(tile_lists, 1, 2), queries, keys, values, out_grad)
    )
    key_value, lists, keys, values = pl.pallas_call(
        functools.partial(pack_keys_kernel, cap, channels[0]),
        out_shape=[packed, pltpu.SMEM(lists.shape, jnp.int32)] + [whole_near] * 2,
        in_specs=[anywhere] * 3,
        out_specs=[vmem, smem, vmem, vmem],
        scratch_shapes=[pltpu.SemaphoreType.DMA((3, heads))],
        compiler_params=params,
        cost_estimate=brief,
        name="pack_keys",
    )(lists, k_far, v_far)
    fetched = [swapped(key_value, channels[0])]
    table = pl.pallas_call(
        functools.partial(table_kernel, channels, cap),
        out_shape=pltpu.SMEM((table_size,), jnp.int32),
        in_specs=[smem],
        out_specs=smem,
        compiler_params=params,
        cost_estimate=brief,
        name="table",
    )(lists)
    for number in range(1, count):
        key_value = pl.pallas_call(
            functools.partial(pack_more_keys_kernel, count, cap, number),
            out_shape=packed,
            in_specs=[smem, vmem, vmem],
            out_specs=vmem,
            scratch_shapes=[pltpu.SemaphoreType.DMA((2, cap))],
            compiler_params=params,
            cost_estimate=brief,
            name="pack_more_keys",
        )(table, keys, values)
        fetched.append(swapped(key_value, channels[number]))
    one_head = pl.BlockSpec((1, tokens, width), lambda head: (head, 0, 0))
    one_square = pl.BlockSpec((1, tokens, tokens), lambda head: (head, 0, 0))
    sent = [pltpu.VMEM((2, early, tokens, width), jnp.bfloat16)] + [packed] * (count - 1)
    own_weight, own_prob_grad, own_rows, *query_grads = pl.pallas_call(
        functools.partial(own_kernel, count, cap, scale),
        grid=(heads,),
        out_shape=[squares] * 2 + [pltpu.VMEM((heads, 3, tokens), jnp.float32)] + sent,
        in_specs=[smem] + [one_head] * 4 + [anywhere] * 2,
        out_specs=[one_square] * 2
        + [pl.BlockSpec((1, 3, tokens), lambda head: (head, 0, 0))]
        + [pl.BlockSpec(memory_space=pltpu.VMEM)] * count,
        scratch_shapes=[copies],
        compiler_params=params,
        cost_estimate=brief,
        name="own_scores",
    )(table, q_far, keys, values, g_far, q_far, g_far)
    query_grads[1:], fetched[0] = lax.optimization_barrier((query_grads[1:], fetched[0]))
    arrived = [swapped(block, channel) for block, channel in zip(query_grads, channels)]
    far_weight, far_prob_grad, own_factors, far_factors, *stats = pl.pallas_call(
        functools.partial(statistics_kernel, count, cap, scale),
        out_shape=[far_squares] * 2
        + [pltpu.VMEM((heads, 2, tokens), jnp.float32)]
        + [pltpu.VMEM((count * cap, 2, tokens), jnp.float32)]
        + [row_stats] * count,
        in_specs=[smem] + [vmem] * (3 + count),
        out_specs=[vmem] * (4 + count),
        scratch_shapes=[pltpu.VMEM((count * cap, 3, tokens), jnp.float32)],
        compiler_params=params,
        cost_estimate=brief,
        name="statistics",
    )(table, queries, out_grad, own_rows, *fetched)
    stats = [swapped(block, channel) for block, channel in zip(stats, channels)]
    terms = pl.pallas_call(
        functools.partial(returned_kernel, count, cap, scale),
        out_shape=pltpu.VMEM((2, cap - early, tokens, width), jnp.bfloat16),
        in_specs=[smem] + [vmem] * 5,
        out_specs=vmem,
        compiler_params=params,
        cost_estimate=brief,
        name="returned",
    )(table, queries, out_grad, far_weight, far_prob_grad, far_factors)
    terms = swapped(terms, channels[0])
    transposed_sums = pltpu.VMEM((heads, width, tokens), jnp.float32)
    *finished, key_sum, value_sum = pl.pallas_call(
        functools.partial(reader_kernel, count, cap, scale),
        out_shape=[whole_near] * 2 + [whole_sum] * 2,
        in_specs=[smem] + [vmem] * (10 + count),
        out_specs=[vmem] * 4,
        scratch_shapes=[transposed_sums] * 2,
        compiler_params=params,
        cost_estimate=lengthy,
        name="reader",
    )(
        table,
        queries,
        keys,
        values,
        out_grad,
        own_weight,
        own_prob_grad,
        own_factors,
        far_weight,
        far_prob_grad,
        far_factors,
        *fetched,
    )
    results = []
    for number in range(count - 1, 0, -1):
        stored = 2 if number == count - 1 else 0
        outputs = stored + (2 if number == 1 else 0)
        *stored_now, key_sum, value_sum = pl.pallas_call(
            functools.partial(owner_kernel, count, cap, scale, number),
            out_shape=[whole] * outputs + [whole_sum] * 2,
            in_specs=[smem] + [vmem] * (6 + stored),
            out_specs=[anywhere] * outputs + [vmem] * 2,
            scratch_shapes=[whole_pair, copies_whole, copies_whole],
            compiler_params=params,
            cost_estimate=brief,
            name="owner",
        )(
            table,
            keys,
            values,
            arrived[number],
            stats[number],
            key_sum,
            value_sum,
            *(finished if stored else []),
        )
        results += stored_now
    *results, key_grad, value_grad = results
    first, key_sum = lax.optimization_barrier((arrived[0], key_sum))
    key_grad, value_grad = pl.pallas_call(
        functools.partial(first_owner_kernel, count, cap, scale),
        out_shape=[whole] * 2,
        in_specs=[smem] + [vmem] * 6 + [anywhere] * 2,
        out_specs=[anywhere] * 2,
        scratch_shapes=[packed, pltpu.SemaphoreType.DMA((2, cap))],
        input_output_aliases={7: 0, 8: 1},
        compiler_params=params,
        cost_estimate=brief,
        name="first_owner",
    )(table, keys, values, first, stats[0], key_sum, value_sum, key_grad, value_grad)
    terms, key_grad = lax.optimization_barrier((terms, key_grad))
    key_grad, value_grad = pl.pallas_call(
        functools.partial(closing_kernel, count, cap),
        out_shape=[whole] * 2,
        in_specs=[smem] + [vmem] * 3 + [anywhere] * 2,
        out_specs=[anywhere] * 2,
        scratch_shapes=[packed, pltpu.SemaphoreType.DMA((2, cap))],
        input_output_aliases={4: 0, 5: 1},
        compiler_params=params,
        cost_estimate=brief,
        name="closing",
    )(table, terms, key_sum, value_sum, key_grad, value_grad)
    return *results, key_grad, value_grad


def solution(mesh):
    tokens_placed = P("mp", ("clips", "seq"), None)
    return jax.shard_map(
        per_device,
        mesh=mesh,
        in_specs=(tokens_placed,) * 4 + (P("mp", None, None),),
        out_specs=(tokens_placed,) * 4,
        check_vma=False,
    )
```

```python
import functools

import jax
import jax.numpy as jnp
from jax import lax
from jax.experimental import pallas as pl
from jax.experimental.pallas import tpu as pltpu
from jax.sharding import PartitionSpec as P

GX = 8
LOG2E = 1.4426950408889634
LOWEST = -3.0e38
VMEM_LIMIT = 24 * 1024 * 1024


def channel_list(tile_count):
    row_tiles = min(4, tile_count // GX)
    layer_size = GX * row_tiles
    distances = [1]
    if row_tiles > 1:
        distances.append(GX)
    if tile_count // layer_size > 1:
        distances.append(layer_size)
    return [(distance, colour) for distance in distances for colour in (0, 1)]


def swap_route(channel, tile_count):
    distance, colour = channel
    route = []
    for low in range(tile_count - distance):
        if (low // distance) % 2 == colour:
            route += [(low, low + distance), (low + distance, low)]
    return route


def swapped(block, channel):
    return lax.ppermute(block, "seq", swap_route(channel, lax.axis_size("seq")))


def partner_of(own_tile, channel):
    distance, colour = channel
    is_low = lax.rem(lax.div(own_tile, distance), 2) == colour
    return jnp.where(is_low, own_tile + distance, own_tile - distance)


def dot_nt(a, b):
    return lax.dot_general(a, b, (((1,), (1,)), ((), ())), preferred_element_type=jnp.float32)


def dot_tn(a, b):
    return lax.dot_general(a, b, (((0,), (0,)), ((), ())), preferred_element_type=jnp.float32)


def dot_nn(a, b):
    return lax.dot_general(a, b, (((1,), (0,)), ((), ())), preferred_element_type=jnp.float32)


class Table:
    def __init__(self, ref, heads, count, cap):
        self.ref, self.heads, self.count, self.cap = ref, heads, count, cap

    def slot_at(self, head, number):
        return head * self.count + number

    def reader_at(self, number, slot):
        return self.heads * self.count + number * self.cap + slot

    def owner_at(self, number, slot):
        return self.reader_at(self.count + number, slot)

    def size(self):
        return self.owner_at(self.count - 1, self.cap - 1) + 1


def names(lists, head, reader, tile):
    entries = range(1, lists.shape[1])
    return functools.reduce(jnp.logical_or, [lists[head, entry, reader] == tile for entry in entries])


def pack_keys_kernel(cap, channel, lists_hbm, keys, values, target, lists, *rest):
    *held, sems = rest
    heads, _, tile_count = lists.shape
    loads = [pltpu.make_async_copy(lists_hbm, lists, sems.at[2, 0])]
    for part, source in enumerate((keys, values)):
        for head in range(heads):
            loads.append(
                pltpu.make_async_copy(source.at[head], held[part].at[head], sems.at[part, head])
            )
    for load in loads:
        load.start()
    loads[0].wait()
    own_tile = lax.axis_index("seq")
    partner = partner_of(own_tile, channel)
    inside = (partner >= 0) & (partner < tile_count)
    reader = jnp.clip(partner, 0, tile_count - 1)
    filled = jnp.int32(0)
    chosen = [jnp.int32(0)] * cap
    for head in range(heads):
        wanted = names(lists, head, reader, own_tile) & inside
        for slot in range(cap):
            chosen[slot] = jnp.where(wanted & (filled == slot), head, chosen[slot])
        filled = filled + wanted.astype(jnp.int32)
    for load in loads[1:]:
        load.wait()
    for slot in range(cap):
        for part in range(2):
            target[part, slot] = held[part][chosen[slot]]


def pack_more_keys_kernel(count, cap, number, table_ref, keys, values, target, sems):
    table = Table(table_ref, keys.shape[0], count, cap)
    for stage in ("start", "wait"):
        for slot in range(cap):
            head = table_ref[table.owner_at(number, slot)]

            @pl.when(head >= 0)
            def _():
                for part, source in enumerate((keys, values)):
                    copy = pltpu.make_async_copy(
                        source.at[head], target.at[part, slot], sems.at[part, slot]
                    )
                    if stage == "start":
                        copy.start()
                    else:
                        copy.wait()


def table_kernel(channels, cap, lists, table_ref):
    heads, _, tile_count = lists.shape
    table = Table(table_ref, heads, len(channels), cap)
    own_tile = lax.axis_index("seq")
    for number, channel in enumerate(channels):
        partner = partner_of(own_tile, channel)
        inside = (partner >= 0) & (partner < tile_count)
        reader = jnp.clip(partner, 0, tile_count - 1)
        for slot in range(cap):
            table_ref[table.owner_at(number, slot)] = -1
            table_ref[table.reader_at(number, slot)] = -1
        filled = [jnp.int32(0), jnp.int32(0)]
        for head in range(heads):
            given = names(lists, head, reader, own_tile) & inside & (filled[0] < cap)
            named = names(lists, head, own_tile, partner) & inside & (filled[1] < cap)
            table_ref[table.slot_at(head, number)] = jnp.where(named, filled[1], -1)

            @pl.when(given)
            def _():
                table_ref[table.owner_at(number, filled[0])] = head

            @pl.when(named)
            def _():
                table_ref[table.reader_at(number, filled[1])] = head

            filled = [filled[0] + given.astype(jnp.int32), filled[1] + named.astype(jnp.int32)]


def own_kernel(count, cap, scale, table_ref, q_ref, k_ref, v_ref, g_ref, queries, grads, *rest):
    weight_ref, prob_grad_ref, rows_ref, *targets, sems = rest
    heads = queries.shape[0]
    table = Table(table_ref, heads, count, cap)

    def copies(stage):
        for number in range(count):
            for slot in range(targets[number].shape[1]):
                head = table_ref[table.reader_at(number, slot)]

                @pl.when(head >= 0)
                def _():
                    for part, source in enumerate((queries, grads)):
                        copy = pltpu.make_async_copy(
                            source.at[head],
                            targets[number].at[part, slot],
                            sems.at[number, part, slot],
                        )
                        if stage == "start":
                            copy.start()
                        else:
                            copy.wait()

    pl.when(pl.program_id(0) == 0)(lambda: copies("start"))
    score = dot_nt(k_ref[0], q_ref[0]) * (scale * LOG2E)
    top = jnp.max(score, axis=0, keepdims=True)
    weight = jnp.exp2(score - top)
    prob_grad = dot_nt(v_ref[0], g_ref[0])
    weight_ref[0] = weight
    prob_grad_ref[0] = prob_grad
    rows_ref[0, 0:1] = top
    rows_ref[0, 1:2] = jnp.sum(weight, axis=0, keepdims=True)
    rows_ref[0, 2:3] = jnp.sum(weight * prob_grad, axis=0, keepdims=True)
    pl.when(pl.program_id(0) == heads - 1)(lambda: copies("wait"))


def statistics_kernel(count, cap, scale, table_ref, q_ref, g_ref, own_rows, *rest):
    fetched, rest = rest[:count], rest[count:]
    weight_ref, prob_grad_ref, own_factors, far_factors = rest[:4]
    stats, far_rows = rest[4 : 4 + count], rest[4 + count]
    heads = q_ref.shape[0]
    table = Table(table_ref, heads, count, cap)
    for number in range(count):
        for slot in range(cap):
            head = jnp.maximum(table_ref[table.reader_at(number, slot)], 0)
            place = number * cap + slot
            score = dot_nt(fetched[number][0, slot], q_ref[head]) * (scale * LOG2E)
            top = jnp.max(score, axis=0, keepdims=True)
            weight = jnp.exp2(score - top)
            prob_grad = dot_nt(fetched[number][1, slot], g_ref[head])
            weight_ref[place] = weight
            prob_grad_ref[place] = prob_grad
            far_rows[place, 0:1] = top
            far_rows[place, 1:2] = jnp.sum(weight, axis=0, keepdims=True)
            far_rows[place, 2:3] = jnp.sum(weight * prob_grad, axis=0, keepdims=True)
    for head in range(heads):
        rows = [own_rows[head]]
        slots = [table_ref[table.slot_at(head, number)] for number in range(count)]
        for number in range(count):
            found = far_rows[number * cap + jnp.maximum(slots[number], 0)]
            missing = jnp.where(
                lax.broadcasted_iota(jnp.int32, found.shape, 0) == 0, LOWEST, 0.0
            )
            rows.append(jnp.where(slots[number] >= 0, found, missing))
        top = functools.reduce(jnp.maximum, [row[0:1] for row in rows])
        factors = [jnp.exp2(row[0:1] - top) for row in rows]
        total = sum(factor * row[1:2] for factor, row in zip(factors, rows))
        inverse = 1.0 / total
        delta = sum(factor * row[2:3] for factor, row in zip(factors, rows)) * inverse
        level = top + jnp.log2(total)
        own_factors[head, 0:1] = factors[0] * inverse
        own_factors[head, 1:2] = delta
        for number in range(count):

            @pl.when(slots[number] >= 0)
            def _():
                place = number * cap + slots[number]
                far_factors[place, 0:1] = factors[1 + number] * inverse
                far_factors[place, 1:2] = delta
                stats[number][slots[number], 0:1] = level
                stats[number][slots[number], 1:2] = delta


def softmax_grad(weight, prob_grad, factors):
    prob = weight * factors[0:1]
    score_grad = prob * (prob_grad - factors[1:2])
    return prob.astype(jnp.bfloat16), score_grad.astype(jnp.bfloat16)


def returned_kernel(count, cap, scale, table_ref, q_ref, g_ref, *rest):
    far_weight, far_prob_grad, far_factors, terms = rest
    table = Table(table_ref, q_ref.shape[0], count, cap)
    returned = terms.shape[1]
    for number in range(returned):
        place = cap - returned + number
        head = jnp.maximum(table_ref[table.reader_at(0, place)], 0)
        prob, score_grad = softmax_grad(
            far_weight[place], far_prob_grad[place], far_factors[place]
        )
        terms[0, number] = (dot_nn(score_grad, q_ref[head]) * scale).astype(jnp.bfloat16)
        terms[1, number] = dot_nn(prob, g_ref[head]).astype(jnp.bfloat16)


def reader_kernel(count, cap, scale, table_ref, q_ref, k_ref, v_ref, g_ref, *rest):
    own_weight, own_prob_grad, own_factors, far_weight, far_prob_grad, far_factors = rest[:6]
    fetched, rest = rest[6 : 6 + count], rest[6 + count :]
    o_ref, dq_ref, dk_ref, dv_ref, o_sum, dq_sum = rest
    heads = q_ref.shape[0]
    table = Table(table_ref, heads, count, cap)
    for head in range(heads):
        prob, score_grad = softmax_grad(own_weight[head], own_prob_grad[head], own_factors[head])
        o_sum[head] = dot_tn(v_ref[head], prob)
        dq_sum[head] = dot_tn(k_ref[head], score_grad)
        dk_ref[head] = dot_nn(score_grad, q_ref[head]) * scale
        dv_ref[head] = dot_nn(prob, g_ref[head])
    for number in range(count):
        for slot in range(cap):
            found = table_ref[table.reader_at(number, slot)]
            head = jnp.maximum(found, 0)
            place = number * cap + slot
            prob, score_grad = softmax_grad(
                far_weight[place], far_prob_grad[place], far_factors[place]
            )
            o_term = dot_tn(fetched[number][1, slot], prob)
            dq_term = dot_tn(fetched[number][0, slot], score_grad)
            o_sum[head] += jnp.where(found >= 0, o_term, 0.0)
            dq_sum[head] += jnp.where(found >= 0, dq_term, 0.0)
    for head in range(heads):
        o_ref[head] = o_sum[head].T.astype(jnp.bfloat16)
        dq_ref[head] = (dq_sum[head] * scale).T.astype(jnp.bfloat16)


def owner_terms(table, number, scale, k_ref, v_ref, arrived, stats, slot):
    found = table.ref[table.owner_at(number, slot)]
    head = jnp.maximum(found, 0)
    query, grad = arrived[0, slot], arrived[1, slot]
    score = dot_nt(k_ref[head], query) * (scale * LOG2E)
    prob = jnp.exp2(score - stats[slot, 0:1])
    prob_grad = dot_nt(v_ref[head], grad)
    score_grad = (prob * (prob_grad - stats[slot, 1:2])).astype(jnp.bfloat16)
    dk_term = dot_nn(score_grad, query) * scale
    dv_term = dot_nn(prob.astype(jnp.bfloat16), grad)
    return found, head, jnp.where(found >= 0, dk_term, 0.0), jnp.where(found >= 0, dv_term, 0.0)


def owner_kernel(count, cap, scale, number, table_ref, k_ref, v_ref, arrived, stats, *rest):
    *rest, dk_sum, dv_sum, rounded, sems, rounded_sems = rest
    heads = k_ref.shape[0]
    table = Table(table_ref, heads, count, cap)
    closing = number == 1
    results = rest[2:]
    if closing:
        *results, dk_out, dv_out = results
    copies = []
    for part in range(len(results) // 2):
        for head in range(heads):
            source, result = results[part], results[part + len(results) // 2]
            copies.append(
                pltpu.make_async_copy(source.at[head], result.at[head], sems.at[part, head])
            )
    for copy in copies:
        copy.start()
    for total, given in zip((dk_sum, dv_sum), rest):
        for head in range(heads):
            total[head] = given[head]
    for slot in range(cap):
        _, head, dk_term, dv_term = owner_terms(
            table, number, scale, k_ref, v_ref, arrived, stats, slot
        )
        dk_sum[head] += dk_term
        dv_sum[head] += dv_term
    complete = []
    if closing:
        awaited = [table_ref[table.owner_at(0, slot)] for slot in range(cap)]
        for head in range(heads):
            wanted = functools.reduce(jnp.logical_and, [owner != head for owner in awaited])
            for part, (total, result) in enumerate(((dk_sum, dk_out), (dv_sum, dv_out))):
                rounded[part, head] = total[head].astype(jnp.bfloat16)
                copy = pltpu.make_async_copy(
                    rounded.at[part, head], result.at[head], rounded_sems.at[part, head]
                )
                complete.append((wanted, copy))
    for wanted, copy in complete:
        pl.when(wanted)(copy.start)
    for copy in copies:
        copy.wait()
    for wanted, copy in complete:
        pl.when(wanted)(copy.wait)


def first_owner_kernel(count, cap, scale, table_ref, k_ref, v_ref, arrived, stats, *rest):
    dk_in, dv_in, _, _, dk_out, dv_out, staged, sems = rest
    table = Table(table_ref, k_ref.shape[0], count, cap)
    stores = []
    for slot in range(arrived.shape[1]):
        found, head, *terms = owner_terms(
            table, 0, scale, k_ref, v_ref, arrived, stats, slot
        )
        for part, (total, result) in enumerate(((dk_in, dk_out), (dv_in, dv_out))):
            staged[part, slot] = (total[head] + terms[part]).astype(jnp.bfloat16)
            store = pltpu.make_async_copy(
                staged.at[part, slot], result.at[head], sems.at[part, slot]
            )
            stores.append((found >= 0, store))
    for wanted, store in stores:
        pl.when(wanted)(store.start)
    for wanted, store in stores:
        pl.when(wanted)(store.wait)


def closing_kernel(count, cap, table_ref, terms, dk_in, dv_in, *rest):
    _, _, dk_out, dv_out, staged, sems = rest
    table = Table(table_ref, dk_in.shape[0], count, cap)
    returned = terms.shape[1]
    stores = []
    for number in range(returned):
        found = table_ref[table.owner_at(0, cap - returned + number)]
        head = jnp.maximum(found, 0)
        for part, (total, result) in enumerate(((dk_in, dk_out), (dv_in, dv_out))):
            term = terms[part, number].astype(jnp.float32)
            staged[part, number] = (total[head] + term).astype(jnp.bfloat16)
            store = pltpu.make_async_copy(
                staged.at[part, number], result.at[head], sems.at[part, number]
            )
            stores.append((found >= 0, store))
    for wanted, store in stores:
        pl.when(wanted)(store.start)
    for wanted, store in stores:
        pl.when(wanted)(store.wait)


def per_device(queries, keys, values, out_grad, tile_lists):
    heads, tokens, width = queries.shape
    channels = channel_list(lax.axis_size("seq"))
    count = len(channels)
    cap = heads // 2
    early = cap - 1
    scale = width ** (-0.5)
    table_size = Table(None, heads, count, cap).size()
    smem = pl.BlockSpec(memory_space=pltpu.SMEM)
    anywhere = pl.BlockSpec(memory_space=pl.ANY)
    vmem = pl.BlockSpec(memory_space=pltpu.VMEM)
    params = pltpu.CompilerParams(vmem_limit_bytes=VMEM_LIMIT)
    brief = pl.CostEstimate(flops=1, bytes_accessed=1, transcendentals=0)
    lengthy = pl.CostEstimate(flops=10**11, bytes_accessed=1, transcendentals=0)
    packed = pltpu.VMEM((2, cap, tokens, width), jnp.bfloat16)
    whole = jax.ShapeDtypeStruct((heads, tokens, width), jnp.bfloat16)
    whole_near = pltpu.VMEM((heads, tokens, width), jnp.bfloat16)
    whole_pair = pltpu.VMEM((2, heads, tokens, width), jnp.bfloat16)
    copies_whole = pltpu.SemaphoreType.DMA((2, heads))
    whole_sum = pltpu.VMEM((heads, tokens, width), jnp.float32)
    squares = pltpu.VMEM((heads, tokens, tokens), jnp.float32)
    far_squares = pltpu.VMEM((count * cap, tokens, tokens), jnp.float32)
    row_stats = pltpu.VMEM((cap, 2, tokens), jnp.float32)
    copies = pltpu.SemaphoreType.DMA((count, 2, cap))
    lists, q_far, k_far, v_far, g_far = (
        pltpu.with_memory_space_constraint(array, pltpu.HBM)
        for array in (jnp.swapaxes(tile_lists, 1, 2), queries, keys, values, out_grad)
    )
    key_value, lists, keys, values = pl.pallas_call(
        functools.partial(pack_keys_kernel, cap, channels[0]),
        out_shape=[packed, pltpu.SMEM(lists.shape, jnp.int32)] + [whole_near] * 2,
        in_specs=[anywhere] * 3,
        out_specs=[vmem, smem, vmem, vmem],
        scratch_shapes=[pltpu.SemaphoreType.DMA((3, heads))],
        compiler_params=params,
        cost_estimate=brief,
        name="pack_keys",
    )(lists, k_far, v_far)
    fetched = [swapped(key_value, channels[0])]
    table = pl.pallas_call(
        functools.partial(table_kernel, channels, cap),
        out_shape=pltpu.SMEM((table_size,), jnp.int32),
        in_specs=[smem],
        out_specs=smem,
        compiler_params=params,
        cost_estimate=brief,
        name="table",
    )(lists)
    for number in range(1, count):
        key_value = pl.pallas_call(
            functools.partial(pack_more_keys_kernel, count, cap, number),
            out_shape=packed,
            in_specs=[smem, vmem, vmem],
            out_specs=vmem,
            scratch_shapes=[pltpu.SemaphoreType.DMA((2, cap))],
            compiler_params=params,
            cost_estimate=brief,
            name="pack_more_keys",
        )(table, keys, values)
        fetched.append(swapped(key_value, channels[number]))
    one_head = pl.BlockSpec((1, tokens, width), lambda head: (head, 0, 0))
    one_square = pl.BlockSpec((1, tokens, tokens), lambda head: (head, 0, 0))
    sent = [pltpu.VMEM((2, early, tokens, width), jnp.bfloat16)] + [packed] * (count - 1)
    own_weight, own_prob_grad, own_rows, *query_grads = pl.pallas_call(
        functools.partial(own_kernel, count, cap, scale),
        grid=(heads,),
        out_shape=[squares] * 2 + [pltpu.VMEM((heads, 3, tokens), jnp.float32)] + sent,
        in_specs=[smem] + [one_head] * 4 + [anywhere] * 2,
        out_specs=[one_square] * 2
        + [pl.BlockSpec((1, 3, tokens), lambda head: (head, 0, 0))]
        + [pl.BlockSpec(memory_space=pltpu.VMEM)] * count,
        scratch_shapes=[copies],
        compiler_params=params,
        cost_estimate=brief,
        name="own_scores",
    )(table, q_far, keys, values, g_far, q_far, g_far)
    query_grads[1:], fetched[0] = lax.optimization_barrier((query_grads[1:], fetched[0]))
    arrived = [swapped(block, channel) for block, channel in zip(query_grads, channels)]
    far_weight, far_prob_grad, own_factors, far_factors, *stats = pl.pallas_call(
        functools.partial(statistics_kernel, count, cap, scale),
        out_shape=[far_squares] * 2
        + [pltpu.VMEM((heads, 2, tokens), jnp.float32)]
        + [pltpu.VMEM((count * cap, 2, tokens), jnp.float32)]
        + [row_stats] * count,
        in_specs=[smem] + [vmem] * (3 + count),
        out_specs=[vmem] * (4 + count),
        scratch_shapes=[pltpu.VMEM((count * cap, 3, tokens), jnp.float32)],
        compiler_params=params,
        cost_estimate=brief,
        name="statistics",
    )(table, queries, out_grad, own_rows, *fetched)
    stats = [swapped(block, channel) for block, channel in zip(stats, channels)]
    terms = pl.pallas_call(
        functools.partial(returned_kernel, count, cap, scale),
        out_shape=pltpu.VMEM((2, cap - early, tokens, width), jnp.bfloat16),
        in_specs=[smem] + [vmem] * 5,
        out_specs=vmem,
        compiler_params=params,
        cost_estimate=brief,
        name="returned",
    )(table, queries, out_grad, far_weight, far_prob_grad, far_factors)
    terms = swapped(terms, channels[0])
    transposed_sums = pltpu.VMEM((heads, width, tokens), jnp.float32)
    *finished, key_sum, value_sum = pl.pallas_call(
        functools.partial(reader_kernel, count, cap, scale),
        out_shape=[whole_near] * 2 + [whole_sum] * 2,
        in_specs=[smem] + [vmem] * (10 + count),
        out_specs=[vmem] * 4,
        scratch_shapes=[transposed_sums] * 2,
        compiler_params=params,
        cost_estimate=lengthy,
        name="reader",
    )(
        table,
        queries,
        keys,
        values,
        out_grad,
        own_weight,
        own_prob_grad,
        own_factors,
        far_weight,
        far_prob_grad,
        far_factors,
        *fetched,
    )
    results = []
    for number in range(count - 1, 0, -1):
        stored = 2 if number == count - 1 else 0
        outputs = stored + (2 if number == 1 else 0)
        *stored_now, key_sum, value_sum = pl.pallas_call(
            functools.partial(owner_kernel, count, cap, scale, number),
            out_shape=[whole] * outputs + [whole_sum] * 2,
            in_specs=[smem] + [vmem] * (6 + stored),
            out_specs=[anywhere] * outputs + [vmem] * 2,
            scratch_shapes=[whole_pair, copies_whole, copies_whole],
            compiler_params=params,
            cost_estimate=brief,
            name="owner",
        )(
            table,
            keys,
            values,
            arrived[number],
            stats[number],
            key_sum,
            value_sum,
            *(finished if stored else []),
        )
        results += stored_now
    *results, key_grad, value_grad = results
    first, key_sum = lax.optimization_barrier((arrived[0], key_sum))
    key_grad, value_grad = pl.pallas_call(
        functools.partial(first_owner_kernel, count, cap, scale),
        out_shape=[whole] * 2,
        in_specs=[smem] + [vmem] * 6 + [anywhere] * 2,
        out_specs=[anywhere] * 2,
        scratch_shapes=[packed, pltpu.SemaphoreType.DMA((2, cap))],
        input_output_aliases={7: 0, 8: 1},
        compiler_params=params,
        cost_estimate=brief,
        name="first_owner",
    )(table, keys, values, first, stats[0], key_sum, value_sum, key_grad, value_grad)
    terms, key_grad = lax.optimization_barrier((terms, key_grad))
    key_grad, value_grad = pl.pallas_call(
        functools.partial(closing_kernel, count, cap),
        out_shape=[whole] * 2,
        in_specs=[smem] + [vmem] * 3 + [anywhere] * 2,
        out_specs=[anywhere] * 2,
        scratch_shapes=[packed, pltpu.SemaphoreType.DMA((2, cap))],
        input_output_aliases={4: 0, 5: 1},
        compiler_params=params,
        cost_estimate=brief,
        name="closing",
    )(table, terms, key_sum, value_sum, key_grad, value_grad)
    return *results, key_grad, value_grad


def solution(mesh):
    tokens_placed = P("mp", ("clips", "seq"), None)
    return jax.shard_map(
        per_device,
        mesh=mesh,
        in_specs=(tokens_placed,) * 4 + (P("mp", None, None),),
        out_specs=(tokens_placed,) * 4,
        check_vma=False,
    )
```

```python
import functools

import jax
import jax.numpy as jnp
from jax import lax
from jax.experimental import pallas as pl
from jax.experimental.pallas import tpu as pltpu
from jax.sharding import PartitionSpec as P

GX = 8
LOG2E = 1.4426950408889634
LOWEST = -3.0e38
VMEM_LIMIT = 24 * 1024 * 1024


def channel_list(tile_count):
    row_tiles = min(4, tile_count // GX)
    layer_size = GX * row_tiles
    distances = [1]
    if row_tiles > 1:
        distances.append(GX)
    if tile_count // layer_size > 1:
        distances.append(layer_size)
    return [(distance, colour) for distance in distances for colour in (0, 1)]


def swap_route(channel, tile_count):
    distance, colour = channel
    route = []
    for low in range(tile_count - distance):
        if (low // distance) % 2 == colour:
            route += [(low, low + distance), (low + distance, low)]
    return route


def swapped(block, channel):
    return lax.ppermute(block, "seq", swap_route(channel, lax.axis_size("seq")))


def partner_of(own_tile, channel):
    distance, colour = channel
    is_low = lax.rem(lax.div(own_tile, distance), 2) == colour
    return jnp.where(is_low, own_tile + distance, own_tile - distance)


def dot_nt(a, b):
    return lax.dot_general(a, b, (((1,), (1,)), ((), ())), preferred_element_type=jnp.float32)


def dot_tn(a, b):
    return lax.dot_general(a, b, (((0,), (0,)), ((), ())), preferred_element_type=jnp.float32)


def dot_nn(a, b):
    return lax.dot_general(a, b, (((1,), (0,)), ((), ())), preferred_element_type=jnp.float32)


class Table:
    def __init__(self, ref, heads, count, cap):
        self.ref, self.heads, self.count, self.cap = ref, heads, count, cap

    def slot_at(self, head, number):
        return head * self.count + number

    def reader_at(self, number, slot):
        return self.heads * self.count + number * self.cap + slot

    def owner_at(self, number, slot):
        return self.reader_at(self.count + number, slot)

    def size(self):
        return self.owner_at(self.count - 1, self.cap - 1) + 1


def names(lists, head, reader, tile):
    entries = range(1, lists.shape[1])
    return functools.reduce(jnp.logical_or, [lists[head, entry, reader] == tile for entry in entries])


def pack_keys_kernel(cap, channel, lists_hbm, keys, values, target, lists, *rest):
    *held, sems = rest
    heads, _, tile_count = lists.shape
    loads = [pltpu.make_async_copy(lists_hbm, lists, sems.at[2])]
    for part, source in enumerate((keys, values)):
        loads.append(pltpu.make_async_copy(source, held[part], sems.at[part]))
    for load in loads:
        load.start()
    loads[0].wait()
    own_tile = lax.axis_index("seq")
    partner = partner_of(own_tile, channel)
    inside = (partner >= 0) & (partner < tile_count)
    reader = jnp.clip(partner, 0, tile_count - 1)
    filled = jnp.int32(0)
    chosen = [jnp.int32(0)] * cap
    for head in range(heads):
        wanted = names(lists, head, reader, own_tile) & inside
        for slot in range(cap):
            chosen[slot] = jnp.where(wanted & (filled == slot), head, chosen[slot])
        filled = filled + wanted.astype(jnp.int32)
    for load in loads[1:]:
        load.wait()
    for slot in range(cap):
        for part in range(2):
            target[part, slot] = held[part][chosen[slot]]


def pack_more_keys_kernel(count, cap, number, table_ref, keys, values, target, sems):
    table = Table(table_ref, keys.shape[0], count, cap)
    for stage in ("start", "wait"):
        for slot in range(cap):
            head = table_ref[table.owner_at(number, slot)]

            @pl.when(head >= 0)
            def _():
                for part, source in enumerate((keys, values)):
                    copy = pltpu.make_async_copy(
                        source.at[head], target.at[part, slot], sems.at[part, slot]
                    )
                    if stage == "start":
                        copy.start()
                    else:
                        copy.wait()


def table_kernel(channels, cap, lists, table_ref):
    heads, _, tile_count = lists.shape
    table = Table(table_ref, heads, len(channels), cap)
    own_tile = lax.axis_index("seq")
    for number, channel in enumerate(channels):
        partner = partner_of(own_tile, channel)
        inside = (partner >= 0) & (partner < tile_count)
        reader = jnp.clip(partner, 0, tile_count - 1)
        for slot in range(cap):
            table_ref[table.owner_at(number, slot)] = -1
            table_ref[table.reader_at(number, slot)] = -1
        filled = [jnp.int32(0), jnp.int32(0)]
        for head in range(heads):
            given = names(lists, head, reader, own_tile) & inside & (filled[0] < cap)
            named = names(lists, head, own_tile, partner) & inside & (filled[1] < cap)
            table_ref[table.slot_at(head, number)] = jnp.where(named, filled[1], -1)

            @pl.when(given)
            def _():
                table_ref[table.owner_at(number, filled[0])] = head

            @pl.when(named)
            def _():
                table_ref[table.reader_at(number, filled[1])] = head

            filled = [filled[0] + given.astype(jnp.int32), filled[1] + named.astype(jnp.int32)]


def own_kernel(count, cap, scale, table_ref, q_ref, k_ref, v_ref, g_ref, queries, grads, *rest):
    weight_ref, prob_grad_ref, rows_ref, *targets, sems = rest
    heads = queries.shape[0]
    table = Table(table_ref, heads, count, cap)

    def copies(stage):
        for number in range(count):
            for slot in range(targets[number].shape[1]):
                head = table_ref[table.reader_at(number, slot)]

                @pl.when(head >= 0)
                def _():
                    for part, source in enumerate((queries, grads)):
                        copy = pltpu.make_async_copy(
                            source.at[head],
                            targets[number].at[part, slot],
                            sems.at[number, part, slot],
                        )
                        if stage == "start":
                            copy.start()
                        else:
                            copy.wait()

    pl.when(pl.program_id(0) == 0)(lambda: copies("start"))
    score = dot_nt(k_ref[0], q_ref[0]) * (scale * LOG2E)
    top = jnp.max(score, axis=0, keepdims=True)
    weight = jnp.exp2(score - top)
    prob_grad = dot_nt(v_ref[0], g_ref[0])
    weight_ref[0] = weight
    prob_grad_ref[0] = prob_grad
    rows_ref[0, 0:1] = top
    rows_ref[0, 1:2] = jnp.sum(weight, axis=0, keepdims=True)
    rows_ref[0, 2:3] = jnp.sum(weight * prob_grad, axis=0, keepdims=True)
    pl.when(pl.program_id(0) == heads - 1)(lambda: copies("wait"))


def statistics_kernel(count, cap, scale, table_ref, q_ref, g_ref, own_rows, *rest):
    fetched, rest = rest[:count], rest[count:]
    weight_ref, prob_grad_ref, own_factors, far_factors = rest[:4]
    stats, far_rows = rest[4 : 4 + count], rest[4 + count]
    heads = q_ref.shape[0]
    table = Table(table_ref, heads, count, cap)
    for number in range(count):
        for slot in range(cap):
            head = jnp.maximum(table_ref[table.reader_at(number, slot)], 0)
            place = number * cap + slot
            score = dot_nt(fetched[number][0, slot], q_ref[head]) * (scale * LOG2E)
            top = jnp.max(score, axis=0, keepdims=True)
            weight = jnp.exp2(score - top)
            prob_grad = dot_nt(fetched[number][1, slot], g_ref[head])
            weight_ref[place] = weight
            prob_grad_ref[place] = prob_grad
            far_rows[place, 0:1] = top
            far_rows[place, 1:2] = jnp.sum(weight, axis=0, keepdims=True)
            far_rows[place, 2:3] = jnp.sum(weight * prob_grad, axis=0, keepdims=True)
    for head in range(heads):
        rows = [own_rows[head]]
        slots = [table_ref[table.slot_at(head, number)] for number in range(count)]
        for number in range(count):
            found = far_rows[number * cap + jnp.maximum(slots[number], 0)]
            missing = jnp.where(
                lax.broadcasted_iota(jnp.int32, found.shape, 0) == 0, LOWEST, 0.0
            )
            rows.append(jnp.where(slots[number] >= 0, found, missing))
        top = functools.reduce(jnp.maximum, [row[0:1] for row in rows])
        factors = [jnp.exp2(row[0:1] - top) for row in rows]
        total = sum(factor * row[1:2] for factor, row in zip(factors, rows))
        inverse = 1.0 / total
        delta = sum(factor * row[2:3] for factor, row in zip(factors, rows)) * inverse
        level = top + jnp.log2(total)
        own_factors[head, 0:1] = factors[0] * inverse
        own_factors[head, 1:2] = delta
        for number in range(count):

            @pl.when(slots[number] >= 0)
            def _():
                place = number * cap + slots[number]
                far_factors[place, 0:1] = factors[1 + number] * inverse
                far_factors[place, 1:2] = delta
                stats[number][slots[number], 0:1] = level
                stats[number][slots[number], 1:2] = delta


def softmax_grad(weight, prob_grad, factors):
    prob = weight * factors[0:1]
    score_grad = prob * (prob_grad - factors[1:2])
    return prob.astype(jnp.bfloat16), score_grad.astype(jnp.bfloat16)


def returned_kernel(count, cap, scale, table_ref, q_ref, g_ref, *rest):
    far_weight, far_prob_grad, far_factors, terms = rest
    table = Table(table_ref, q_ref.shape[0], count, cap)
    returned = terms.shape[1]
    for number in range(returned):
        place = cap - returned + number
        head = jnp.maximum(table_ref[table.reader_at(0, place)], 0)
        prob, score_grad = softmax_grad(
            far_weight[place], far_prob_grad[place], far_factors[place]
        )
        terms[0, number] = (dot_nn(score_grad, q_ref[head]) * scale).astype(jnp.bfloat16)
        terms[1, number] = dot_nn(prob, g_ref[head]).astype(jnp.bfloat16)


def reader_kernel(count, cap, scale, table_ref, q_ref, k_ref, v_ref, g_ref, *rest):
    own_weight, own_prob_grad, own_factors, far_weight, far_prob_grad, far_factors = rest[:6]
    fetched, rest = rest[6 : 6 + count], rest[6 + count :]
    o_ref, dq_ref, dk_ref, dv_ref, o_sum, dq_sum = rest
    heads = q_ref.shape[0]
    table = Table(table_ref, heads, count, cap)
    for head in range(heads):
        prob, score_grad = softmax_grad(own_weight[head], own_prob_grad[head], own_factors[head])
        o_sum[head] = dot_tn(v_ref[head], prob)
        dq_sum[head] = dot_tn(k_ref[head], score_grad)
        dk_ref[head] = dot_nn(score_grad, q_ref[head]) * scale
        dv_ref[head] = dot_nn(prob, g_ref[head])
    for number in range(count):
        for slot in range(cap):
            found = table_ref[table.reader_at(number, slot)]
            head = jnp.maximum(found, 0)
            place = number * cap + slot
            prob, score_grad = softmax_grad(
                far_weight[place], far_prob_grad[place], far_factors[place]
            )
            o_term = dot_tn(fetched[number][1, slot], prob)
            dq_term = dot_tn(fetched[number][0, slot], score_grad)
            o_sum[head] += jnp.where(found >= 0, o_term, 0.0)
            dq_sum[head] += jnp.where(found >= 0, dq_term, 0.0)
    for head in range(heads):
        o_ref[head] = o_sum[head].T.astype(jnp.bfloat16)
        dq_ref[head] = (dq_sum[head] * scale).T.astype(jnp.bfloat16)


def owner_terms(table, number, scale, k_ref, v_ref, arrived, stats, slot):
    found = table.ref[table.owner_at(number, slot)]
    head = jnp.maximum(found, 0)
    query, grad = arrived[0, slot], arrived[1, slot]
    score = dot_nt(k_ref[head], query) * (scale * LOG2E)
    prob = jnp.exp2(score - stats[slot, 0:1])
    prob_grad = dot_nt(v_ref[head], grad)
    score_grad = (prob * (prob_grad - stats[slot, 1:2])).astype(jnp.bfloat16)
    dk_term = dot_nn(score_grad, query) * scale
    dv_term = dot_nn(prob.astype(jnp.bfloat16), grad)
    return found, head, jnp.where(found >= 0, dk_term, 0.0), jnp.where(found >= 0, dv_term, 0.0)


def owner_kernel(count, cap, scale, number, table_ref, k_ref, v_ref, arrived, stats, *rest):
    *rest, dk_sum, dv_sum, rounded, sems, rounded_sems = rest
    heads = k_ref.shape[0]
    table = Table(table_ref, heads, count, cap)
    closing = number == 1
    results = rest[2:]
    if closing:
        *results, dk_out, dv_out = results
    copies = []
    for part in range(len(results) // 2):
        for head in range(heads):
            source, result = results[part], results[part + len(results) // 2]
            copies.append(
                pltpu.make_async_copy(source.at[head], result.at[head], sems.at[part, head])
            )
    for copy in copies:
        copy.start()
    for total, given in zip((dk_sum, dv_sum), rest):
        for head in range(heads):
            total[head] = given[head]
    for slot in range(cap):
        _, head, dk_term, dv_term = owner_terms(
            table, number, scale, k_ref, v_ref, arrived, stats, slot
        )
        dk_sum[head] += dk_term
        dv_sum[head] += dv_term
    complete = []
    if closing:
        awaited = [table_ref[table.owner_at(0, slot)] for slot in range(cap)]
        for head in range(heads):
            wanted = functools.reduce(jnp.logical_and, [owner != head for owner in awaited])
            for part, (total, result) in enumerate(((dk_sum, dk_out), (dv_sum, dv_out))):
                rounded[part, head] = total[head].astype(jnp.bfloat16)
                copy = pltpu.make_async_copy(
                    rounded.at[part, head], result.at[head], rounded_sems.at[part, head]
                )
                complete.append((wanted, copy))
    for wanted, copy in complete:
        pl.when(wanted)(copy.start)
    for copy in copies:
        copy.wait()
    for wanted, copy in complete:
        pl.when(wanted)(copy.wait)


def first_owner_kernel(count, cap, scale, table_ref, k_ref, v_ref, arrived, stats, *rest):
    dk_in, dv_in, _, _, dk_out, dv_out, staged, sems = rest
    table = Table(table_ref, k_ref.shape[0], count, cap)
    stores = []
    for slot in range(arrived.shape[1]):
        found, head, *terms = owner_terms(
            table, 0, scale, k_ref, v_ref, arrived, stats, slot
        )
        for part, (total, result) in enumerate(((dk_in, dk_out), (dv_in, dv_out))):
            staged[part, slot] = (total[head] + terms[part]).astype(jnp.bfloat16)
            store = pltpu.make_async_copy(
                staged.at[part, slot], result.at[head], sems.at[part, slot]
            )
            stores.append((found >= 0, store))
    for wanted, store in stores:
        pl.when(wanted)(store.start)
    for wanted, store in stores:
        pl.when(wanted)(store.wait)


def closing_kernel(count, cap, table_ref, terms, dk_in, dv_in, *rest):
    _, _, dk_out, dv_out, staged, sems = rest
    table = Table(table_ref, dk_in.shape[0], count, cap)
    returned = terms.shape[1]
    stores = []
    for number in range(returned):
        found = table_ref[table.owner_at(0, cap - returned + number)]
        head = jnp.maximum(found, 0)
        for part, (total, result) in enumerate(((dk_in, dk_out), (dv_in, dv_out))):
            term = terms[part, number].astype(jnp.float32)
            staged[part, number] = (total[head] + term).astype(jnp.bfloat16)
            store = pltpu.make_async_copy(
                staged.at[part, number], result.at[head], sems.at[part, number]
            )
            stores.append((found >= 0, store))
    for wanted, store in stores:
        pl.when(wanted)(store.start)
    for wanted, store in stores:
        pl.when(wanted)(store.wait)


def per_device(queries, keys, values, out_grad, tile_lists):
    heads, tokens, width = queries.shape
    channels = channel_list(lax.axis_size("seq"))
    count = len(channels)
    cap = heads // 2
    early = cap - 1
    scale = width ** (-0.5)
    table_size = Table(None, heads, count, cap).size()
    smem = pl.BlockSpec(memory_space=pltpu.SMEM)
    anywhere = pl.BlockSpec(memory_space=pl.ANY)
    vmem = pl.BlockSpec(memory_space=pltpu.VMEM)
    params = pltpu.CompilerParams(vmem_limit_bytes=VMEM_LIMIT)
    brief = pl.CostEstimate(flops=1, bytes_accessed=1, transcendentals=0)
    lengthy = pl.CostEstimate(flops=10**11, bytes_accessed=1, transcendentals=0)
    packed = pltpu.VMEM((2, cap, tokens, width), jnp.bfloat16)
    whole = jax.ShapeDtypeStruct((heads, tokens, width), jnp.bfloat16)
    whole_near = pltpu.VMEM((heads, tokens, width), jnp.bfloat16)
    whole_pair = pltpu.VMEM((2, heads, tokens, width), jnp.bfloat16)
    copies_whole = pltpu.SemaphoreType.DMA((2, heads))
    whole_sum = pltpu.VMEM((heads, tokens, width), jnp.float32)
    squares = pltpu.VMEM((heads, tokens, tokens), jnp.float32)
    far_squares = pltpu.VMEM((count * cap, tokens, tokens), jnp.float32)
    row_stats = pltpu.VMEM((cap, 2, tokens), jnp.float32)
    copies = pltpu.SemaphoreType.DMA((count, 2, cap))
    lists, q_far, k_far, v_far, g_far = (
        pltpu.with_memory_space_constraint(array, pltpu.HBM)
        for array in (jnp.swapaxes(tile_lists, 1, 2), queries, keys, values, out_grad)
    )
    key_value, lists, keys, values = pl.pallas_call(
        functools.partial(pack_keys_kernel, cap, channels[0]),
        out_shape=[packed, pltpu.SMEM(lists.shape, jnp.int32)] + [whole_near] * 2,
        in_specs=[anywhere] * 3,
        out_specs=[vmem, smem, vmem, vmem],
        scratch_shapes=[pltpu.SemaphoreType.DMA((3,))],
        compiler_params=params,
        cost_estimate=brief,
        name="pack_keys",
    )(lists, k_far, v_far)
    fetched = [swapped(key_value, channels[0])]
    table = pl.pallas_call(
        functools.partial(table_kernel, channels, cap),
        out_shape=pltpu.SMEM((table_size,), jnp.int32),
        in_specs=[smem],
        out_specs=smem,
        compiler_params=params,
        cost_estimate=brief,
        name="table",
    )(lists)
    for number in range(1, count):
        key_value = pl.pallas_call(
            functools.partial(pack_more_keys_kernel, count, cap, number),
            out_shape=packed,
            in_specs=[smem, vmem, vmem],
            out_specs=vmem,
            scratch_shapes=[pltpu.SemaphoreType.DMA((2, cap))],
            compiler_params=params,
            cost_estimate=brief,
            name="pack_more_keys",
        )(table, keys, values)
        fetched.append(swapped(key_value, channels[number]))
    one_head = pl.BlockSpec((1, tokens, width), lambda head: (head, 0, 0))
    one_square = pl.BlockSpec((1, tokens, tokens), lambda head: (head, 0, 0))
    sent = [pltpu.VMEM((2, early, tokens, width), jnp.bfloat16)] + [packed] * (count - 1)
    own_weight, own_prob_grad, own_rows, *query_grads = pl.pallas_call(
        functools.partial(own_kernel, count, cap, scale),
        grid=(heads,),
        out_shape=[squares] * 2 + [pltpu.VMEM((heads, 3, tokens), jnp.float32)] + sent,
        in_specs=[smem] + [one_head] * 4 + [anywhere] * 2,
        out_specs=[one_square] * 2
        + [pl.BlockSpec((1, 3, tokens), lambda head: (head, 0, 0))]
        + [pl.BlockSpec(memory_space=pltpu.VMEM)] * count,
        scratch_shapes=[copies],
        compiler_params=params,
        cost_estimate=brief,
        name="own_scores",
    )(table, q_far, keys, values, g_far, q_far, g_far)
    query_grads[1:], fetched[0] = lax.optimization_barrier((query_grads[1:], fetched[0]))
    arrived = [swapped(block, channel) for block, channel in zip(query_grads, channels)]
    far_weight, far_prob_grad, own_factors, far_factors, *stats = pl.pallas_call(
        functools.partial(statistics_kernel, count, cap, scale),
        out_shape=[far_squares] * 2
        + [pltpu.VMEM((heads, 2, tokens), jnp.float32)]
        + [pltpu.VMEM((count * cap, 2, tokens), jnp.float32)]
        + [row_stats] * count,
        in_specs=[smem] + [vmem] * (3 + count),
        out_specs=[vmem] * (4 + count),
        scratch_shapes=[pltpu.VMEM((count * cap, 3, tokens), jnp.float32)],
        compiler_params=params,
        cost_estimate=brief,
        name="statistics",
    )(table, queries, out_grad, own_rows, *fetched)
    stats = [swapped(block, channel) for block, channel in zip(stats, channels)]
    terms = pl.pallas_call(
        functools.partial(returned_kernel, count, cap, scale),
        out_shape=pltpu.VMEM((2, cap - early, tokens, width), jnp.bfloat16),
        in_specs=[smem] + [vmem] * 5,
        out_specs=vmem,
        compiler_params=params,
        cost_estimate=brief,
        name="returned",
    )(table, queries, out_grad, far_weight, far_prob_grad, far_factors)
    terms = swapped(terms, channels[0])
    transposed_sums = pltpu.VMEM((heads, width, tokens), jnp.float32)
    *finished, key_sum, value_sum = pl.pallas_call(
        functools.partial(reader_kernel, count, cap, scale),
        out_shape=[whole_near] * 2 + [whole_sum] * 2,
        in_specs=[smem] + [vmem] * (10 + count),
        out_specs=[vmem] * 4,
        scratch_shapes=[transposed_sums] * 2,
        compiler_params=params,
        cost_estimate=lengthy,
        name="reader",
    )(
        table,
        queries,
        keys,
        values,
        out_grad,
        own_weight,
        own_prob_grad,
        own_factors,
        far_weight,
        far_prob_grad,
        far_factors,
        *fetched,
    )
    results = []
    for number in range(count - 1, 0, -1):
        stored = 2 if number == count - 1 else 0
        outputs = stored + (2 if number == 1 else 0)
        *stored_now, key_sum, value_sum = pl.pallas_call(
            functools.partial(owner_kernel, count, cap, scale, number),
            out_shape=[whole] * outputs + [whole_sum] * 2,
            in_specs=[smem] + [vmem] * (6 + stored),
            out_specs=[anywhere] * outputs + [vmem] * 2,
            scratch_shapes=[whole_pair, copies_whole, copies_whole],
            compiler_params=params,
            cost_estimate=brief,
            name="owner",
        )(
            table,
            keys,
            values,
            arrived[number],
            stats[number],
            key_sum,
            value_sum,
            *(finished if stored else []),
        )
        results += stored_now
    *results, key_grad, value_grad = results
    first, key_sum = lax.optimization_barrier((arrived[0], key_sum))
    key_grad, value_grad = pl.pallas_call(
        functools.partial(first_owner_kernel, count, cap, scale),
        out_shape=[whole] * 2,
        in_specs=[smem] + [vmem] * 6 + [anywhere] * 2,
        out_specs=[anywhere] * 2,
        scratch_shapes=[packed, pltpu.SemaphoreType.DMA((2, cap))],
        input_output_aliases={7: 0, 8: 1},
        compiler_params=params,
        cost_estimate=brief,
        name="first_owner",
    )(table, keys, values, first, stats[0], key_sum, value_sum, key_grad, value_grad)
    terms, key_grad = lax.optimization_barrier((terms, key_grad))
    key_grad, value_grad = pl.pallas_call(
        functools.partial(closing_kernel, count, cap),
        out_shape=[whole] * 2,
        in_specs=[smem] + [vmem] * 3 + [anywhere] * 2,
        out_specs=[anywhere] * 2,
        scratch_shapes=[packed, pltpu.SemaphoreType.DMA((2, cap))],
        input_output_aliases={4: 0, 5: 1},
        compiler_params=params,
        cost_estimate=brief,
        name="closing",
    )(table, terms, key_sum, value_sum, key_grad, value_grad)
    return *results, key_grad, value_grad


def solution(mesh):
    tokens_placed = P("mp", ("clips", "seq"), None)
    return jax.shard_map(
        per_device,
        mesh=mesh,
        in_specs=(tokens_placed,) * 4 + (P("mp", None, None),),
        out_specs=(tokens_placed,) * 4,
        check_vma=False,
    )
```

```python
import functools

import jax
import jax.numpy as jnp
from jax import lax
from jax.experimental import pallas as pl
from jax.experimental.pallas import tpu as pltpu
from jax.sharding import PartitionSpec as P

GX = 8
LOG2E = 1.4426950408889634
LOWEST = -3.0e38
VMEM_LIMIT = 24 * 1024 * 1024


def channel_list(tile_count):
    row_tiles = min(4, tile_count // GX)
    layer_size = GX * row_tiles
    distances = [1]
    if row_tiles > 1:
        distances.append(GX)
    if tile_count // layer_size > 1:
        distances.append(layer_size)
    return [(distance, colour) for distance in distances for colour in (0, 1)]


def swap_route(channel, tile_count):
    distance, colour = channel
    route = []
    for low in range(tile_count - distance):
        if (low // distance) % 2 == colour:
            route += [(low, low + distance), (low + distance, low)]
    return route


def swapped(block, channel):
    return lax.ppermute(block, "seq", swap_route(channel, lax.axis_size("seq")))


def partner_of(own_tile, channel):
    distance, colour = channel
    is_low = lax.rem(lax.div(own_tile, distance), 2) == colour
    return jnp.where(is_low, own_tile + distance, own_tile - distance)


def dot_nt(a, b):
    return lax.dot_general(a, b, (((1,), (1,)), ((), ())), preferred_element_type=jnp.float32)


def dot_tn(a, b):
    return lax.dot_general(a, b, (((0,), (0,)), ((), ())), preferred_element_type=jnp.float32)


def dot_nn(a, b):
    return lax.dot_general(a, b, (((1,), (0,)), ((), ())), preferred_element_type=jnp.float32)


class Table:
    def __init__(self, ref, heads, count, cap):
        self.ref, self.heads, self.count, self.cap = ref, heads, count, cap

    def slot_at(self, head, number):
        return head * self.count + number

    def reader_at(self, number, slot):
        return self.heads * self.count + number * self.cap + slot

    def owner_at(self, number, slot):
        return self.reader_at(self.count + number, slot)

    def size(self):
        return self.owner_at(self.count - 1, self.cap - 1) + 1


def names(lists, head, reader, tile):
    entries = range(1, lists.shape[1])
    return functools.reduce(jnp.logical_or, [lists[head, entry, reader] == tile for entry in entries])


def pack_keys_kernel(cap, channel, lists_hbm, keys, values, target, lists, *rest):
    *held, sems = rest
    heads, _, tile_count = lists.shape
    loads = [pltpu.make_async_copy(lists_hbm, lists, sems.at[2])]
    for part, source in enumerate((keys, values)):
        loads.append(pltpu.make_async_copy(source, held[part], sems.at[part]))
    for load in loads:
        load.start()
    loads[0].wait()
    own_tile = lax.axis_index("seq")
    partner = partner_of(own_tile, channel)
    inside = (partner >= 0) & (partner < tile_count)
    reader = jnp.clip(partner, 0, tile_count - 1)
    filled = jnp.int32(0)
    chosen = [jnp.int32(0)] * cap
    for head in range(heads):
        wanted = names(lists, head, reader, own_tile) & inside
        for slot in range(cap):
            chosen[slot] = jnp.where(wanted & (filled == slot), head, chosen[slot])
        filled = filled + wanted.astype(jnp.int32)
    for load in loads[1:]:
        load.wait()
    for slot in range(cap):
        for part in range(2):
            target[part, slot] = held[part][chosen[slot]]


def pack_more_keys_kernel(count, cap, number, table_ref, keys, values, target, sems):
    table = Table(table_ref, keys.shape[0], count, cap)
    for stage in ("start", "wait"):
        for slot in range(cap):
            head = table_ref[table.owner_at(number, slot)]

            @pl.when(head >= 0)
            def _():
                for part, source in enumerate((keys, values)):
                    copy = pltpu.make_async_copy(
                        source.at[head], target.at[part, slot], sems.at[part, slot]
                    )
                    if stage == "start":
                        copy.start()
                    else:
                        copy.wait()


def table_kernel(channels, cap, lists, table_ref):
    heads, _, tile_count = lists.shape
    table = Table(table_ref, heads, len(channels), cap)
    own_tile = lax.axis_index("seq")
    for number, channel in enumerate(channels):
        partner = partner_of(own_tile, channel)
        inside = (partner >= 0) & (partner < tile_count)
        reader = jnp.clip(partner, 0, tile_count - 1)
        for slot in range(cap):
            table_ref[table.owner_at(number, slot)] = -1
            table_ref[table.reader_at(number, slot)] = -1
        filled = [jnp.int32(0), jnp.int32(0)]
        for head in range(heads):
            given = names(lists, head, reader, own_tile) & inside & (filled[0] < cap)
            named = names(lists, head, own_tile, partner) & inside & (filled[1] < cap)
            table_ref[table.slot_at(head, number)] = jnp.where(named, filled[1], -1)

            @pl.when(given)
            def _():
                table_ref[table.owner_at(number, filled[0])] = head

            @pl.when(named)
            def _():
                table_ref[table.reader_at(number, filled[1])] = head

            filled = [filled[0] + given.astype(jnp.int32), filled[1] + named.astype(jnp.int32)]


def own_kernel(count, cap, scale, table_ref, q_ref, k_ref, v_ref, g_ref, queries, grads, *rest):
    weight_ref, prob_grad_ref, rows_ref, *targets, sems = rest
    heads = queries.shape[0]
    table = Table(table_ref, heads, count, cap)

    def copies(stage):
        for number in range(count):
            for slot in range(targets[number].shape[1]):
                head = table_ref[table.reader_at(number, slot)]

                @pl.when(head >= 0)
                def _():
                    for part, source in enumerate((queries, grads)):
                        copy = pltpu.make_async_copy(
                            source.at[head],
                            targets[number].at[part, slot],
                            sems.at[number, part, slot],
                        )
                        if stage == "start":
                            copy.start()
                        else:
                            copy.wait()

    pl.when(pl.program_id(0) == 0)(lambda: copies("start"))
    score = dot_nt(k_ref[0], q_ref[0]) * (scale * LOG2E)
    top = jnp.max(score, axis=0, keepdims=True)
    weight = jnp.exp2(score - top)
    prob_grad = dot_nt(v_ref[0], g_ref[0])
    weight_ref[0] = weight
    prob_grad_ref[0] = prob_grad
    rows_ref[0, 0:1] = top
    rows_ref[0, 1:2] = jnp.sum(weight, axis=0, keepdims=True)
    rows_ref[0, 2:3] = jnp.sum(weight * prob_grad, axis=0, keepdims=True)
    pl.when(pl.program_id(0) == heads - 1)(lambda: copies("wait"))


def statistics_kernel(count, cap, scale, table_ref, q_ref, g_ref, own_rows, *rest):
    fetched, rest = rest[:count], rest[count:]
    weight_ref, prob_grad_ref, own_factors, far_factors = rest[:4]
    stats, far_rows = rest[4 : 4 + count], rest[4 + count]
    heads = q_ref.shape[0]
    table = Table(table_ref, heads, count, cap)
    for number in range(count):
        for slot in range(cap):
            head = jnp.maximum(table_ref[table.reader_at(number, slot)], 0)
            place = number * cap + slot
            score = dot_nt(fetched[number][0, slot], q_ref[head]) * (scale * LOG2E)
            top = jnp.max(score, axis=0, keepdims=True)
            weight = jnp.exp2(score - top)
            prob_grad = dot_nt(fetched[number][1, slot], g_ref[head])
            weight_ref[place] = weight
            prob_grad_ref[place] = prob_grad
            far_rows[place, 0:1] = top
            far_rows[place, 1:2] = jnp.sum(weight, axis=0, keepdims=True)
            far_rows[place, 2:3] = jnp.sum(weight * prob_grad, axis=0, keepdims=True)
    for head in range(heads):
        rows = [own_rows[head]]
        slots = [table_ref[table.slot_at(head, number)] for number in range(count)]
        for number in range(count):
            found = far_rows[number * cap + jnp.maximum(slots[number], 0)]
            missing = jnp.where(
                lax.broadcasted_iota(jnp.int32, found.shape, 0) == 0, LOWEST, 0.0
            )
            rows.append(jnp.where(slots[number] >= 0, found, missing))
        top = functools.reduce(jnp.maximum, [row[0:1] for row in rows])
        factors = [jnp.exp2(row[0:1] - top) for row in rows]
        total = sum(factor * row[1:2] for factor, row in zip(factors, rows))
        inverse = 1.0 / total
        delta = sum(factor * row[2:3] for factor, row in zip(factors, rows)) * inverse
        level = top + jnp.log2(total)
        own_factors[head, 0:1] = factors[0] * inverse
        own_factors[head, 1:2] = delta
        for number in range(count):

            @pl.when(slots[number] >= 0)
            def _():
                place = number * cap + slots[number]
                far_factors[place, 0:1] = factors[1 + number] * inverse
                far_factors[place, 1:2] = delta
                stats[number][slots[number], 0:1] = level
                stats[number][slots[number], 1:2] = delta


def softmax_grad(weight, prob_grad, factors):
    prob = weight * factors[0:1]
    score_grad = prob * (prob_grad - factors[1:2])
    return prob.astype(jnp.bfloat16), score_grad.astype(jnp.bfloat16)


def returned_kernel(count, cap, scale, table_ref, q_ref, g_ref, *rest):
    far_weight, far_prob_grad, far_factors, terms = rest
    table = Table(table_ref, q_ref.shape[0], count, cap)
    returned = terms.shape[1]
    for number in range(returned):
        place = cap - returned + number
        head = jnp.maximum(table_ref[table.reader_at(0, place)], 0)
        prob, score_grad = softmax_grad(
            far_weight[place], far_prob_grad[place], far_factors[place]
        )
        terms[0, number] = (dot_nn(score_grad, q_ref[head]) * scale).astype(jnp.bfloat16)
        terms[1, number] = dot_nn(prob, g_ref[head]).astype(jnp.bfloat16)


def reader_kernel(count, cap, scale, table_ref, q_ref, k_ref, v_ref, g_ref, *rest):
    own_weight, own_prob_grad, own_factors, far_weight, far_prob_grad, far_factors = rest[:6]
    fetched, rest = rest[6 : 6 + count], rest[6 + count :]
    o_ref, dq_ref, dk_ref, dv_ref, o_sum, dq_sum = rest
    heads = q_ref.shape[0]
    table = Table(table_ref, heads, count, cap)
    for head in range(heads):
        prob, score_grad = softmax_grad(own_weight[head], own_prob_grad[head], own_factors[head])
        o_sum[head] = dot_tn(v_ref[head], prob)
        dq_sum[head] = dot_tn(k_ref[head], score_grad)
        dk_ref[head] = dot_nn(score_grad, q_ref[head]) * scale
        dv_ref[head] = dot_nn(prob, g_ref[head])
    for number in range(count):
        for slot in range(cap):
            found = table_ref[table.reader_at(number, slot)]
            head = jnp.maximum(found, 0)
            place = number * cap + slot
            prob, score_grad = softmax_grad(
                far_weight[place], far_prob_grad[place], far_factors[place]
            )
            o_term = dot_tn(fetched[number][1, slot], prob)
            dq_term = dot_tn(fetched[number][0, slot], score_grad)
            o_sum[head] += jnp.where(found >= 0, o_term, 0.0)
            dq_sum[head] += jnp.where(found >= 0, dq_term, 0.0)
    for head in range(heads):
        o_ref[head] = o_sum[head].T.astype(jnp.bfloat16)
        dq_ref[head] = (dq_sum[head] * scale).T.astype(jnp.bfloat16)


def owner_terms(table, number, scale, k_ref, v_ref, arrived, stats, slot):
    found = table.ref[table.owner_at(number, slot)]
    head = jnp.maximum(found, 0)
    query, grad = arrived[0, slot], arrived[1, slot]
    score = dot_nt(k_ref[head], query) * (scale * LOG2E)
    prob = jnp.exp2(score - stats[slot, 0:1])
    prob_grad = dot_nt(v_ref[head], grad)
    score_grad = (prob * (prob_grad - stats[slot, 1:2])).astype(jnp.bfloat16)
    dk_term = dot_nn(score_grad, query) * scale
    dv_term = dot_nn(prob.astype(jnp.bfloat16), grad)
    return found, head, jnp.where(found >= 0, dk_term, 0.0), jnp.where(found >= 0, dv_term, 0.0)


def owner_kernel(count, cap, scale, number, table_ref, k_ref, v_ref, arrived, stats, *rest):
    *rest, dk_sum, dv_sum, rounded, sems, rounded_sems = rest
    heads = k_ref.shape[0]
    table = Table(table_ref, heads, count, cap)
    closing = number == 1
    results = rest[2:]
    if closing:
        *results, dk_out, dv_out = results
    copies = []
    for part in range(len(results) // 2):
        for head in range(heads):
            source, result = results[part], results[part + len(results) // 2]
            copies.append(
                pltpu.make_async_copy(source.at[head], result.at[head], sems.at[part, head])
            )
    for copy in copies:
        copy.start()
    for total, given in zip((dk_sum, dv_sum), rest):
        for head in range(heads):
            total[head] = given[head]
    for slot in range(cap):
        _, head, dk_term, dv_term = owner_terms(
            table, number, scale, k_ref, v_ref, arrived, stats, slot
        )
        dk_sum[head] += dk_term
        dv_sum[head] += dv_term
    complete = []
    if closing:
        awaited = [table_ref[table.owner_at(0, slot)] for slot in range(cap)]
        for head in range(heads):
            wanted = functools.reduce(jnp.logical_and, [owner != head for owner in awaited])
            for part, (total, result) in enumerate(((dk_sum, dk_out), (dv_sum, dv_out))):
                rounded[part, head] = total[head].astype(jnp.bfloat16)
                copy = pltpu.make_async_copy(
                    rounded.at[part, head], result.at[head], rounded_sems.at[part, head]
                )
                complete.append((wanted, copy))
    for wanted, copy in complete:
        pl.when(wanted)(copy.start)
    for copy in copies:
        copy.wait()
    for wanted, copy in complete:
        pl.when(wanted)(copy.wait)


def first_owner_kernel(count, cap, scale, table_ref, k_ref, v_ref, arrived, stats, *rest):
    dk_in, dv_in, _, _, dk_out, dv_out, staged, sems = rest
    table = Table(table_ref, k_ref.shape[0], count, cap)
    stores = []
    for slot in range(arrived.shape[1]):
        found, head, *terms = owner_terms(
            table, 0, scale, k_ref, v_ref, arrived, stats, slot
        )
        for part, (total, result) in enumerate(((dk_in, dk_out), (dv_in, dv_out))):
            staged[part, slot] = (total[head] + terms[part]).astype(jnp.bfloat16)
            store = pltpu.make_async_copy(
                staged.at[part, slot], result.at[head], sems.at[part, slot]
            )
            stores.append((found >= 0, store))
    for wanted, store in stores:
        pl.when(wanted)(store.start)
    for wanted, store in stores:
        pl.when(wanted)(store.wait)


def closing_kernel(count, cap, table_ref, terms, dk_in, dv_in, *rest):
    _, _, dk_out, dv_out, staged, sems = rest
    table = Table(table_ref, dk_in.shape[0], count, cap)
    returned = terms.shape[1]
    for number in range(returned):
        head = table_ref[table.owner_at(0, cap - returned + number)]

        @pl.when(head >= 0)
        def _():
            stores = []
            for part, (total, result) in enumerate(((dk_in, dk_out), (dv_in, dv_out))):
                term = terms[part, number].astype(jnp.float32)
                staged[part, number] = (total[head] + term).astype(jnp.bfloat16)
                stores.append(
                    pltpu.make_async_copy(
                        staged.at[part, number], result.at[head], sems.at[part, number]
                    )
                )
                stores[-1].start()
            for store in stores:
                store.wait()


def per_device(queries, keys, values, out_grad, tile_lists):
    heads, tokens, width = queries.shape
    channels = channel_list(lax.axis_size("seq"))
    count = len(channels)
    cap = heads // 2
    early = cap - 1
    scale = width ** (-0.5)
    table_size = Table(None, heads, count, cap).size()
    smem = pl.BlockSpec(memory_space=pltpu.SMEM)
    anywhere = pl.BlockSpec(memory_space=pl.ANY)
    vmem = pl.BlockSpec(memory_space=pltpu.VMEM)
    params = pltpu.CompilerParams(vmem_limit_bytes=VMEM_LIMIT)
    brief = pl.CostEstimate(flops=1, bytes_accessed=1, transcendentals=0)
    lengthy = pl.CostEstimate(flops=10**11, bytes_accessed=1, transcendentals=0)
    packed = pltpu.VMEM((2, cap, tokens, width), jnp.bfloat16)
    whole = jax.ShapeDtypeStruct((heads, tokens, width), jnp.bfloat16)
    whole_near = pltpu.VMEM((heads, tokens, width), jnp.bfloat16)
    whole_pair = pltpu.VMEM((2, heads, tokens, width), jnp.bfloat16)
    copies_whole = pltpu.SemaphoreType.DMA((2, heads))
    whole_sum = pltpu.VMEM((heads, tokens, width), jnp.float32)
    squares = pltpu.VMEM((heads, tokens, tokens), jnp.float32)
    far_squares = pltpu.VMEM((count * cap, tokens, tokens), jnp.float32)
    row_stats = pltpu.VMEM((cap, 2, tokens), jnp.float32)
    copies = pltpu.SemaphoreType.DMA((count, 2, cap))
    lists, q_far, k_far, v_far, g_far = (
        pltpu.with_memory_space_constraint(array, pltpu.HBM)
        for array in (jnp.swapaxes(tile_lists, 1, 2), queries, keys, values, out_grad)
    )
    key_value, lists, keys, values = pl.pallas_call(
        functools.partial(pack_keys_kernel, cap, channels[0]),
        out_shape=[packed, pltpu.SMEM(lists.shape, jnp.int32)] + [whole_near] * 2,
        in_specs=[anywhere] * 3,
        out_specs=[vmem, smem, vmem, vmem],
        scratch_shapes=[pltpu.SemaphoreType.DMA((3,))],
        compiler_params=params,
        cost_estimate=brief,
        name="pack_keys",
    )(lists, k_far, v_far)
    fetched = [swapped(key_value, channels[0])]
    table = pl.pallas_call(
        functools.partial(table_kernel, channels, cap),
        out_shape=pltpu.SMEM((table_size,), jnp.int32),
        in_specs=[smem],
        out_specs=smem,
        compiler_params=params,
        cost_estimate=brief,
        name="table",
    )(lists)
    for number in range(1, count):
        key_value = pl.pallas_call(
            functools.partial(pack_more_keys_kernel, count, cap, number),
            out_shape=packed,
            in_specs=[smem, vmem, vmem],
            out_specs=vmem,
            scratch_shapes=[pltpu.SemaphoreType.DMA((2, cap))],
            compiler_params=params,
            cost_estimate=brief,
            name="pack_more_keys",
        )(table, keys, values)
        fetched.append(swapped(key_value, channels[number]))
    one_head = pl.BlockSpec((1, tokens, width), lambda head: (head, 0, 0))
    one_square = pl.BlockSpec((1, tokens, tokens), lambda head: (head, 0, 0))
    sent = [pltpu.VMEM((2, early, tokens, width), jnp.bfloat16)] + [packed] * (count - 1)
    own_weight, own_prob_grad, own_rows, *query_grads = pl.pallas_call(
        functools.partial(own_kernel, count, cap, scale),
        grid=(heads,),
        out_shape=[squares] * 2 + [pltpu.VMEM((heads, 3, tokens), jnp.float32)] + sent,
        in_specs=[smem] + [one_head] * 4 + [anywhere] * 2,
        out_specs=[one_square] * 2
        + [pl.BlockSpec((1, 3, tokens), lambda head: (head, 0, 0))]
        + [pl.BlockSpec(memory_space=pltpu.VMEM)] * count,
        scratch_shapes=[copies],
        compiler_params=params,
        cost_estimate=brief,
        name="own_scores",
    )(table, q_far, keys, values, g_far, q_far, g_far)
    query_grads[1:], fetched[0] = lax.optimization_barrier((query_grads[1:], fetched[0]))
    arrived = [swapped(block, channel) for block, channel in zip(query_grads, channels)]
    far_weight, far_prob_grad, own_factors, far_factors, *stats = pl.pallas_call(
        functools.partial(statistics_kernel, count, cap, scale),
        out_shape=[far_squares] * 2
        + [pltpu.VMEM((heads, 2, tokens), jnp.float32)]
        + [pltpu.VMEM((count * cap, 2, tokens), jnp.float32)]
        + [row_stats] * count,
        in_specs=[smem] + [vmem] * (3 + count),
        out_specs=[vmem] * (4 + count),
        scratch_shapes=[pltpu.VMEM((count * cap, 3, tokens), jnp.float32)],
        compiler_params=params,
        cost_estimate=brief,
        name="statistics",
    )(table, queries, out_grad, own_rows, *fetched)
    stats = [swapped(block, channel) for block, channel in zip(stats, channels)]
    terms = pl.pallas_call(
        functools.partial(returned_kernel, count, cap, scale),
        out_shape=pltpu.VMEM((2, cap - early, tokens, width), jnp.bfloat16),
        in_specs=[smem] + [vmem] * 5,
        out_specs=vmem,
        compiler_params=params,
        cost_estimate=brief,
        name="returned",
    )(table, queries, out_grad, far_weight, far_prob_grad, far_factors)
    terms = swapped(terms, channels[0])
    transposed_sums = pltpu.VMEM((heads, width, tokens), jnp.float32)
    *finished, key_sum, value_sum = pl.pallas_call(
        functools.partial(reader_kernel, count, cap, scale),
        out_shape=[whole_near] * 2 + [whole_sum] * 2,
        in_specs=[smem] + [vmem] * (10 + count),
        out_specs=[vmem] * 4,
        scratch_shapes=[transposed_sums] * 2,
        compiler_params=params,
        cost_estimate=lengthy,
        name="reader",
    )(
        table,
        queries,
        keys,
        values,
        out_grad,
        own_weight,
        own_prob_grad,
        own_factors,
        far_weight,
        far_prob_grad,
        far_factors,
        *fetched,
    )
    results = []
    for number in range(count - 1, 0, -1):
        stored = 2 if number == count - 1 else 0
        outputs = stored + (2 if number == 1 else 0)
        *stored_now, key_sum, value_sum = pl.pallas_call(
            functools.partial(owner_kernel, count, cap, scale, number),
            out_shape=[whole] * outputs + [whole_sum] * 2,
            in_specs=[smem] + [vmem] * (6 + stored),
            out_specs=[anywhere] * outputs + [vmem] * 2,
            scratch_shapes=[whole_pair, copies_whole, copies_whole],
            compiler_params=params,
            cost_estimate=brief,
            name="owner",
        )(
            table,
            keys,
            values,
            arrived[number],
            stats[number],
            key_sum,
            value_sum,
            *(finished if stored else []),
        )
        results += stored_now
    *results, key_grad, value_grad = results
    first, key_sum = lax.optimization_barrier((arrived[0], key_sum))
    key_grad, value_grad = pl.pallas_call(
        functools.partial(first_owner_kernel, count, cap, scale),
        out_shape=[whole] * 2,
        in_specs=[smem] + [vmem] * 6 + [anywhere] * 2,
        out_specs=[anywhere] * 2,
        scratch_shapes=[packed, pltpu.SemaphoreType.DMA((2, cap))],
        input_output_aliases={7: 0, 8: 1},
        compiler_params=params,
        cost_estimate=brief,
        name="first_owner",
    )(table, keys, values, first, stats[0], key_sum, value_sum, key_grad, value_grad)
    terms, key_grad = lax.optimization_barrier((terms, key_grad))
    key_grad, value_grad = pl.pallas_call(
        functools.partial(closing_kernel, count, cap),
        out_shape=[whole] * 2,
        in_specs=[smem] + [vmem] * 3 + [anywhere] * 2,
        out_specs=[anywhere] * 2,
        scratch_shapes=[packed, pltpu.SemaphoreType.DMA((2, cap))],
        input_output_aliases={4: 0, 5: 1},
        compiler_params=params,
        cost_estimate=brief,
        name="closing",
    )(table, terms, key_sum, value_sum, key_grad, value_grad)
    return *results, key_grad, value_grad


def solution(mesh):
    tokens_placed = P("mp", ("clips", "seq"), None)
    return jax.shard_map(
        per_device,
        mesh=mesh,
        in_specs=(tokens_placed,) * 4 + (P("mp", None, None),),
        out_specs=(tokens_placed,) * 4,
        check_vma=False,
    )
```
